128 devices in a mesh: section: 2 (over z_lo), dp: 32 (over x, y, core), tensor: 2 (over z_hi).
Axes of the slice: x: 4, y: 4, z: 4 (z_hi: 2, z_lo: 2; z = z_hi * 2 + z_lo), core: 2. Of those that a mesh axis runs over, the one named last changes fastest.
Arguments:
- inputs: bfloat16 [2, 2048, 1536], P(None, 'dp'), may hold values from -6 to 6
- cotangent: bfloat16 [2, 2048, 1536], P(None, 'dp'), may hold values from -6 to 6
- segments: int32 [2, 2048], replicated, may hold values from 0 to 4, as said below
- routes: int32 [2, 2048, 8], P(None, 'dp'), may hold values from 0 to 15, all different within a row; in each aligned block of 64 rows (0 to 63, 64 to 127, ..., all dimensions but the last counted through in order) at most 40 rows name the same one
- norm_first: float32 [2, 1536], P('section'), may hold values from 0.5 to 1.5
- w_query: bfloat16 [2, 1536, 1536], P('section', None, 'tensor'), may hold values from -0.15625 to 0.15625
- w_key: bfloat16 [2, 1536, 512], P('section', None, 'tensor'), may hold values from -0.15625 to 0.15625
- w_value: bfloat16 [2, 1536, 512], P('section', None, 'tensor'), may hold values from -0.15625 to 0.15625
- w_out: bfloat16 [2, 1536, 1536], P('section', 'tensor'), may hold values from -1.25 to 1.25
- norm_second: float32 [2, 1536], P('section'), may hold values from 0.5 to 1.5
- w_router: bfloat16 [2, 1536, 16], P('section'), may hold values from -0.078125 to 0.078125
- w_gate: bfloat16 [2, 64, 384, 512], P('section', 'dp', None, 'tensor'), may hold values from -0.15625 to 0.15625
- w_up: bfloat16 [2, 64, 384, 512], P('section', 'dp', None, 'tensor'), may hold values from -0.15625 to 0.15625
- w_down: bfloat16 [2, 64, 512, 384], P('section', 'dp', 'tensor'), may hold values from -1 to 1
Outputs:
- layer_outputs: float32 [2, 2, 2048, 1536], P('section', None, 'dp')
- input_grads: float32 [2, 2, 2048, 1536], P('section', None, 'dp')
- grad_norm_first: float32 [2, 1536], P('section')
- grad_w_query: float32 [2, 1536, 1536], P('section', None, 'tensor')
- grad_w_key: float32 [2, 1536, 512], P('section', None, 'tensor')
- grad_w_value: float32 [2, 1536, 512], P('section', None, 'tensor')
- grad_w_out: float32 [2, 1536, 1536], P('section', 'tensor')
- grad_norm_second: float32 [2, 1536], P('section')
- grad_w_router: float32 [2, 1536, 16], P('section')
- grad_w_gate: float32 [2, 64, 384, 512], P('section', 'dp', None, 'tensor')
- grad_w_up: float32 [2, 64, 384, 512], P('section', 'dp', None, 'tensor')
- grad_w_down: float32 [2, 64, 512, 384], P('section', 'dp', 'tensor')
The draws below stay inside these ranges and needn't reach their ends.
Inputs may be any that keep to these rules, and one draw needn't show every extreme that they name: `segments`: each micro-batch is one sequence of 2048 tokens; document ids never fall along it, and one document runs from the tokens of the first index of dp to those of the last. `routes`: each token names 8 different experts; among the rows of one index of dp in one micro-batch no expert is named more than 40 times, a bound that some block reaches.
All inputs are finite; a program needn't handle non-finite values.
Results may differ from the reference program's by a relative error of at most 0.035.
Values may be sent and summed in bfloat16 or wider, within the bound.
No kernel may reach another device: no remote copies, remote signals or barrier semaphores. Data moves between devices by JAX's collectives and lax.ppermute only.
A program may use at most 256 MiB of HBM per device.

```python
import math
import jax
import jax.numpy as jnp
import numpy as np
from jax import lax

D = 1536
HEADS = 24
KV = 8
HD = 64
FF = 512
TOPK = 8
GROUP = 8
EXPERTS = 16
REPS = 4
MICRO = 2
LAYERS = 2
QW = 1536
KW = 512
LENGTH = 2048
TOK_DEV = 64
CAP = 40
TOKENS = 2048
N_DP = 32
N_TENSOR = 2


def draw_segments(key, part):
    key = jax.random.fold_in(key, 7)
    count = MICRO
    first, second, third, fourth = jax.random.split(key, 4)
    start = jax.random.randint(first, (count, 1), 1, TOK_DEV)
    early = jax.random.randint(second, (count, 1), 1, start + 1)
    finish = jax.random.randint(third, (count, 1), LENGTH - TOK_DEV + 1, LENGTH)
    late = jax.random.randint(fourth, (count, 1), finish, LENGTH)
    places = jnp.arange(LENGTH, dtype=jnp.int32)[None, :]
    local = (places >= early).astype(jnp.int32) + (places >= start).astype(jnp.int32) + (places >= finish).astype(jnp.int32) + (places >= late).astype(jnp.int32)
    return local.reshape(MICRO, TOKENS).astype(jnp.int32)


def shard_levels(key, shape, cuts, low, top_value):
    loudness = 1.0
    for dim, shards_of in cuts:
        draws = jax.random.uniform(jax.random.fold_in(jax.random.fold_in(key, 6), dim), (shards_of,), jnp.float32, low / len(cuts), top_value / len(cuts))
        loudness = loudness * jnp.repeat(jnp.exp(draws), shape[dim] // shards_of).reshape((-1,) + (1,) * (len(shape) - 1 - dim))
    return loudness


def shared_out(own_key, own, number, rows, count, top, bound, slope):
    sequence = jax.random.permutation(own_key, count)
    heavy_load, usual = load_shares(count, rows * top, bound, slope, True), load_shares(count, rows * top, bound, slope, False)
    places = jnp.arange(count)

    def named(lengths, turn):
        used = int((lengths > 0).sum())
        fixed = max(1, used // 4)
        passed = fixed + (places - fixed + turn * (used - fixed)) % max(1, count - fixed)
        return jnp.zeros((count,), jnp.int32).at[sequence[jnp.where(places < fixed, places, passed)]].set(jnp.asarray(lengths, jnp.int32))

    lengths = jnp.where(number % 4 == 0, named(heavy_load, number // 4), named(usual, number - number // 4 - 1))
    mixed = jax.random.permutation(jax.random.fold_in(own, 3), count)
    donor, sink = mixed[0:count // 2 * 2:2], mixed[1:count // 2 * 2:2]
    margin = jnp.minimum(lengths[donor] - 1, bound - lengths[sink]) // 2
    margin = jnp.where((donor == sequence[0]) | (sink == sequence[0]) | (lengths[sink] == 0), 0, jnp.maximum(margin, 0))
    passed = jax.random.randint(jax.random.fold_in(own, 4), (count // 2,), 0, 1 << 20) % (margin + 1)
    lengths = lengths.at[donor].add(-passed).at[sink].add(passed)
    items = jnp.searchsorted(jnp.cumsum(lengths), jnp.arange(rows * top), side="right").astype(jnp.int32)
    listing = items.reshape(top, rows).T
    listing = listing[jax.random.permutation(jax.random.fold_in(own, 1), rows)]
    turn = jax.random.randint(jax.random.fold_in(own, 2), (rows, 1), 0, top)
    return jnp.take_along_axis(listing, (jnp.arange(top)[None, :] + turn) % top, axis=1)


def load_shares(number_of, total, most, slope, full):
    weights = [(1 << 20) // math.isqrt(standing ** slope) + 1 for standing in range(1, number_of + 1)]
    largest = most if full else min(most, max(-(-total // number_of), total * weights[0] // sum(weights)))
    least = 1 if total - largest >= number_of - 1 else 0
    given, spare = [largest] + [least] * (number_of - 1), total - largest - least * (number_of - 1)
    while spare > 0:
        free = [i for i in range(1, number_of) if given[i] < largest] or [i for i in range(1, number_of) if given[i] < most]
        whole, left = sum([weights[i] for i in free]), spare
        for i in free:
            addition = min(most - given[i], max(1, left * weights[i] // whole), spare)
            given[i] = given[i] + addition
            spare = spare - addition
    return np.array(given)


def bell_draw(own_key, extent, scale, reach, cuts=(), held_as=jnp.bfloat16):
    entries = jax.random.normal(own_key, extent, jnp.float32) * scale
    if len(cuts) > 0:
        entries = shard_levels(own_key, extent, cuts, -0.22, 0.18) * entries
    return jnp.clip(entries, min=-reach, max=reach).astype(held_as)


def setup_inputs(seed: int = 0) -> dict:
    splits = jax.random.split(jax.random.key(seed), 15)
    inputs = bell_draw(splits[0], (MICRO, TOKENS, D), 1.0, 6.0, ((1, 32),))
    cotangent = bell_draw(splits[1], (MICRO, TOKENS, D), 1.0, 6.0, ((1, 32),))
    segments = draw_segments(jax.random.fold_in(splits[14], 71), 0)
    routes_keys = jax.random.split(jax.random.fold_in(splits[3], 1), MICRO * TOKENS // TOK_DEV)
    routes_turns = jax.random.permutation(jax.random.fold_in(splits[3], 3), MICRO * TOKENS // TOK_DEV)
    routes = jax.vmap(lambda own, number: shared_out(jax.random.fold_in(splits[3], 2), own, number, TOK_DEV, EXPERTS, TOPK, CAP, 2))(routes_keys, routes_turns).reshape((MICRO, TOKENS, TOPK))
    norm_first = jnp.clip(1.0 + 0.1 * jax.random.normal(splits[4], (LAYERS, D), jnp.float32), 0.5, 1.5)
    w_query = bell_draw(splits[5], (LAYERS, D, QW), D ** -0.5, 0.15625, ((0, 2), (2, 2)))
    w_key = bell_draw(splits[6], (LAYERS, D, KW), D ** -0.5, 0.15625, ((0, 2), (2, 2)))
    w_value = bell_draw(splits[7], (LAYERS, D, KW), D ** -0.5, 0.15625, ((0, 2), (2, 2)))
    w_out = bell_draw(splits[8], (LAYERS, QW, D), (QW // 64) ** -0.5, 1.25, ((0, 2), (1, 2)))
    norm_second = jnp.clip(1.0 + 0.1 * jax.random.normal(splits[9], (LAYERS, D), jnp.float32), 0.5, 1.5)
    w_router = bell_draw(splits[10], (LAYERS, D, EXPERTS), (4 * D) ** -0.5, 0.078125, ((0, 2),))
    w_gate = bell_draw(splits[11], (LAYERS, REPS * EXPERTS, D // REPS, FF), D ** -0.5, 0.15625, ((0, 2), (1, 32), (3, 2)))
    w_up = bell_draw(splits[12], (LAYERS, REPS * EXPERTS, D // REPS, FF), D ** -0.5, 0.15625, ((0, 2), (1, 32), (3, 2)))
    w_down = bell_draw(splits[13], (LAYERS, REPS * EXPERTS, FF, D // REPS), (FF // 16) ** -0.5, 1.0, ((0, 2), (1, 32), (2, 2)))
    return dict(inputs=inputs, cotangent=cotangent, segments=segments, routes=routes, norm_first=norm_first, w_query=w_query, w_key=w_key, w_value=w_value, w_out=w_out, norm_second=norm_second, w_router=w_router, w_gate=w_gate, w_up=w_up, w_down=w_down)


EPSILON = 1e-06
SCALE = 0.125
NEGATIVE = -1e+30
HIGH = lax.Precision.HIGHEST

@jax.custom_vjp
def low(v):
    return lax.optimization_barrier(v.astype(jnp.bfloat16)).astype(jnp.float32)

@jax.custom_vjp
def low_back(v):
    return v

def low_keep(v):
    return (low(v), None)

def low_pass(kept, grad):
    return (grad,)

def back_keep(v):
    return (v, None)

def back_low(kept, grad):
    return (low(grad),)
low.defvjp(low_keep, low_pass)
low_back.defvjp(back_keep, back_low)

def dense(left, right):
    return jnp.dot(left, right, precision=HIGH)

def norm_apply(value, gain):
    return value * lax.rsqrt(lax.optimization_barrier(jnp.mean(value * value, axis=-1, keepdims=True)) + EPSILON) * gain

def route_slots(block):
    flat = block.reshape(-1)
    onehot = (flat[:, None] == jnp.arange(EXPERTS, dtype=jnp.int32)[None, :]).astype(jnp.int32)
    counts = jnp.cumsum(onehot, axis=0)
    return lax.optimization_barrier(jnp.sum(onehot * (counts - 1), axis=1)).astype(jnp.int32)

def sequence_attention(pieces):
    query, keys, values, labels = pieces
    grouped = query.reshape(LENGTH, KV, HEADS // KV, HD)
    key_heads = keys.reshape(LENGTH, KV, HD)
    value_heads = values.reshape(LENGTH, KV, HD)
    scores = low_back(jnp.einsum('qkgd,tkd->kgqt', grouped, key_heads, precision=HIGH) * SCALE)
    places = jnp.arange(LENGTH, dtype=jnp.int32)
    allowed = (labels[:, None] == labels[None, :]) & (places[None, :] <= places[:, None])
    scores = jnp.where(allowed[None, None], scores, NEGATIVE)
    weights = low(jax.nn.softmax(scores, axis=-1))
    mixed = jnp.einsum('kgqt,tkd->qkgd', weights, value_heads, precision=HIGH)
    return low(low_back(mixed.reshape(LENGTH, HEADS * HD)))

def expert_block(pieces):
    rows, gate_matrix, up_matrix, down_matrix = pieces
    share = FF // N_TENSOR
    total = jnp.zeros((rows.shape[0], D), jnp.float32)
    for rank in range(N_TENSOR):
        part_rows = low_back(rows)
        gate_pre = low_back(dense(part_rows, gate_matrix[:, rank * share:(rank + 1) * share]))
        up_pre = low_back(dense(part_rows, up_matrix[:, rank * share:(rank + 1) * share]))
        hidden = low(jax.nn.silu(gate_pre) * up_pre)
        total = total + low(low_back(dense(hidden, down_matrix[rank * share:(rank + 1) * share, :])))
    return total

def unpack_rows(weight):
    return weight.reshape(REPS, EXPERTS, D // REPS, FF).transpose(1, 0, 2, 3).reshape(EXPERTS, D, FF)

def unpack_columns(weight):
    return weight.reshape(REPS, EXPERTS, FF, D // REPS).transpose(1, 2, 0, 3).reshape(EXPERTS, FF, D)

def layer(hidden, labels, route_rows, gain_one, query_weight, key_weight, value_weight, out_weight, gain_two, router_weight, gate_weight, up_weight, down_weight):
    activation = low(norm_apply(hidden, gain_one))
    query = low(low_back(dense(activation, query_weight)))
    keys = low(low_back(dense(activation, key_weight)))
    values = low(low_back(dense(activation, value_weight)))
    count = TOKENS // LENGTH
    attended = lax.map(jax.checkpoint(sequence_attention), (query.reshape(count, LENGTH, HEADS * HD), keys.reshape(count, LENGTH, KV * HD), values.reshape(count, LENGTH, KV * HD), labels.reshape(count, LENGTH)))
    attended = attended.reshape(TOKENS, HEADS * HD)
    middle = hidden + low_back(dense(attended, out_weight))
    second_input = low(norm_apply(middle, gain_two))
    logits = dense(second_input, router_weight)
    picked = (route_rows[:, :, None] == jnp.arange(EXPERTS, dtype=jnp.int32)[None, None, :]).astype(jnp.float32)
    chosen = lax.optimization_barrier(jnp.sum(picked * logits[:, None, :], axis=2))
    gates = jax.nn.softmax(chosen, axis=1)
    slots = jax.vmap(route_slots)(route_rows.reshape(N_DP, TOK_DEV, TOPK)).reshape(TOKENS * TOPK)
    source = jnp.arange(TOKENS * TOPK, dtype=jnp.int32) // (TOK_DEV * TOPK)
    group_index = source // GROUP
    position = source % GROUP
    target = (group_index * EXPERTS + route_rows.reshape(-1).astype(jnp.int32)) * (GROUP * CAP) + position * CAP + slots
    owner = jnp.full((REPS * EXPERTS * GROUP * CAP,), TOKENS, jnp.int32).at[target].set(jnp.arange(TOKENS * TOPK, dtype=jnp.int32) // TOPK)
    padded = jnp.concatenate([second_input, jnp.zeros((1, D), jnp.float32)], axis=0)
    rows = padded[owner].reshape(REPS, EXPERTS, GROUP * CAP, D).transpose(1, 0, 2, 3).reshape(EXPERTS, REPS * GROUP * CAP, D)
    produced = lax.map(jax.checkpoint(expert_block), (rows, unpack_rows(gate_weight), unpack_rows(up_weight), unpack_columns(down_weight)))
    produced = produced.reshape(EXPERTS, REPS, GROUP * CAP, D).transpose(1, 0, 2, 3).reshape(REPS * EXPERTS * GROUP * CAP, D)
    gathered = produced[target].reshape(TOKENS, TOPK, D)
    return middle + lax.optimization_barrier(jnp.sum(gates[:, :, None] * gathered, axis=1))

def reference(inputs, cotangent, segments, routes, norm_first, w_query, w_key, w_value, w_out, norm_second, w_router, w_gate, w_up, w_down):
    step_layer = jax.checkpoint(layer)

    def forward(start, deltas, gain_one, query_weight, key_weight, value_weight, out_weight, gain_two, router_weight, gate_weight, up_weight, down_weight):
        results = []
        for batch in range(MICRO):
            hidden = start[batch]
            outputs = []
            for depth in range(LAYERS):
                hidden = hidden + deltas[depth, batch]
                hidden = step_layer(hidden, segments[batch], routes[batch], gain_one[depth], query_weight[depth], key_weight[depth], value_weight[depth], out_weight[depth], gain_two[depth], router_weight[depth], gate_weight[depth], up_weight[depth], down_weight[depth])
                outputs.append(hidden)
            results.append(jnp.stack(outputs))
        return jnp.stack(results, axis=1)
    start = inputs.astype(jnp.float32)
    deltas = jnp.zeros((LAYERS, MICRO, TOKENS, D), jnp.float32)
    primal, pull = jax.vjp(forward, start, deltas, norm_first.astype(jnp.float32), w_query.astype(jnp.float32), w_key.astype(jnp.float32), w_value.astype(jnp.float32), w_out.astype(jnp.float32), norm_second.astype(jnp.float32), w_router.astype(jnp.float32), w_gate.astype(jnp.float32), w_up.astype(jnp.float32), w_down.astype(jnp.float32))
    tangent = jnp.zeros_like(primal).at[LAYERS - 1].set(cotangent.astype(jnp.float32))
    grads = pull(tangent)
    return (primal, grads[1], grads[2], grads[3], grads[4], grads[5], grads[6], grads[7], grads[8], grads[9], grads[10], grads[11])
```

```python
import jax
import jax.numpy as jnp
from jax import lax
from jax.sharding import PartitionSpec as P

D = 1536
HD = 64
EXPERTS = 16
NX, NY = 4, 4
EPSILON = 1e-06
SCALE = 0.125
NEGATIVE = -1e30
BF = jnp.bfloat16
F32 = jnp.float32


def moved(value, dx, dy, dc):
    route = []
    for x in range(NX):
        for y in range(NY):
            for c in range(2):
                target = (((x + dx) % NX) * NY + (y + dy) % NY) * 2 + (c ^ dc)
                route.append(((x * NY + y) * 2 + c, target))
    return lax.ppermute(value, "dp", route)


def swapped(value, axis):
    return lax.ppermute(value, axis, [(0, 1), (1, 0)])


def along_y(block):
    return jnp.concatenate([block] + [moved(block, 0, j, 0) for j in (1, 2, 3)], axis=0)


def along_x(block):
    return jnp.concatenate([block] + [moved(block, j, 0, 0) for j in (1, 2, 3)], axis=0)


def back_y(sums):
    parts = sums.reshape(4, -1, sums.shape[-1])
    total = parts[0].astype(F32)
    for j in (1, 2, 3):
        total = total + moved(parts[j], 0, -j, 0).astype(F32)
    return total


def back_x(sums):
    parts = sums.reshape(4, -1, sums.shape[-1])
    total = parts[0].astype(F32)
    for j in (1, 2, 3):
        total = total + moved(parts[j], -j, 0, 0).astype(F32)
    return total


def group_gather(block):
    column = along_y(block)
    return column, moved(column, 0, 0, 1)


def group_sum(own, other):
    both = own.astype(F32) + moved(other, 0, 0, 1).astype(F32)
    return back_y(both.astype(BF))


def tensor_sum(value):
    low = value.astype(BF)
    return low.astype(F32) + swapped(low, "tensor").astype(F32)


def norm_apply(value, gain):
    inverse = lax.rsqrt(jnp.mean(value * value, axis=-1, keepdims=True) + EPSILON)
    return value * inverse * gain


def norm_back(value, gain, grad):
    inverse = lax.rsqrt(jnp.mean(value * value, axis=-1, keepdims=True) + EPSILON)
    scaled = grad * gain
    inner = jnp.mean(scaled * value, axis=-1, keepdims=True)
    gain_grad = jnp.sum(grad * value * inverse, axis=0)
    return (inverse * scaled - inverse * inverse * inverse * value * inner, gain_grad)


def dot(left, right):
    return jnp.dot(left, right, preferred_element_type=F32)


def over_rows(left, right):
    return lax.dot_general(left, right, (((0,), (0,)), ((), ())), preferred_element_type=F32)


def against(left, right):
    return lax.dot_general(left, right, (((1,), (1,)), ((), ())), preferred_element_type=F32)


def scores_of(query, keys, allowed):
    grouped = query.reshape(query.shape[0], 4, 3, HD)
    key_heads = keys.reshape(keys.shape[0], 4, HD)
    scores = jnp.einsum("qkgd,tkd->kgqt", grouped, key_heads, preferred_element_type=F32) * SCALE
    return jnp.where(allowed[None, None], scores, NEGATIVE)


def attend_forward(query, pairs, allowed):
    scores = scores_of(query, pairs[:, :256], allowed)
    top = jnp.max(scores, axis=-1, keepdims=True)
    raised = jnp.exp(scores - top)
    total = jnp.sum(raised, axis=-1, keepdims=True)
    weights = (raised / total).astype(BF)
    value_heads = pairs[:, 256:].reshape(-1, 4, HD)
    mixed = jnp.einsum("kgqt,tkd->qkgd", weights, value_heads, preferred_element_type=F32)
    return mixed.reshape(query.shape).astype(BF), top + jnp.log(total)


def attend_backward(query, pairs, allowed, log_total, grad_mixed, mixed):
    count = query.shape[0]
    scores = scores_of(query, pairs[:, :256], allowed)
    weights = jnp.exp(scores - log_total)
    grouped = query.reshape(count, 4, 3, HD)
    grad_heads = grad_mixed.reshape(count, 4, 3, HD)
    key_heads = pairs[:, :256].reshape(-1, 4, HD)
    value_heads = pairs[:, 256:].reshape(-1, 4, HD)
    grad_values = jnp.einsum("kgqt,qkgd->tkd", weights.astype(BF), grad_heads, preferred_element_type=F32)
    grad_weights = jnp.einsum("qkgd,tkd->kgqt", grad_heads, value_heads, preferred_element_type=F32)
    inner = jnp.einsum("qkgd,qkgd->kgq", grad_heads.astype(F32), mixed.reshape(count, 4, 3, HD).astype(F32))
    grad_scores = (weights * (grad_weights - inner[..., None])).astype(BF)
    grad_query = jnp.einsum("kgqt,tkd->qkgd", grad_scores, key_heads, preferred_element_type=F32) * SCALE
    grad_keys = jnp.einsum("kgqt,qkgd->tkd", grad_scores, grouped, preferred_element_type=F32) * SCALE
    grad_pairs = jnp.concatenate([grad_keys.reshape(-1, 256), grad_values.reshape(-1, 256)], axis=1)
    return grad_query.reshape(query.shape).astype(BF), grad_pairs.astype(BF)


def gates_of(tokens, router, routed):
    logits = dot(tokens, router)
    top = jnp.max(jnp.where(routed > 0, logits, NEGATIVE), axis=1, keepdims=True)
    raised = jnp.where(routed > 0, jnp.exp(jnp.minimum(logits - top, 0.0)), 0.0)
    return raised / jnp.sum(raised, axis=1, keepdims=True)


def experts_forward(tokens, gates, weights):
    split = tokens.reshape(-1, 4, 384)
    gate_pre = jnp.einsum("trd,redf->etf", split, weights[:, 0:2], preferred_element_type=F32)
    up_pre = jnp.einsum("trd,redf->etf", split, weights[:, 2:4], preferred_element_type=F32)
    mid = (jax.nn.silu(gate_pre) * up_pre * gates.T[:, :, None]).astype(BF)
    produced = jnp.einsum("etf,redf->trd", mid, weights[:, 4:6], preferred_element_type=F32)
    return produced.reshape(-1, D), (gate_pre, up_pre, mid)


def experts_backward(tokens, gates, saved, grad_out, weights):
    gate_pre, up_pre, mid = saved
    split = tokens.reshape(-1, 4, 384)
    grad_split = grad_out.reshape(-1, 4, 384)
    raw = jnp.einsum("trd,redf->etf", grad_split, weights[:, 4:6], preferred_element_type=F32)
    sigmoid = jax.nn.sigmoid(gate_pre)
    activated = gate_pre * sigmoid
    grad_gates = jnp.sum(activated * up_pre * raw, axis=2).T
    scaled = raw * gates.T[:, :, None]
    grad_gate = (scaled * up_pre * sigmoid * (1.0 + gate_pre * (1.0 - sigmoid))).astype(BF)
    grad_up = (scaled * activated).astype(BF)
    down_grad = jnp.einsum("trd,etf->redf", grad_split, mid, preferred_element_type=F32).astype(BF)
    gate_grad = jnp.einsum("trd,etf->redf", split, grad_gate, preferred_element_type=F32).astype(BF)
    up_grad = jnp.einsum("trd,etf->redf", split, grad_up, preferred_element_type=F32).astype(BF)
    grad_tokens = jnp.einsum("etf,redf->trd", grad_gate, weights[:, 0:2], preferred_element_type=F32)
    grad_tokens = grad_tokens + jnp.einsum("etf,redf->trd", grad_up, weights[:, 2:4], preferred_element_type=F32)
    weight_grads = jnp.concatenate([gate_grad, up_grad, down_grad], axis=1)
    return grad_tokens.reshape(-1, D), grad_gates, weight_grads


X_GROUPS = [[(x * NY + y) * 2 + c for x in range(NX)] for y in range(NY) for c in range(2)]


Y_GROUPS = [[(x * NY + y) * 2 + c for y in range(NY) for c in range(2)] for x in range(NX)]


def replica_gather(shard):
    return lax.all_gather(shard, "dp", axis=0, axis_index_groups=X_GROUPS)


def replica_scatter(grads):
    flat = grads.reshape(-1, grads.shape[-1])
    return lax.psum_scatter(flat, "dp", scatter_dimension=0, axis_index_groups=X_GROUPS, tiled=True)


def after(value, *others):
    return lax.optimization_barrier((value, *others))[0]


def per_device(
    inputs,
    cotangent,
    segments,
    routes,
    norm_first,
    w_query,
    w_key,
    w_value,
    w_out,
    norm_second,
    w_router,
    w_gate,
    w_up,
    w_down,
):
    section = lax.axis_index("section")
    place = lax.axis_index("dp")
    here_x, here_y, here_c = place // (NY * 2), place // 2 % NY, place % 2
    first = section == 0
    rows = inputs.shape[1]

    def in_order(own, other):
        return jnp.where(first, own, other), jnp.where(first, other, own)

    def pick(pair):
        return lax.dynamic_index_in_dim(pair, section, 0, False)

    qkv_own = jnp.concatenate([w_query[0], w_key[0], w_value[0]], axis=1)
    act_both = norm_apply(inputs.astype(F32), norm_first[0]).astype(BF)
    qkv_both = dot(act_both.reshape(2 * rows, D), qkv_own).astype(BF)
    qkv_sent = lax.ppermute(qkv_both[rows:], "section", [(0, 1)])
    qkv_first = jnp.where(first, qkv_both[:rows], qkv_sent)

    pack = jnp.concatenate([norm_first, norm_second, w_router[0].T.astype(F32)], axis=0)
    packs = in_order(pack, swapped(pack, "section"))
    experts = jnp.concatenate([w_gate[0], w_up[0], jnp.swapaxes(w_down[0], 1, 2)], axis=0)
    experts = after(experts, qkv_sent)
    experts_both = in_order(experts, swapped(experts, "section"))
    expert_weights = [replica_gather(e) for e in experts_both]

    def whole(own, rows_half, *earlier):
        half = lax.dynamic_slice_in_dim(own, here_c * rows_half, rows_half, 0)
        half = swapped(after(half, *earlier), "section")
        rest = moved(half, 0, 0, 1)
        low = jnp.where(here_c == 0, half, rest)
        high = jnp.where(here_c == 0, rest, half)
        return jnp.concatenate([low, high], axis=0)

    outs_w = in_order(w_out[0], whole(w_out[0], 384, experts_both[0]))
    qkvs_w = None

    labels = pick(segments)
    query_places = place * rows + jnp.arange(rows, dtype=jnp.int32)
    query_labels = lax.dynamic_slice_in_dim(labels, place * rows, rows, 0)
    starts = jnp.sum((labels[None, :] < query_labels[:, None]).astype(jnp.int32), axis=1)
    shift = jnp.arange(4, dtype=jnp.int32)
    key_x = (here_x - shift + NX) % NX
    key_y = (here_y - shift + NY) % NY
    key_c = jnp.stack([here_c, 1 - here_c])
    blocks = (key_x[None, None, :] * NY + key_y[None, :, None]) * 2 + key_c[:, None, None]
    key_places = (blocks[..., None] * rows + jnp.arange(rows, dtype=jnp.int32)).reshape(-1)
    allowed = (key_places[None, :] <= query_places[:, None]) & (key_places[None, :] >= starts[:, None])

    own_routes = pick(routes)
    expert_ids = jnp.arange(EXPERTS, dtype=jnp.int32)
    routed_own = jnp.sum((own_routes[:, :, None] == expert_ids).astype(F32), axis=1)
    given = pick(cotangent)
    sent = jnp.concatenate([given, jnp.pad(routed_own.astype(BF), ((0, 0), (0, 128 - EXPERTS)))], axis=1)
    got = group_gather(sent)
    got = jnp.concatenate(got, axis=0)
    routed = got[:, D : D + EXPERTS].astype(F32)
    given_all = got[:, :D]
    local = lax.broadcasted_iota(jnp.int32, (EXPERTS, 2), 0) == (
        2 * (place % 8) + lax.broadcasted_iota(jnp.int32, (EXPERTS, 2), 1)
    )
    local = local.astype(F32)

    hidden = pick(inputs).astype(F32)
    saved = []
    for layer in range(2):
        gain_one, gain_two = packs[layer][0], packs[layer][1]
        router = packs[layer][2:].T.astype(BF)
        activation = norm_apply(hidden, gain_one).astype(BF)
        qkv = qkv_first if layer == 0 else dot(activation, qkvs_w[1]).astype(BF)
        query, pair = qkv[:, :768], qkv[:, 768:]
        column = along_y(along_x(pair))
        pairs = jnp.concatenate([column, moved(column, 0, 0, 1)], axis=0)
        mixed, log_total = attend_forward(query, pairs, allowed)
        middle = hidden + tensor_sum(dot(mixed, outs_w[layer]))
        second = norm_apply(middle, gain_two).astype(BF)
        tokens = jnp.concatenate(group_gather(second), axis=0)
        gates = jnp.dot(gates_of(tokens, router, routed), local, precision=lax.Precision.HIGHEST)
        if layer == 0:
            qkvs_w = in_order(qkv_own, whole(qkv_own, 768, middle))
        produced, kept = experts_forward(tokens, gates, expert_weights[layer])
        produced = produced.astype(BF)
        half = produced.shape[0] // 2
        branch = tensor_sum(group_sum(produced[:half], produced[half:]).reshape(rows, D))
        result = middle + branch
        lefts = []
        for factor, width in ((activation, 192), (mixed, 96)):
            cut = jnp.swapaxes(factor.reshape(rows, 8, width), 0, 1)
            lefts.append(lax.all_gather(cut, "dp", axis=0, axis_index_groups=Y_GROUPS))
        saved.append((lefts, hidden, activation, query, pairs, mixed, log_total, middle, second, tokens, gates, kept, branch, result))
        hidden = result

    me = place % 8
    group_order = (key_y[None, :] * 2 + key_c[:, None]).reshape(-1)

    def left_of(gathered):
        mine = lax.dynamic_index_in_dim(gathered, me, 1, False)
        return jnp.take(mine, group_order, axis=0).reshape(8 * rows, -1)

    grad_output = given.astype(F32)
    grads = []
    for layer in (1, 0):
        lefts, hidden, activation, query, pairs, mixed, log_total, middle, second, tokens, gates, kept, branch, _ = saved[layer]
        gain_one, gain_two = packs[layer][0], packs[layer][1]
        router = packs[layer][2:].T.astype(BF)
        if layer == 1:
            grad_all = given_all
        else:
            grad_all = jnp.concatenate(group_gather(grad_output.astype(BF)), axis=0)
        grad_tokens, grad_gates, weight_grads = experts_backward(tokens, gates, kept, grad_all, expert_weights[layer])
        expert_part = replica_scatter(weight_grads)
        gated = gates * grad_gates
        router_local = jnp.dot(router.astype(F32), local, precision=lax.Precision.HIGHEST)
        grad_tokens = (grad_tokens + against(gated, router_local)).astype(BF)
        half = grad_tokens.shape[0] // 2
        grad_second = tensor_sum(group_sum(grad_tokens[:half], grad_tokens[half:]).reshape(rows, D))
        inner = jnp.sum(grad_output * branch, axis=1, keepdims=True)
        own_gates = gates_of(second, router, routed_own)
        grad_second = grad_second - against(inner * own_gates, router.astype(F32))
        grad_from_norm, gain_two_grad = norm_back(middle, gain_two, grad_second)
        grad_middle = grad_output + grad_from_norm
        grad_branch = grad_middle.astype(BF)
        inner_high = inner.astype(BF)
        inner_low = (inner - inner_high.astype(F32)).astype(BF)
        lanes = jnp.concatenate([inner_high, inner_low, jnp.zeros((rows, 126), BF)], axis=1)
        right = jnp.concatenate(group_gather(jnp.concatenate([grad_branch, lanes], axis=1)), axis=0)
        inner_all = right[:, D : D + 1].astype(F32) + right[:, D + 1 : D + 2].astype(F32)
        out_grad = over_rows(left_of(lefts[1]), right[:, :D])
        logit_grads = gated - 0.5 * gates * inner_all
        router_grad = over_rows(logit_grads, tokens.astype(F32))
        out_grad = jnp.concatenate([out_grad, router_grad, gain_two_grad[None], jnp.zeros((13, D), F32)], axis=0)
        out_blocks = jnp.swapaxes(out_grad.astype(BF).reshape(112, 4, 384), 0, 1)
        out_part = back_x(jnp.take(out_blocks, key_x, axis=0)).reshape(112, 384)
        grad_mixed = against(grad_branch, outs_w[layer]).astype(BF)
        grad_query, grad_pairs = attend_backward(query, pairs, allowed, log_total, grad_mixed, mixed)
        both = grad_pairs[:1024].astype(F32) + moved(grad_pairs[1024:], 0, 0, 1).astype(F32)
        grad_pair = back_x(back_y(both.astype(BF)).astype(BF)).reshape(rows, 512).astype(BF)
        grad_qkv = jnp.concatenate([grad_query, grad_pair], axis=1)
        right = jnp.concatenate(group_gather(grad_qkv), axis=0)
        qkv_grad = over_rows(left_of(lefts[0]), right).astype(BF)
        qkv_part = back_x(jnp.take(qkv_grad.reshape(4, 48, 1280), key_x, axis=0)).reshape(48, 1280)
        grad_activation = tensor_sum(against(grad_qkv, qkvs_w[layer]))
        grad_from_first, gain_one_grad = norm_back(hidden, gain_one, grad_activation)
        grad_output = grad_middle + grad_from_first
        grads.append((grad_output, qkv_part, out_part, gain_one_grad, expert_part))
    grads = grads[::-1]

    def own_of(a, b):
        return jnp.where(first, a, b)

    def from_other(for_first, for_second):
        return swapped(own_of(for_second, for_first).astype(BF), "section").astype(F32)

    def over_sections(a, b):
        return own_of(a, b).astype(F32) + from_other(a, b)

    def by_batch(own, other):
        return jnp.stack([jnp.where(first, own, other), jnp.where(first, other, own)])[None]

    results = by_batch(own_of(saved[0][-1], saved[1][-1]), from_other(saved[0][-1], saved[1][-1]))
    input_grads = by_batch(own_of(grads[0][0], grads[1][0]), from_other(grads[0][0], grads[1][0]))
    qkv_sum = over_sections(grads[0][1], grads[1][1]).astype(BF)
    out_sum = over_sections(grads[0][2], grads[1][2]).astype(BF)
    gain_one_sum = over_sections(grads[0][3], grads[1][3]).astype(BF)
    qkv_all = lax.all_gather(qkv_sum, "dp", axis=0).reshape(4, 8, 48, 1280)
    out_all = lax.all_gather(out_sum, "dp", axis=0).reshape(4, 8, 112, 384)
    gain_one_all = lax.all_gather(gain_one_sum, "dp", axis=0)
    qkv_all = jnp.swapaxes(qkv_all, 0, 1).reshape(D, 1280).astype(F32)
    out_rows = out_all[:, :, :96]
    out_full = jnp.transpose(out_rows, (1, 2, 0, 3)).reshape(768, D).astype(F32)
    router_sum = jnp.transpose(out_all[:, :, 96:98], (1, 2, 0, 3)).reshape(EXPERTS, D)
    router_sum = tensor_sum(router_sum)
    gain_two_sum = jnp.sum(out_all[:, :, 98].astype(F32), axis=1).reshape(1, D)
    gain_one_sum = jnp.sum(gain_one_all.astype(F32), axis=0)[None]
    expert_sum = over_sections(grads[0][4], grads[1][4]).reshape(3, 2, 384, 256)
    return (
        results,
        input_grads,
        gain_one_sum,
        qkv_all[None, :, :768],
        qkv_all[None, :, 768:1024],
        qkv_all[None, :, 1024:],
        out_full[None],
        gain_two_sum,
        router_sum.T[None],
        expert_sum[0][None],
        expert_sum[1][None],
        jnp.swapaxes(expert_sum[2], 1, 2)[None],
    )


def solution(mesh):
    in_specs = (
        P(None, "dp", None),
        P(None, "dp", None),
        P(),
        P(None, "dp", None),
        P("section", None),
        P("section", None, "tensor"),
        P("section", None, "tensor"),
        P("section", None, "tensor"),
        P("section", "tensor", None),
        P("section", None),
        P("section", None, None),
        P("section", "dp", None, "tensor"),
        P("section", "dp", None, "tensor"),
        P("section", "dp", "tensor", None),
    )
    out_specs = (
        P("section", None, "dp", None),
        P("section", None, "dp", None),
        P("section", None),
        P("section", None, "tensor"),
        P("section", None, "tensor"),
        P("section", None, "tensor"),
        P("section", "tensor", None),
        P("section", None),
        P("section", None, None),
        P("section", "dp", None, "tensor"),
        P("section", "dp", None, "tensor"),
        P("section", "dp", "tensor", None),
    )
    return jax.shard_map(
        per_device, mesh=mesh, in_specs=in_specs, out_specs=out_specs, check_vma=False
    )
```

```python
import functools

import jax
import jax.numpy as jnp
from jax import lax
from jax.experimental import pallas as pl
from jax.experimental.pallas import tpu as pltpu
from jax.sharding import PartitionSpec as P

D = 1536
HD = 64
EXPERTS = 16
NX, NY = 4, 4
EPSILON = 1e-06
SCALE = 0.125
NEGATIVE = -1e30
BF = jnp.bfloat16
F32 = jnp.float32


def moved(value, dx, dy, dc):
    route = []
    for x in range(NX):
        for y in range(NY):
            for c in range(2):
                target = (((x + dx) % NX) * NY + (y + dy) % NY) * 2 + (c ^ dc)
                route.append(((x * NY + y) * 2 + c, target))
    return lax.ppermute(value, "dp", route)


def swapped(value, axis):
    return lax.ppermute(value, axis, [(0, 1), (1, 0)])


def along_y(block):
    return jnp.concatenate([block] + [moved(block, 0, j, 0) for j in (1, 2, 3)], axis=0)


def along_x(block):
    return jnp.concatenate([block] + [moved(block, j, 0, 0) for j in (1, 2, 3)], axis=0)


def back_y(sums):
    parts = sums.reshape(4, -1, sums.shape[-1])
    total = parts[0].astype(F32)
    for j in (1, 2, 3):
        total = total + moved(parts[j], 0, -j, 0).astype(F32)
    return total


def back_x(sums):
    parts = sums.reshape(4, -1, sums.shape[-1])
    total = parts[0].astype(F32)
    for j in (1, 2, 3):
        total = total + moved(parts[j], -j, 0, 0).astype(F32)
    return total


def group_gather(block):
    column = along_y(block)
    return column, moved(column, 0, 0, 1)


def group_sum(own, other):
    both = own.astype(F32) + moved(other, 0, 0, 1).astype(F32)
    return back_y(both.astype(BF))


def tensor_sum(value):
    low = value.astype(BF)
    return low.astype(F32) + swapped(low, "tensor").astype(F32)


def norm_apply(value, gain):
    inverse = lax.rsqrt(jnp.mean(value * value, axis=-1, keepdims=True) + EPSILON)
    return value * inverse * gain


def norm_back(value, gain, grad):
    inverse = lax.rsqrt(jnp.mean(value * value, axis=-1, keepdims=True) + EPSILON)
    scaled = grad * gain
    inner = jnp.mean(scaled * value, axis=-1, keepdims=True)
    gain_grad = jnp.sum(grad * value * inverse, axis=0)
    return (inverse * scaled - inverse * inverse * inverse * value * inner, gain_grad)


def dot(left, right):
    return jnp.dot(left, right, preferred_element_type=F32)


def over_rows(left, right):
    return lax.dot_general(left, right, (((0,), (0,)), ((), ())), preferred_element_type=F32)


def against(left, right):
    return lax.dot_general(left, right, (((1,), (1,)), ((), ())), preferred_element_type=F32)


def nn(a, b):
    return lax.dot_general(a, b, (((1,), (0,)), ((), ())), preferred_element_type=F32)


def nt(a, b):
    return lax.dot_general(a, b, (((1,), (1,)), ((), ())), preferred_element_type=F32)


def tn(a, b):
    return lax.dot_general(a, b, (((0,), (0,)), ((), ())), preferred_element_type=F32)


SMEM = pl.BlockSpec(memory_space=pltpu.SMEM)
VMEM = pl.BlockSpec(memory_space=pltpu.VMEM)
ANY = pl.BlockSpec(memory_space=pl.ANY)


def shaped(*shape, dtype=BF):
    return jax.ShapeDtypeStruct(shape, dtype)


def params(mib):
    del mib
    return pltpu.CompilerParams(vmem_limit_bytes=58 << 20)


def cost(flops, bytes_accessed, exps=0):
    return pl.CostEstimate(flops=flops, bytes_accessed=bytes_accessed, transcendentals=exps)


def stacked(refs):
    return jnp.concatenate([ref[...] for ref in refs], axis=0)


def spread(block):
    lane = lax.broadcasted_iota(jnp.int32, (64, 128), 1)
    parts = []
    for k in range(6):
        wide = block[:, (k // 2) * 128 : (k // 2 + 1) * 128].astype(F32)
        half = k // 3
        if k % 2 != half:
            wide = pltpu.roll(wide, 64, 1)
        parts.append(jnp.where((lane >= 64) == (half == 1), wide, 0.0))
    return jnp.concatenate(parts, axis=0)


def gathered(turned):
    rows = turned.T
    lane = lax.broadcasted_iota(jnp.int32, (64, 128), 1)
    outs = []
    for b in range(3):
        two = []
        for k in (2 * b, 2 * b + 1):
            part = rows[k * 64 : (k + 1) * 64]
            if k % 2 != k // 3:
                part = pltpu.roll(part, 64, 1)
            two.append(part)
        outs.append(jnp.where(lane < 64, two[0], two[1]))
    return jnp.concatenate(outs, axis=1)


def bias_of(place_ref, h, start_ref):
    row = lax.broadcasted_iota(jnp.int32, (1024, 128), 0)
    token = lax.broadcasted_iota(jnp.int32, (1024, 128), 1) & 63
    x = (place_ref[0] - (row >> 6)) & 3
    y = (place_ref[1] - (row >> 8)) & 3
    c = place_ref[2] if h == 0 else 1 - place_ref[2]
    key = ((x * 4 + y) * 2 + c) * 64 + (row & 63)
    query = ((place_ref[0] * 4 + place_ref[1]) * 2 + place_ref[2]) * 64 + token
    bias = jnp.where((key <= query) & (key >= start_ref[...]), 0.0, NEGATIVE)
    return jnp.concatenate([bias, bias, bias], axis=1)


def attend_kernel(place_ref, st_ref, q_ref, *refs):
    keys = [stacked(refs[0:4]), stacked(refs[4:8])]
    values = [stacked(refs[8:12]), stacked(refs[12:16])]
    out_ref, lse_ref = refs[16:]
    query = (spread(q_ref[...]) * 0.125).astype(BF)
    scores = [nt(k, query) + bias_of(place_ref, h, st_ref) for h, k in enumerate(keys)]
    top = jnp.maximum(*[jnp.max(s, axis=0, keepdims=True) for s in scores])
    total = jnp.zeros_like(top)
    mixed = jnp.zeros((128, 384), F32)
    for s, v in zip(scores, values):
        raised = jnp.exp(s - top)
        total = total + jnp.sum(raised, axis=0, keepdims=True)
        mixed = mixed + tn(v, raised.astype(BF))
    out_ref[...] = gathered(mixed / total).astype(BF)
    lse_ref[0] = top + jnp.log(total)


def column(rows, width, base):
    return pl.BlockSpec((rows, width), lambda j: (0, j + base))


PAIRS = [SMEM, pl.BlockSpec((1, 128), lambda j: (0, 0))], [column(256, 128, 0)] * 8 + [column(256, 128, 2)] * 8
LSE = pl.BlockSpec((1, 1, 384), lambda j: (j, 0, 0))


def ignoring(count, kernel):
    return lambda *refs: kernel(*refs[count:])


def attend_forward(masks, query, pieces, *earlier):
    return pl.pallas_call(
        ignoring(len(earlier), attend_kernel),
        grid=(2,),
        in_specs=[ANY] * len(earlier) + PAIRS[0] + [column(64, 384, 0)] + PAIRS[1],
        out_specs=[column(64, 384, 0), LSE],
        out_shape=[shaped(64, 768), shaped(2, 1, 384, dtype=F32)],
        compiler_params=params(40),
        cost_estimate=cost(12 * 64 * 2048 * 64 * 4, 2 << 20, 12 * 64 * 2048),
        name="attend_forward",
    )(*earlier, *masks, query, *pieces, *pieces)


def attend_back_kernel(place_ref, st_ref, q_ref, do_ref, lse_ref, *refs):
    j = pl.program_id(0)
    key_columns = pl.ds(pl.multiple_of(j * 128, 128), 128)
    value_columns = pl.ds(pl.multiple_of(256 + j * 128, 128), 128)
    keys = [stacked(refs[0:4]), stacked(refs[4:8])]
    values = [stacked(refs[8:12]), stacked(refs[12:16])]
    dq_ref, near_ref, far_ref = refs[16:]
    query = (spread(q_ref[...]) * 0.125).astype(BF)
    grad = spread(do_ref[...]).astype(BF)
    weights, raws = [], []
    inner = jnp.zeros((1, 384), F32)
    for h, (k, v) in enumerate(zip(keys, values)):
        s = nt(k, query) + bias_of(place_ref, h, st_ref)
        w = jnp.exp(s - lse_ref[0])
        raw = nt(v, grad)
        inner = inner + jnp.sum(w * raw, axis=0, keepdims=True)
        weights.append(w)
        raws.append(raw)
    turned = jnp.zeros((128, 384), F32)
    for w, raw, k, out_ref in zip(weights, raws, keys, (near_ref, far_ref)):
        ds = (w * (raw - inner)).astype(BF)
        out_ref[:, key_columns] = nn(ds, query).astype(BF)
        out_ref[:, value_columns] = nn(w.astype(BF), grad).astype(BF)
        turned = turned + tn(k, ds)
    dq_ref[...] = gathered(turned * 0.125).astype(BF)


def attend_backward(masks, query, grad, lse, pieces, *earlier):
    return pl.pallas_call(
        ignoring(len(earlier), attend_back_kernel),
        grid=(2,),
        in_specs=[ANY] * len(earlier) + PAIRS[0] + [column(64, 384, 0)] * 2 + [LSE] + PAIRS[1],
        out_specs=[column(64, 384, 0)] + [pl.BlockSpec((1024, 512), lambda j: (0, 0))] * 2,
        out_shape=[shaped(64, 768), shaped(1024, 512), shaped(1024, 512)],
        compiler_params=params(48),
        cost_estimate=cost(12 * 64 * 2048 * 64 * 10, 4 << 20, 12 * 64 * 2048),
        name="attend_backward",
    )(*earlier, *masks, query, grad, lse, *pieces, *pieces)


def whole(*shape):
    return pl.BlockSpec(shape, lambda j: (0,) * len(shape))


def expert_kernel(where_ref, weight_ref, router_ref, routed_ref, *refs):
    token_refs, (pa_ref, pb_ref, pre_ref, mid_ref, gates_ref, all_ref) = refs[:8], refs[8:]
    for h, out_ref in enumerate((pa_ref, pb_ref)):
        rows = pl.ds(h * 256, 256)
        tokens = stacked(token_refs[4 * h : 4 * h + 4])
        all_ref[rows] = tokens
        parts = [tokens[:, r * 384 : (r + 1) * 384] for r in range(4)]
        routed = routed_ref[rows, 0:16].astype(F32) > 0
        logits = jnp.where(routed, nt(tokens, router_ref[...]), NEGATIVE)
        raised = jnp.exp(logits - jnp.max(logits, axis=1, keepdims=True))
        raised = jnp.where(routed, raised, 0.0)
        gates = raised / jnp.sum(raised, axis=1, keepdims=True)
        expert = lax.broadcasted_iota(jnp.int32, (256, 16), 1) - 2 * where_ref[3]
        gates = jnp.where((expert == 0) | (expert == 1), gates, 0.0)
        gates_ref[rows] = gates
        mids = []
        for e in range(2):
            gate_pre = sum(nn(parts[r], weight_ref[r, e]) for r in range(4))
            up_pre = sum(nn(parts[r], weight_ref[r, 2 + e]) for r in range(4))
            pre_ref[rows, e * 256 : (e + 1) * 256] = gate_pre.astype(BF)
            pre_ref[rows, (2 + e) * 256 : (3 + e) * 256] = up_pre.astype(BF)
            gate = jnp.sum(jnp.where(expert == e, gates, 0.0), axis=1, keepdims=True)
            mid = (gate_pre * jax.nn.sigmoid(gate_pre) * up_pre * gate).astype(BF)
            mid_ref[rows, e * 256 : (e + 1) * 256] = mid
            mids.append(mid)
        for r in range(4):
            made = nt(mids[0], weight_ref[r, 4]) + nt(mids[1], weight_ref[r, 5])
            out_ref[:, r * 384 : (r + 1) * 384] = made.astype(BF)


def experts_forward(where, tokens, routed, router, weights):
    return pl.pallas_call(
        expert_kernel,
        grid=(1,),
        in_specs=[SMEM, whole(4, 6, 384, 256), whole(16, D), whole(512, 128)] + [whole(64, D)] * 8,
        out_specs=[whole(256, D)] * 2 + [whole(512, 1024), whole(512, 512), whole(512, 16), whole(512, D)],
        out_shape=[shaped(256, D), shaped(256, D), shaped(512, 1024), shaped(512, 512)]
        + [shaped(512, 16, dtype=F32), shaped(512, D)],
        compiler_params=params(48),
        cost_estimate=cost(512 * 1536 * 1536 * 2, 10 << 20, 512 * 512),
        name="experts_forward",
    )(where, weights, router, routed, *tokens)


def expert_back_kernel(order_ref, weight_ref, router_ref, pre_ref, gates_ref, *refs):
    grad_refs, (pa_ref, pb_ref, gpre_ref, gated_ref) = refs[:-4], refs[-4:]
    if len(grad_refs) > 1:
        grad_refs, all_ref = grad_refs[:8], refs[8]
    for h, out_ref in enumerate((pa_ref, pb_ref)):
        rows = pl.ds(h * 256, 256)
        if len(grad_refs) > 1:
            grad_out = stacked(grad_refs[4 * h : 4 * h + 4])
            all_ref[rows] = grad_out
        else:
            grad_out = grad_refs[0][rows]
        parts = [grad_out[:, r * 384 : (r + 1) * 384] for r in range(4)]
        gates = gates_ref[rows]
        expert = lax.broadcasted_iota(jnp.int32, (256, 16), 1) - 2 * order_ref[3]
        gated = jnp.zeros((256, 16), F32)
        grads = []
        for e in range(2):
            raw = sum(nn(parts[r], weight_ref[r, 4 + e]) for r in range(4))
            gate_pre = pre_ref[rows, e * 256 : (e + 1) * 256].astype(F32)
            up_pre = pre_ref[rows, (2 + e) * 256 : (3 + e) * 256].astype(F32)
            sigmoid = jax.nn.sigmoid(gate_pre)
            activated = gate_pre * sigmoid
            grad_gates = jnp.sum(activated * up_pre * raw, axis=1, keepdims=True)
            gated = jnp.where(expert == e, gates * grad_gates, gated)
            raw = raw * jnp.sum(jnp.where(expert == e, gates, 0.0), axis=1, keepdims=True)
            grad_gate = (raw * up_pre * sigmoid * (1.0 + gate_pre * (1.0 - sigmoid))).astype(BF)
            grad_up = (raw * activated).astype(BF)
            gpre_ref[rows, e * 256 : (e + 1) * 256] = grad_gate
            gpre_ref[rows, (2 + e) * 256 : (3 + e) * 256] = grad_up
            grads.append((grad_gate, grad_up))
        gated_ref[rows] = gated
        high = gated.astype(BF)
        low = (gated - high.astype(F32)).astype(BF)
        for r in range(4):
            router = router_ref[:, r * 384 : (r + 1) * 384]
            made = nn(high, router) + nn(low, router)
            for e in range(2):
                made = made + nt(grads[e][0], weight_ref[r, e]) + nt(grads[e][1], weight_ref[r, 2 + e])
            out_ref[:, r * 384 : (r + 1) * 384] = made.astype(BF)


def experts_backward(where, grads, pre, gates, router, weights, *earlier):
    pieces = len(grads) > 1
    outs = pl.pallas_call(
        ignoring(len(earlier), expert_back_kernel),
        grid=(1,),
        in_specs=[ANY] * len(earlier)
        + [SMEM, whole(4, 6, 384, 256), whole(16, D), whole(512, 1024), whole(512, 16)]
        + ([whole(64, D)] * 8 if pieces else [whole(512, D)]),
        out_specs=[whole(512, D)] * pieces + [whole(256, D), whole(256, D), whole(512, 1024), whole(512, 16)],
        out_shape=[shaped(512, D)] * pieces
        + [shaped(256, D), shaped(256, D), shaped(512, 1024), shaped(512, 16, dtype=F32)],
        compiler_params=params(48),
        cost_estimate=cost(512 * 1536 * 1536 * 2, 10 << 20, 512 * 512),
        name="experts_backward",
    )(*earlier, where, weights, router, pre, gates, *grads)
    return outs if pieces else [grads[0]] + list(outs)


def expert_weight_kernel(gpre_ref, mid_ref, tokens_ref, grads_ref, out_ref):
    for n in range(6):
        left_ref, right_ref = (tokens_ref, gpre_ref) if n < 4 else (grads_ref, mid_ref)
        out_ref[0, n] = tn(left_ref[...], right_ref[:, (n % 4) * 256 : (n % 4 + 1) * 256]).astype(BF)


def expert_weight_grads(tokens, grads, gpre, mid, *earlier):
    return pl.pallas_call(
        ignoring(len(earlier), expert_weight_kernel),
        grid=(4,),
        in_specs=[ANY] * len(earlier) + [whole(512, 1024), whole(512, 512)] + [column(512, 384, 0)] * 2,
        out_specs=pl.BlockSpec((1, 6, 384, 256), lambda r: (r, 0, 0, 0)),
        out_shape=shaped(4, 6, 384, 256),
        compiler_params=params(40),
        cost_estimate=cost(512 * 1536 * 1536 * 2, 10 << 20),
        name="expert_weight_grads",
    )(*earlier, gpre, mid, tokens, grads)


def chosen(size, width, me):
    row = lax.broadcasted_iota(jnp.int32, (size, width), 0)
    lane = lax.broadcasted_iota(jnp.int32, (size, width), 1)
    return (row == lane + me * width).astype(BF)


def source(where_ref, b):
    return ((where_ref[1] - (b & 3)) & 3) * 2 + (where_ref[2] if b < 4 else 1 - where_ref[2])


def out_slice_kernel(where_ref, left_ref, right_ref, gated_ref, gates_ref, gains_ref, tokens_ref, out_ref):
    me = where_ref[3]
    pick = chosen(768, 96, me)
    left = jnp.concatenate([nn(left_ref[b, :, 1536:2304], pick).astype(BF) for b in range(8)], axis=0)
    right = jnp.concatenate([right_ref[b, :, 0:1536] for b in range(8)], axis=0)
    rows = tn(left, right)
    lane = lax.broadcasted_iota(jnp.int32, (64, 16), 1)
    logits = []
    for b in range(8):
        block = slice(b * 64, (b + 1) * 64)
        lanes = right_ref[source(where_ref, b), :, 1536:1664].astype(F32)
        inner = lanes[:, 0:1] + lanes[:, 1:2]
        grad = gated_ref[block] - 0.5 * gates_ref[block] * inner
        one = [jnp.sum(jnp.where(lane == 2 * me + e, grad, 0.0), axis=1, keepdims=True) for e in range(2)]
        logits.append(jnp.where(lane == 0, one[0], jnp.where(lane == 1, one[1], 0.0)).astype(BF))
    extra = tn(jnp.concatenate(logits, axis=0), tokens_ref[...])
    row = lax.broadcasted_iota(jnp.int32, (16, D), 0)
    gains = gains_ref[...]
    extra = jnp.where(row == 2, gains[0:1], jnp.where(row == 3, gains[1:2], extra))
    for r in range(4):
        to = (where_ref[0] - r) & 3
        out_ref[to, 0:96] = rows[:, r * 384 : (r + 1) * 384].astype(BF)
        out_ref[to, 96:112] = extra[:, r * 384 : (r + 1) * 384].astype(BF)


def out_slice(where, left, right, gated, gates, gains, tokens, *earlier):
    return pl.pallas_call(
        ignoring(len(earlier), out_slice_kernel),
        grid=(1,),
        in_specs=[ANY] * len(earlier)
        + [SMEM, whole(8, 64, 2304), whole(8, 64, 1664), whole(512, 16), whole(512, 16), whole(2, D), whole(512, D)],
        out_specs=whole(4, 112, 384),
        out_shape=shaped(4, 112, 384),
        compiler_params=params(40),
        cost_estimate=cost(512 * 1536 * 256, 6 << 20),
        name="out_slice",
    )(*earlier, where, left, right, gated, gates, gains, tokens)


def qkv_slice_kernel(relative, where_ref, left_ref, gain_ref, *refs):
    out_ref = refs[-1]
    me = where_ref[3]
    pick = chosen(1536, 192, me)
    if relative:
        right = stacked(refs[:8])
        order = [source(where_ref, b) for b in range(8)]
    else:
        right = jnp.concatenate([refs[0][b, :, 1664:2944] for b in range(8)], axis=0)
        order = list(range(8))
    left = jnp.concatenate([nn(left_ref[b, :, 0:1536], pick).astype(BF) for b in order], axis=0)
    rows = tn(left, right).astype(BF)
    row = lax.broadcasted_iota(jnp.int32, (8, 384), 0)
    for r in range(4):
        to = (where_ref[0] - r) & 3
        out_ref[to, 0:48] = rows[r * 48 : (r + 1) * 48]
        out_ref[to, 48:56, 0:384] = jnp.where(row == 0, gain_ref[:, r * 384 : (r + 1) * 384], 0.0).astype(BF)
        out_ref[to, 48:56, 384:1280] = jnp.zeros((8, 896), BF)


def qkv_slice(where, left, gain, rights, *earlier):
    relative = len(rights) == 8
    specs = [whole(64, 1280)] * 8 if relative else [whole(8, 64, 2944)]
    return pl.pallas_call(
        ignoring(len(earlier), functools.partial(qkv_slice_kernel, relative)),
        grid=(1,),
        in_specs=[ANY] * len(earlier) + [SMEM, whole(8, 64, 2304), whole(1, D)] + specs,
        out_specs=whole(4, 56, 1280),
        out_shape=shaped(4, 56, 1280),
        compiler_params=params(40),
        cost_estimate=cost(512 * 1536 * 512, 6 << 20),
        name="qkv_slice",
    )(*earlier, where, left, gain, *rights)


def qkv_rows_kernel(in_ref, q_ref, k_ref, v_ref):
    for x in range(4):
        rows = slice(x * 48, (x + 1) * 48)
        q_ref[rows] = in_ref[x, 0, 0:48, 0:768].astype(F32)
        k_ref[rows] = in_ref[x, 0, 0:48, 768:1024].astype(F32)
        v_ref[rows] = in_ref[x, 0, 0:48, 1024:1280].astype(F32)


def qkv_rows(everything):
    rows = lambda width: pl.BlockSpec((192, width), lambda j: (j, 0))
    return pl.pallas_call(
        qkv_rows_kernel,
        grid=(8,),
        in_specs=[pl.BlockSpec((4, 1, 56, 1280), lambda j: (0, j, 0, 0))],
        out_specs=[rows(768), rows(256), rows(256)],
        out_shape=[shaped(D, 768, dtype=F32), shaped(D, 256, dtype=F32), shaped(D, 256, dtype=F32)],
        compiler_params=params(32),
        cost_estimate=cost(0, 12 << 20),
        name="qkv_rows",
    )(everything)


def out_rows_kernel(in_ref, out_ref):
    for x in range(4):
        out_ref[:, x * 384 : (x + 1) * 384] = in_ref[x, 0, 0:96].astype(F32)


def out_rows(everything):
    return pl.pallas_call(
        out_rows_kernel,
        grid=(8,),
        in_specs=[pl.BlockSpec((4, 1, 112, 384), lambda j: (0, j, 0, 0))],
        out_specs=pl.BlockSpec((96, D), lambda j: (j, 0)),
        out_shape=shaped(768, D, dtype=F32),
        compiler_params=params(32),
        cost_estimate=cost(0, 7 << 20),
        name="out_rows",
    )(everything)


def gates_of(tokens, router, routed):
    logits = dot(tokens, router)
    top = jnp.max(jnp.where(routed > 0, logits, NEGATIVE), axis=1, keepdims=True)
    raised = jnp.where(routed > 0, jnp.exp(jnp.minimum(logits - top, 0.0)), 0.0)
    return raised / jnp.sum(raised, axis=1, keepdims=True)


X_GROUPS = [[(x * NY + y) * 2 + c for x in range(NX)] for y in range(NY) for c in range(2)]


Y_GROUPS = [[(x * NY + y) * 2 + c for y in range(NY) for c in range(2)] for x in range(NX)]


def replica_gather(shard):
    return lax.all_gather(shard, "dp", axis=0, axis_index_groups=X_GROUPS)


def replica_scatter(grads):
    flat = grads.reshape(-1, grads.shape[-1])
    return lax.psum_scatter(flat, "dp", scatter_dimension=0, axis_index_groups=X_GROUPS, tiled=True)


def after(value, *others):
    return lax.optimization_barrier((value, *others))[0]


def group_pieces(block):
    near = [block] + [moved(block, 0, j, 0) for j in (1, 2, 3)]
    return near + [moved(piece, 0, 0, 1) for piece in near]


def ordered(value):
    probe = value[(0,) * value.ndim]
    return probe == probe


def behind(value, earlier):
    return jnp.where(ordered(earlier), value, jnp.zeros_like(value))


def per_device(
    inputs,
    cotangent,
    segments,
    routes,
    norm_first,
    w_query,
    w_key,
    w_value,
    w_out,
    norm_second,
    w_router,
    w_gate,
    w_up,
    w_down,
):
    section = lax.axis_index("section")
    place = lax.axis_index("dp")
    here_x, here_y, here_c = place // (NY * 2), place // 2 % NY, place % 2
    me = place % 8
    first = section == 0
    rows = inputs.shape[1]

    def in_order(own, other):
        return jnp.where(first, own, other), jnp.where(first, other, own)

    def pick(pair):
        return lax.dynamic_index_in_dim(pair, section, 0, False)

    qkv_own = jnp.concatenate([w_query[0], w_key[0], w_value[0]], axis=1)
    act_both = norm_apply(inputs.astype(F32), norm_first[0]).astype(BF)
    qkv_both = dot(act_both.reshape(2 * rows, D), qkv_own).astype(BF)
    qkv_sent = lax.ppermute(qkv_both[rows:], "section", [(0, 1)])
    qkv_first = jnp.where(first, qkv_both[:rows], qkv_sent)

    pack = jnp.concatenate([norm_first, norm_second, w_router[0].T.astype(F32)], axis=0)
    packs = in_order(pack, swapped(pack, "section"))
    routers = [p[2:].astype(BF) for p in packs]
    experts = jnp.concatenate([w_gate[0], w_up[0], jnp.swapaxes(w_down[0], 1, 2)], axis=0)
    experts_other = swapped(experts, "section")
    expert_weights = [None, None]
    dense = jnp.concatenate(
        [lax.dynamic_slice_in_dim(qkv_own, place * 48, 48, 0)[:, i * 256 : (i + 1) * 256] for i in range(5)]
        + [lax.dynamic_slice_in_dim(w_out[0], place * 24, 24, 0)[:, i * 256 : (i + 1) * 256] for i in range(6)],
        axis=0,
    )
    dense = swapped(dense, "section")
    where = jnp.stack([here_x, here_y, here_c, me]).astype(jnp.int32)

    labels = pick(segments)
    query_labels = lax.dynamic_slice_in_dim(labels, place * rows, rows, 0)
    starts = jnp.sum((labels[None, :] < query_labels[:, None]).astype(jnp.int32), axis=1)
    masks = (where, jnp.concatenate([starts, starts])[None])

    own_routes = pick(routes)
    expert_ids = jnp.arange(EXPERTS, dtype=jnp.int32)
    routed_own = jnp.sum((own_routes[:, :, None] == expert_ids).astype(F32), axis=1)
    given = pick(cotangent)
    sent = jnp.concatenate([given, jnp.pad(routed_own.astype(BF), ((0, 0), (0, 128 - EXPERTS)))], axis=1)
    got = group_pieces(sent)
    given_all = jnp.concatenate(got, axis=0)
    routed = jnp.concatenate([piece[:, D:] for piece in got], axis=0)

    hidden = pick(inputs).astype(F32)
    saved = []
    outs_w = qkvs_w = None
    for layer in range(2):
        gain_one, gain_two = packs[layer][0], packs[layer][1]
        activation = norm_apply(hidden, gain_one).astype(BF)
        qkv = qkv_first if layer == 0 else dot(activation, qkvs_w[1]).astype(BF)
        query, pair = qkv[:, :768], qkv[:, 768:]
        slab = along_x(pair)
        if layer == 0:
            experts_first = jnp.where(first & ordered(slab), experts, experts_other)
            expert_weights[0] = replica_gather(experts_first)
            slab = behind(slab, experts_first)
        near = [slab] + [moved(slab, 0, j, 0) for j in (1, 2, 3)]
        pieces = near + [moved(piece, 0, 0, 1) for piece in near]
        mixed, log_total = attend_forward(masks, query, pieces, *([] if layer == 0 else [saved[0][-2]]))
        if layer == 0:
            mixed_sent = lax.ppermute(mixed, "section", [(1, 0)])
            partial = dot(jnp.concatenate([mixed, mixed_sent], axis=0), w_out[0]).astype(BF)
            both_axes = ("section", "tensor")
            straight = lax.ppermute(partial[rows:], both_axes, [(0, 2), (1, 3)])
            across = lax.ppermute(partial[rows:], both_axes, [(0, 3), (1, 2)])
            turned = lax.ppermute(partial[:rows], both_axes, [(0, 1), (1, 0)])
            middle = hidden + (
                jnp.where(first, partial[:rows], straight).astype(F32) + jnp.where(first, turned, across).astype(F32)
            )
            dense_all = lax.all_gather(behind(dense, pieces[3]), "dp", axis=0)
            other_qkv = jnp.swapaxes(dense_all[:, :240].reshape(32, 5, 48, 256), 1, 2).reshape(D, 1280)
            other_out = jnp.swapaxes(dense_all[:, 240:].reshape(32, 6, 24, 256), 1, 2).reshape(768, D)
            qkvs_w = in_order(qkv_own, other_qkv)
            outs_w = in_order(w_out[0], other_out)
            experts_second = jnp.where(first & ordered(mixed), experts_other, experts)
            expert_weights[1] = replica_gather(experts_second)
        else:
            middle = hidden + tensor_sum(dot(mixed, outs_w[layer]))
        second = norm_apply(middle, gain_two).astype(BF)
        tokens = group_pieces(second)
        made_near, made_far, pre, mid, gates, tokens = experts_forward(
            where, tokens, routed, routers[layer], expert_weights[layer]
        )
        made = group_sum(made_near, made_far).reshape(rows, D).astype(BF)
        if layer == 0:
            made = behind(made, qkvs_w[1])
        branch = tensor_sum(made)
        result = middle + branch
        cut = behind(jnp.concatenate([activation, mixed], axis=1), result)
        lefts = lax.all_gather(cut, "dp", axis=0, axis_index_groups=Y_GROUPS)
        saved.append(
            (hidden, query, pieces, log_total, middle, second, tokens, pre, mid, gates, branch, lefts, cut, result)
        )
        hidden = result

    def own_of(a, b):
        return jnp.where(first, a, b)

    def from_other(for_first, for_second):
        return swapped(own_of(for_second, for_first).astype(BF), "section").astype(F32)

    def over_sections(a, b):
        return own_of(a, b).astype(F32) + from_other(a, b)

    grad_output = given.astype(F32)
    grads = []
    earlier = [saved[1][-2]]
    for layer in (1, 0):
        hidden, query, pieces, log_total, middle, second, tokens, pre, mid, gates, branch, lefts, _, _ = saved[layer]
        gain_one, gain_two = packs[layer][0], packs[layer][1]
        router = routers[layer]
        grad_pieces = [given_all] if layer == 1 else group_pieces(grad_output.astype(BF))
        grad_all, back_near, back_far, grad_pre, gated = experts_backward(
            where, grad_pieces, pre, gates, router, expert_weights[layer], *earlier
        )
        both = (back_near.astype(F32) + moved(back_far, 0, 0, 1).astype(F32)).astype(BF)
        weight_grads = expert_weight_grads(tokens, grad_all, grad_pre, mid, both)
        expert_part = replica_scatter(weight_grads)
        grad_second = tensor_sum(back_y(both).reshape(rows, D))
        inner = jnp.sum(grad_output * branch, axis=1, keepdims=True)
        own_gates = gates_of(second, router.T, routed_own)
        grad_second = grad_second - dot(inner * own_gates, router.astype(F32))
        grad_from_norm, gain_two_grad = norm_back(middle, gain_two, grad_second)
        grad_middle = grad_output + grad_from_norm
        grad_branch = grad_middle.astype(BF)
        inner_high = inner.astype(BF)
        inner_low = (inner - inner_high.astype(F32)).astype(BF)
        lanes = jnp.concatenate([inner_high, inner_low, jnp.zeros((rows, 126), BF)], axis=1)
        right = jnp.concatenate([grad_branch, lanes], axis=1)
        grad_mixed = against(grad_branch, outs_w[layer]).astype(BF)
        if layer == 1:
            earlier = [weight_grads, lefts, saved[0][-3]]
        else:
            earlier = [weight_grads, right, grads[0][3]]
        grad_query, back_near, back_far = attend_backward(masks, query, grad_mixed, log_total, pieces, *earlier)
        both = (back_near.astype(F32) + moved(back_far, 0, 0, 1).astype(F32)).astype(BF)
        if layer == 0:
            late = grads[0]
            out_blocks = [out_slice(where, *late[2], both)]
            late_qkv = qkv_slice(where, late[2][0], jnp.zeros((1, D), F32), [late[2][1]], both)
            late_qkv = back_x(late_qkv.reshape(224, 1280)).reshape(56, 1280)
        half = back_y(both)
        grad_pair = back_x(half.astype(BF)).reshape(rows, 512).astype(BF)
        grad_qkv = jnp.concatenate([grad_query, grad_pair], axis=1)
        grad_activation = tensor_sum(against(grad_qkv, qkvs_w[layer]))
        grad_from_first, gain_one_grad = norm_back(hidden, gain_one, grad_activation)
        grad_input = grad_middle + grad_from_first
        if layer == 1:
            gains = jnp.stack([gain_two_grad, gain_one_grad])
            right = jnp.concatenate([right, grad_qkv], axis=1)
            earlier = [right]
            right = lax.all_gather(right, "dp", axis=0, axis_index_groups=Y_GROUPS)
            grads.append((grad_input, None, (lefts, right, gated, gates, gains, tokens), expert_part))
        else:
            gains = jnp.stack([gain_two_grad, jnp.zeros_like(gain_two_grad)])
            right = lax.all_gather(right, "dp", axis=0, axis_index_groups=Y_GROUPS)
            out_blocks = [out_slice(where, lefts, right, gated, gates, gains, tokens, half)] + out_blocks
            out_blocks = over_sections(*out_blocks).astype(BF)
            out_sum = back_x(out_blocks.reshape(448, 384)).reshape(112, 384).astype(BF)
            qkv_blocks = qkv_slice(where, lefts, gain_one_grad[None], group_pieces(grad_qkv), out_sum, expert_part)
            qkv_part = back_x(qkv_blocks.reshape(224, 1280)).reshape(56, 1280)
            grads.append((grad_input, qkv_part, None, expert_part))
        grad_output = grad_input
    grads = grads[::-1]

    def by_batch(own, other):
        return jnp.stack([jnp.where(first, own, other), jnp.where(first, other, own)])[None]

    results = by_batch(own_of(saved[0][-1], saved[1][-1]), from_other(saved[0][-1], saved[1][-1]))
    input_grads = by_batch(own_of(grads[0][0], grads[1][0]), from_other(grads[0][0], grads[1][0]))
    qkv_sum = over_sections(grads[0][1], late_qkv).astype(BF)
    out_all = lax.all_gather(out_sum, "dp", axis=0).reshape(4, 8, 112, 384)
    qkv_all = lax.all_gather(qkv_sum, "dp", axis=0).reshape(4, 8, 56, 1280)
    query_sum, key_sum, value_sum = qkv_rows(qkv_all)
    out_full = out_rows(out_all)
    router_sum = jnp.transpose(out_all[:, :, 96:98], (1, 2, 0, 3)).reshape(EXPERTS, D)
    router_sum = tensor_sum(router_sum)
    gain_two_sum = jnp.sum(out_all[:, :, 98].astype(F32), axis=1).reshape(1, D)
    gain_one_sum = jnp.sum(out_all[:, :, 99].astype(F32) + qkv_all[:, :, 48, :384].astype(F32), axis=1).reshape(1, D)
    expert_sum = over_sections(grads[0][3], grads[1][3]).reshape(3, 2, 384, 256)
    return (
        results,
        input_grads,
        gain_one_sum,
        query_sum[None],
        key_sum[None],
        value_sum[None],
        out_full[None],
        gain_two_sum,
        router_sum.T[None],
        expert_sum[0][None],
        expert_sum[1][None],
        jnp.swapaxes(expert_sum[2], 1, 2)[None],
    )


def solution(mesh):
    in_specs = (
        P(None, "dp", None),
        P(None, "dp", None),
        P(),
        P(None, "dp", None),
        P("section", None),
        P("section", None, "tensor"),
        P("section", None, "tensor"),
        P("section", None, "tensor"),
        P("section", "tensor", None),
        P("section", None),
        P("section", None, None),
        P("section", "dp", None, "tensor"),
        P("section", "dp", None, "tensor"),
        P("section", "dp", "tensor", None),
    )
    out_specs = (
        P("section", None, "dp", None),
        P("section", None, "dp", None),
        P("section", None),
        P("section", None, "tensor"),
        P("section", None, "tensor"),
        P("section", None, "tensor"),
        P("section", "tensor", None),
        P("section", None),
        P("section", None, None),
        P("section", "dp", None, "tensor"),
        P("section", "dp", None, "tensor"),
        P("section", "dp", "tensor", None),
    )
    return jax.shard_map(
        per_device, mesh=mesh, in_specs=in_specs, out_specs=out_specs, check_vma=False
    )
```

```python
import functools

import jax
import jax.numpy as jnp
from jax import lax
from jax.experimental import pallas as pl
from jax.experimental.pallas import tpu as pltpu
from jax.sharding import PartitionSpec as P

D = 1536
HD = 64
EXPERTS = 16
NX, NY = 4, 4
EPSILON = 1e-06
SCALE = 0.125
NEGATIVE = -1e30
BF = jnp.bfloat16
F32 = jnp.float32


def moved(value, dx, dy, dc):
    route = []
    for x in range(NX):
        for y in range(NY):
            for c in range(2):
                target = (((x + dx) % NX) * NY + (y + dy) % NY) * 2 + (c ^ dc)
                route.append(((x * NY + y) * 2 + c, target))
    return lax.ppermute(value, "dp", route)


def swapped(value, axis):
    return lax.ppermute(value, axis, [(0, 1), (1, 0)])


def along_y(block):
    return jnp.concatenate([block] + [moved(block, 0, j, 0) for j in (1, 2, 3)], axis=0)


def along_x(block):
    return jnp.concatenate([block] + [moved(block, j, 0, 0) for j in (1, 2, 3)], axis=0)


def back_y(sums):
    parts = sums.reshape(4, -1, sums.shape[-1])
    total = parts[0].astype(F32)
    for j in (1, 2, 3):
        total = total + moved(parts[j], 0, -j, 0).astype(F32)
    return total


def back_x(sums):
    parts = sums.reshape(4, -1, sums.shape[-1])
    total = parts[0].astype(F32)
    for j in (1, 2, 3):
        total = total + moved(parts[j], -j, 0, 0).astype(F32)
    return total


def group_gather(block):
    column = along_y(block)
    return column, moved(column, 0, 0, 1)


def group_sum(own, other):
    both = own.astype(F32) + moved(other, 0, 0, 1).astype(F32)
    return back_y(both.astype(BF))


def tensor_sum(value):
    low = value.astype(BF)
    return low.astype(F32) + swapped(low, "tensor").astype(F32)


def norm_apply(value, gain):
    inverse = lax.rsqrt(jnp.mean(value * value, axis=-1, keepdims=True) + EPSILON)
    return value * inverse * gain


def norm_back(value, gain, grad):
    inverse = lax.rsqrt(jnp.mean(value * value, axis=-1, keepdims=True) + EPSILON)
    scaled = grad * gain
    inner = jnp.mean(scaled * value, axis=-1, keepdims=True)
    gain_grad = jnp.sum(grad * value * inverse, axis=0)
    return (inverse * scaled - inverse * inverse * inverse * value * inner, gain_grad)


def dot(left, right):
    return jnp.dot(left, right, preferred_element_type=F32)


def over_rows(left, right):
    return lax.dot_general(left, right, (((0,), (0,)), ((), ())), preferred_element_type=F32)


def against(left, right):
    return lax.dot_general(left, right, (((1,), (1,)), ((), ())), preferred_element_type=F32)


def nn(a, b):
    return lax.dot_general(a, b, (((1,), (0,)), ((), ())), preferred_element_type=F32)


def nt(a, b):
    return lax.dot_general(a, b, (((1,), (1,)), ((), ())), preferred_element_type=F32)


def tn(a, b):
    return lax.dot_general(a, b, (((0,), (0,)), ((), ())), preferred_element_type=F32)


SMEM = pl.BlockSpec(memory_space=pltpu.SMEM)
VMEM = pl.BlockSpec(memory_space=pltpu.VMEM)
ANY = pl.BlockSpec(memory_space=pl.ANY)


def shaped(*shape, dtype=BF):
    return jax.ShapeDtypeStruct(shape, dtype)


def params(mib):
    del mib
    return pltpu.CompilerParams(vmem_limit_bytes=58 << 20)


def cost(flops, bytes_accessed, exps=0):
    return pl.CostEstimate(flops=flops, bytes_accessed=bytes_accessed, transcendentals=exps)


def stacked(refs):
    return jnp.concatenate([ref[...] for ref in refs], axis=0)


def spread(block):
    lane = lax.broadcasted_iota(jnp.int32, (64, 128), 1)
    parts = []
    for k in range(6):
        wide = block[:, (k // 2) * 128 : (k // 2 + 1) * 128].astype(F32)
        half = k // 3
        if k % 2 != half:
            wide = pltpu.roll(wide, 64, 1)
        parts.append(jnp.where((lane >= 64) == (half == 1), wide, 0.0))
    return jnp.concatenate(parts, axis=0)


def gathered(turned):
    rows = turned.T
    lane = lax.broadcasted_iota(jnp.int32, (64, 128), 1)
    outs = []
    for b in range(3):
        two = []
        for k in (2 * b, 2 * b + 1):
            part = rows[k * 64 : (k + 1) * 64]
            if k % 2 != k // 3:
                part = pltpu.roll(part, 64, 1)
            two.append(part)
        outs.append(jnp.where(lane < 64, two[0], two[1]))
    return jnp.concatenate(outs, axis=1)


def bias_of(place_ref, h, start_ref):
    row = lax.broadcasted_iota(jnp.int32, (1024, 128), 0)
    token = lax.broadcasted_iota(jnp.int32, (1024, 128), 1) & 63
    x = (place_ref[0] - (row >> 6)) & 3
    y = (place_ref[1] - (row >> 8)) & 3
    c = place_ref[2] if h == 0 else 1 - place_ref[2]
    key = ((x * 4 + y) * 2 + c) * 64 + (row & 63)
    query = ((place_ref[0] * 4 + place_ref[1]) * 2 + place_ref[2]) * 64 + token
    bias = jnp.where((key <= query) & (key >= start_ref[...]), 0.0, NEGATIVE)
    return jnp.concatenate([bias, bias, bias], axis=1)


def attend_kernel(place_ref, st_ref, q_ref, *refs):
    keys = [stacked(refs[0:4]), stacked(refs[4:8])]
    values = [stacked(refs[8:12]), stacked(refs[12:16])]
    out_ref, lse_ref = refs[16:]
    query = (spread(q_ref[...]) * 0.125).astype(BF)
    scores = [nt(k, query) + bias_of(place_ref, h, st_ref) for h, k in enumerate(keys)]
    top = jnp.maximum(*[jnp.max(s, axis=0, keepdims=True) for s in scores])
    total = jnp.zeros_like(top)
    mixed = jnp.zeros((128, 384), F32)
    for s, v in zip(scores, values):
        raised = jnp.exp(s - top)
        total = total + jnp.sum(raised, axis=0, keepdims=True)
        mixed = mixed + tn(v, raised.astype(BF))
    out_ref[...] = gathered(mixed / total).astype(BF)
    lse_ref[0] = top + jnp.log(total)


def column(rows, width, base):
    return pl.BlockSpec((rows, width), lambda j: (0, j + base))


PAIRS = [SMEM, pl.BlockSpec((1, 128), lambda j: (0, 0))], [column(256, 128, 0)] * 8 + [column(256, 128, 2)] * 8
LSE = pl.BlockSpec((1, 1, 384), lambda j: (j, 0, 0))


def ignoring(count, kernel):
    return lambda *refs: kernel(*refs[count:])


def attend_forward(masks, query, pieces, *earlier):
    return pl.pallas_call(
        ignoring(len(earlier), attend_kernel),
        grid=(2,),
        in_specs=[ANY] * len(earlier) + PAIRS[0] + [column(64, 384, 0)] + PAIRS[1],
        out_specs=[column(64, 384, 0), LSE],
        out_shape=[shaped(64, 768), shaped(2, 1, 384, dtype=F32)],
        compiler_params=params(40),
        cost_estimate=cost(12 * 64 * 2048 * 64 * 4, 2 << 20, 12 * 64 * 2048),
        name="attend_forward",
    )(*earlier, *masks, query, *pieces, *pieces)


def attend_back_kernel(place_ref, st_ref, q_ref, do_ref, lse_ref, *refs):
    j = pl.program_id(0)
    key_columns = pl.ds(pl.multiple_of(j * 128, 128), 128)
    value_columns = pl.ds(pl.multiple_of(256 + j * 128, 128), 128)
    keys = [stacked(refs[0:4]), stacked(refs[4:8])]
    values = [stacked(refs[8:12]), stacked(refs[12:16])]
    dq_ref, near_ref, far_ref = refs[16:]
    query = (spread(q_ref[...]) * 0.125).astype(BF)
    grad = spread(do_ref[...]).astype(BF)
    weights, raws = [], []
    inner = jnp.zeros((1, 384), F32)
    for h, (k, v) in enumerate(zip(keys, values)):
        s = nt(k, query) + bias_of(place_ref, h, st_ref)
        w = jnp.exp(s - lse_ref[0])
        raw = nt(v, grad)
        inner = inner + jnp.sum(w * raw, axis=0, keepdims=True)
        weights.append(w)
        raws.append(raw)
    turned = jnp.zeros((128, 384), F32)
    for w, raw, k, out_ref in zip(weights, raws, keys, (near_ref, far_ref)):
        ds = (w * (raw - inner)).astype(BF)
        out_ref[:, key_columns] = nn(ds, query).astype(BF)
        out_ref[:, value_columns] = nn(w.astype(BF), grad).astype(BF)
        turned = turned + tn(k, ds)
    dq_ref[...] = gathered(turned * 0.125).astype(BF)


def attend_backward(masks, query, grad, lse, pieces, *earlier):
    return pl.pallas_call(
        ignoring(len(earlier), attend_back_kernel),
        grid=(2,),
        in_specs=[ANY] * len(earlier) + PAIRS[0] + [column(64, 384, 0)] * 2 + [LSE] + PAIRS[1],
        out_specs=[column(64, 384, 0)] + [pl.BlockSpec((1024, 512), lambda j: (0, 0))] * 2,
        out_shape=[shaped(64, 768), shaped(1024, 512), shaped(1024, 512)],
        compiler_params=params(48),
        cost_estimate=cost(12 * 64 * 2048 * 64 * 10, 4 << 20, 12 * 64 * 2048),
        name="attend_backward",
    )(*earlier, *masks, query, grad, lse, *pieces, *pieces)


def choose_kernel(layer, section_ref, gate_ref, up_ref, down_ref, sent_gate_ref, sent_ref, out_ref, sems):
    def copied(pairs):
        copies = [pltpu.make_async_copy(a, b, sems.at[i]) for i, (a, b) in enumerate(pairs)]
        for copy in copies:
            copy.start()
        for copy in copies:
            copy.wait()

    gates, ups, downs = out_ref.at[0:2], out_ref.at[2:4], out_ref.at[4:6]

    @pl.when(section_ref[0] == layer)
    def _():
        copied([(gate_ref, gates), (up_ref, ups), (down_ref, downs)])

    @pl.when(section_ref[0] != layer)
    def _():
        copied([(sent_gate_ref, gates), (sent_ref, out_ref.at[2:6])])


def choose(layer, section, parts, *earlier):
    return pl.pallas_call(
        ignoring(len(earlier), lambda *refs: choose_kernel(layer, *refs)),
        in_specs=[ANY] * len(earlier) + [SMEM] + [ANY] * len(parts),
        out_specs=VMEM,
        out_shape=shaped(6, 384, 256),
        scratch_shapes=[pltpu.SemaphoreType.DMA((3,))],
        compiler_params=params(16),
        cost_estimate=cost(0, 3 << 20),
        name="choose",
    )(*earlier, section, *parts)


def side_by_side(parts, axis, *earlier):
    def kernel(*refs):
        refs[-1][...] = jnp.concatenate([ref[...] for ref in refs[:-1]], axis=axis)

    shape = list(parts[0].shape)
    shape[axis] = sum(part.shape[axis] for part in parts)
    return pl.pallas_call(
        ignoring(len(earlier), kernel),
        in_specs=[ANY] * len(earlier) + [VMEM] * len(parts),
        out_specs=VMEM,
        out_shape=jax.ShapeDtypeStruct(tuple(shape), parts[0].dtype),
        compiler_params=params(16),
        cost_estimate=cost(0, 2 << 20),
        name="side_by_side",
    )(*earlier, *parts)


def fetched(own, refs, held, sems, where_ref, others):
    def copies(pairs):
        return [pltpu.make_async_copy(a, b, sems.at[i]) for i, (a, b) in enumerate(pairs)]

    mine, sent = copies(refs), copies(others)
    is_own = where_ref[4] == own

    @pl.when(is_own)
    def _():
        for copy in mine:
            copy.start()

    @pl.when(jnp.logical_not(is_own))
    def _():
        for copy in sent:
            copy.start()

    def wait():
        @pl.when(is_own)
        def _():
            for copy in mine:
                copy.wait()

        @pl.when(jnp.logical_not(is_own))
        def _():
            for copy in sent:
                copy.wait()

    return wait


def fetch_qkv(layer, where_ref, q_ref, k_ref, v_ref, sent_ref, held, sems):
    own = [(q_ref, held.at[:, 0:768]), (k_ref, held.at[:, 768:1024]), (v_ref, held.at[:, 1024:1280])]
    return fetched(layer, own, held, sems, where_ref, [(sent_ref.at[:, 0:1280], held)])


def fetch_out(layer, where_ref, out_ref, sent_ref, held, sems):
    halves = [
        (sent_ref.at[h * 768 : (h + 1) * 768, 1280:2048], held.at[:, h * 768 : (h + 1) * 768]) for h in range(2)
    ]
    return fetched(layer, [(out_ref, held)], held, sems, where_ref, halves)


QKV_HELD = [pltpu.VMEM((1536, 1280), BF), pltpu.SemaphoreType.DMA((3,))]
OUT_HELD = [pltpu.VMEM((768, 1536), BF), pltpu.SemaphoreType.DMA((2,))]


def normed(value, gain):
    inverse = lax.rsqrt(jnp.mean(value * value, axis=-1, keepdims=True) + EPSILON)
    return inverse, value * inverse * gain


def qkv_kernel(layer, where_ref, hidden_ref, gain_ref, q_ref, k_ref, v_ref, sent_ref, act_ref, out_ref, held, sems):
    wait = fetch_qkv(layer, where_ref, q_ref, k_ref, v_ref, sent_ref, held, sems)
    act = normed(hidden_ref[...], gain_ref[...])[1].astype(BF)
    act_ref[...] = act
    wait()
    out_ref[...] = nn(act, held[...]).astype(BF)


def qkv_of(layer, where, hidden, gain, weights, sent):
    return pl.pallas_call(
        functools.partial(qkv_kernel, layer),
        in_specs=[SMEM, VMEM, VMEM] + [ANY] * 4,
        out_specs=[VMEM, VMEM],
        out_shape=[shaped(64, D), shaped(64, 1280)],
        scratch_shapes=QKV_HELD,
        compiler_params=params(40),
        cost_estimate=cost(64 * 1536 * 1280 * 2, 4 << 20),
        name="qkv_of",
    )(where, hidden, gain, *weights, sent)


def out_kernel(layer, where_ref, mixed_ref, out_w_ref, sent_ref, out_ref, held, sems):
    fetch_out(layer, where_ref, out_w_ref, sent_ref, held, sems)()
    out_ref[...] = nn(mixed_ref[...], held[...]).astype(BF)


def out_of(layer, where, mixed, weight, sent):
    return pl.pallas_call(
        functools.partial(out_kernel, layer),
        in_specs=[SMEM, VMEM] + [ANY] * 2,
        out_specs=VMEM,
        out_shape=shaped(64, D),
        scratch_shapes=OUT_HELD,
        compiler_params=params(40),
        cost_estimate=cost(64 * 1536 * 768 * 2, 3 << 20),
        name="out_of",
    )(where, mixed, weight, sent)


def act_back_kernel(layer, where_ref, grad_ref, q_ref, k_ref, v_ref, sent_ref, out_ref, held, sems):
    fetch_qkv(layer, where_ref, q_ref, k_ref, v_ref, sent_ref, held, sems)()
    out_ref[...] = nt(grad_ref[...], held[...]).astype(BF)


def act_back(layer, where, grad, weights, sent, *earlier):
    return pl.pallas_call(
        ignoring(len(earlier), functools.partial(act_back_kernel, layer)),
        in_specs=[ANY] * len(earlier) + [SMEM, VMEM] + [ANY] * 4,
        out_specs=VMEM,
        out_shape=shaped(64, D),
        scratch_shapes=QKV_HELD,
        compiler_params=params(40),
        cost_estimate=cost(64 * 1536 * 1280 * 2, 4 << 20),
        name="act_back",
    )(*earlier, where, grad, *weights, sent)


def middle_back_kernel(
    layer, where_ref, low_ref, got_ref, grad_ref, branch_ref, middle_ref, gain_ref, router_ref, routed_ref, out_w_ref, sent_ref,
    grad_middle_ref, right_ref, mixed_ref, gain_grad_ref, held, sems,
):
    wait = fetch_out(layer, where_ref, out_w_ref, sent_ref, held, sems)
    grad, middle, gain = grad_ref[...], middle_ref[...], gain_ref[...]
    inverse, second = normed(middle, gain)
    routed = routed_ref[...] > 0
    logits = jnp.where(routed, nt(second.astype(BF), router_ref[...]), NEGATIVE)
    raised = jnp.exp(logits - jnp.max(logits, axis=1, keepdims=True))
    raised = jnp.where(routed, raised, 0.0)
    gates = raised / jnp.sum(raised, axis=1, keepdims=True)
    inner = jnp.sum(grad * branch_ref[...], axis=1, keepdims=True)
    own = inner * gates
    high = own.astype(BF)
    low = (own - high.astype(F32)).astype(BF)
    total = low_ref[...].astype(F32) + got_ref[...].astype(F32)
    total = total - nn(high, router_ref[...]) - nn(low, router_ref[...])
    scaled = total * gain
    mean = jnp.mean(scaled * middle, axis=-1, keepdims=True)
    gain_grad_ref[...] = jnp.sum(total * middle * inverse, axis=0, keepdims=True)
    grad_middle = grad + inverse * scaled - inverse * inverse * inverse * middle * mean
    grad_middle_ref[...] = grad_middle
    grad_branch = grad_middle.astype(BF)
    right_ref[:, 0:1536] = grad_branch
    inner_high = inner.astype(BF).astype(F32)
    lane = lax.broadcasted_iota(jnp.int32, (64, 128), 1)
    lanes = jnp.where(lane == 0, inner_high, jnp.where(lane == 1, inner - inner_high, 0.0))
    right_ref[:, 1536:1664] = lanes.astype(BF)
    wait()
    mixed_ref[...] = nt(grad_branch, held[...]).astype(BF)


def middle_back(layer, where, low, got, grad, branch, middle, gain, router, routed, weight, sent):
    return pl.pallas_call(
        functools.partial(middle_back_kernel, layer),
        in_specs=[SMEM] + [VMEM] * 8 + [ANY] * 2,
        out_specs=[VMEM] * 4,
        out_shape=[shaped(64, D, dtype=F32), shaped(64, 1664), shaped(64, 768), shaped(1, D, dtype=F32)],
        scratch_shapes=OUT_HELD,
        compiler_params=params(40),
        cost_estimate=cost(64 * 1536 * 768 * 2, 5 << 20),
        name="middle_back",
    )(where, low, got, grad, branch, middle, gain, router, routed, weight, sent)


def whole(*shape):
    return pl.BlockSpec(shape, lambda j: (0,) * len(shape))


def expert_kernel(where_ref, weight_ref, router_ref, *refs):
    token_refs, routed_refs, (pa_ref, pb_ref, pre_ref, mid_ref, gates_ref, all_ref) = refs[:8], refs[8:16], refs[16:]
    for h, out_ref in enumerate((pa_ref, pb_ref)):
        rows = pl.ds(h * 256, 256)
        tokens = stacked(token_refs[4 * h : 4 * h + 4])
        all_ref[rows] = tokens
        parts = [tokens[:, r * 384 : (r + 1) * 384] for r in range(4)]
        routed = stacked(routed_refs[4 * h : 4 * h + 4])[:, 0:16].astype(F32) > 0
        logits = jnp.where(routed, nt(tokens, router_ref[...]), NEGATIVE)
        raised = jnp.exp(logits - jnp.max(logits, axis=1, keepdims=True))
        raised = jnp.where(routed, raised, 0.0)
        gates = raised / jnp.sum(raised, axis=1, keepdims=True)
        expert = lax.broadcasted_iota(jnp.int32, (256, 16), 1) - 2 * where_ref[3]
        gates = jnp.where((expert == 0) | (expert == 1), gates, 0.0)
        gates_ref[rows] = gates
        mids = []
        for e in range(2):
            gate_pre = sum(nn(parts[r], weight_ref[r, e]) for r in range(4))
            up_pre = sum(nn(parts[r], weight_ref[r, 2 + e]) for r in range(4))
            pre_ref[rows, e * 256 : (e + 1) * 256] = gate_pre.astype(BF)
            pre_ref[rows, (2 + e) * 256 : (3 + e) * 256] = up_pre.astype(BF)
            gate = jnp.sum(jnp.where(expert == e, gates, 0.0), axis=1, keepdims=True)
            mid = (gate_pre * jax.nn.sigmoid(gate_pre) * up_pre * gate).astype(BF)
            mid_ref[rows, e * 256 : (e + 1) * 256] = mid
            mids.append(mid)
        for r in range(4):
            made = nt(mids[0], weight_ref[r, 4]) + nt(mids[1], weight_ref[r, 5])
            out_ref[:, r * 384 : (r + 1) * 384] = made.astype(BF)


def experts_forward(where, tokens, given, router, weights, *earlier):
    routed = pl.BlockSpec((64, 128), lambda j: (0, 12))
    return pl.pallas_call(
        ignoring(len(earlier), expert_kernel),
        grid=(1,),
        in_specs=[ANY] * len(earlier)
        + [SMEM, whole(4, 6, 384, 256), whole(16, D)] + [whole(64, D)] * 8 + [routed] * 8,
        out_specs=[whole(256, D)] * 2 + [whole(512, 1024), whole(512, 512), whole(512, 16), whole(512, D)],
        out_shape=[shaped(256, D), shaped(256, D), shaped(512, 1024), shaped(512, 512)]
        + [shaped(512, 16, dtype=F32), shaped(512, D)],
        compiler_params=params(48),
        cost_estimate=cost(512 * 1536 * 1536 * 2, 10 << 20, 512 * 512),
        name="experts_forward",
    )(*earlier, where, weights, router, *tokens, *given)


def expert_back_kernel(order_ref, weight_ref, router_ref, pre_ref, gates_ref, *refs):
    grad_refs, (all_ref, pa_ref, pb_ref, gpre_ref, gated_ref) = refs[:8], refs[8:]
    for h, out_ref in enumerate((pa_ref, pb_ref)):
        rows = pl.ds(h * 256, 256)
        grad_out = stacked(grad_refs[4 * h : 4 * h + 4])
        all_ref[rows] = grad_out
        parts = [grad_out[:, r * 384 : (r + 1) * 384] for r in range(4)]
        gates = gates_ref[rows]
        expert = lax.broadcasted_iota(jnp.int32, (256, 16), 1) - 2 * order_ref[3]
        gated = jnp.zeros((256, 16), F32)
        grads = []
        for e in range(2):
            raw = sum(nn(parts[r], weight_ref[r, 4 + e]) for r in range(4))
            gate_pre = pre_ref[rows, e * 256 : (e + 1) * 256].astype(F32)
            up_pre = pre_ref[rows, (2 + e) * 256 : (3 + e) * 256].astype(F32)
            sigmoid = jax.nn.sigmoid(gate_pre)
            activated = gate_pre * sigmoid
            grad_gates = jnp.sum(activated * up_pre * raw, axis=1, keepdims=True)
            gated = jnp.where(expert == e, gates * grad_gates, gated)
            raw = raw * jnp.sum(jnp.where(expert == e, gates, 0.0), axis=1, keepdims=True)
            grad_gate = (raw * up_pre * sigmoid * (1.0 + gate_pre * (1.0 - sigmoid))).astype(BF)
            grad_up = (raw * activated).astype(BF)
            gpre_ref[rows, e * 256 : (e + 1) * 256] = grad_gate
            gpre_ref[rows, (2 + e) * 256 : (3 + e) * 256] = grad_up
            grads.append((grad_gate, grad_up))
        gated_ref[rows] = gated
        high = gated.astype(BF)
        low = (gated - high.astype(F32)).astype(BF)
        for r in range(4):
            router = router_ref[:, r * 384 : (r + 1) * 384]
            made = nn(high, router) + nn(low, router)
            for e in range(2):
                made = made + nt(grads[e][0], weight_ref[r, e]) + nt(grads[e][1], weight_ref[r, 2 + e])
            out_ref[:, r * 384 : (r + 1) * 384] = made.astype(BF)


def experts_backward(where, grads, pre, gates, router, weights, *earlier):
    return pl.pallas_call(
        ignoring(len(earlier), expert_back_kernel),
        grid=(1,),
        in_specs=[ANY] * len(earlier)
        + [SMEM, whole(4, 6, 384, 256), whole(16, D), whole(512, 1024), whole(512, 16)]
        + [whole(64, D)] * 8,
        out_specs=[whole(512, D), whole(256, D), whole(256, D), whole(512, 1024), whole(512, 16)],
        out_shape=[shaped(512, D), shaped(256, D), shaped(256, D), shaped(512, 1024), shaped(512, 16, dtype=F32)],
        compiler_params=params(48),
        cost_estimate=cost(512 * 1536 * 1536 * 2, 10 << 20, 512 * 512),
        name="experts_backward",
    )(*earlier, where, weights, router, pre, gates, *grads)


def last_expert_kernel(where_ref, weight_ref, router_ref, *refs):
    token_refs, given_refs = refs[:8], refs[8:16]
    pa_ref, pb_ref, mid_ref, gpre_ref, gates_ref, gated_ref, tokens_ref, all_ref = refs[16:]
    for h, out_ref in enumerate((pa_ref, pb_ref)):
        rows = pl.ds(h * 256, 256)
        tokens = stacked(token_refs[4 * h : 4 * h + 4])
        tokens_ref[rows] = tokens
        given = stacked(given_refs[4 * h : 4 * h + 4])
        grad_out = given[:, 0:1536]
        all_ref[rows] = grad_out
        parts = [tokens[:, r * 384 : (r + 1) * 384] for r in range(4)]
        grad_parts = [grad_out[:, r * 384 : (r + 1) * 384] for r in range(4)]
        routed = given[:, 1536:1552].astype(F32) > 0
        logits = jnp.where(routed, nt(tokens, router_ref[...]), NEGATIVE)
        raised = jnp.exp(logits - jnp.max(logits, axis=1, keepdims=True))
        raised = jnp.where(routed, raised, 0.0)
        gates = raised / jnp.sum(raised, axis=1, keepdims=True)
        expert = lax.broadcasted_iota(jnp.int32, (256, 16), 1) - 2 * where_ref[3]
        gates = jnp.where((expert == 0) | (expert == 1), gates, 0.0)
        gates_ref[rows] = gates
        gated = jnp.zeros((256, 16), F32)
        mids, grads = [], []
        for e in range(2):
            gate_pre = sum(nn(parts[r], weight_ref[r, e]) for r in range(4))
            up_pre = sum(nn(parts[r], weight_ref[r, 2 + e]) for r in range(4))
            raw = sum(nn(grad_parts[r], weight_ref[r, 4 + e]) for r in range(4))
            gate = jnp.sum(jnp.where(expert == e, gates, 0.0), axis=1, keepdims=True)
            sigmoid = jax.nn.sigmoid(gate_pre)
            activated = gate_pre * sigmoid
            product = activated * up_pre
            mid = (product * gate).astype(BF)
            mid_ref[rows, e * 256 : (e + 1) * 256] = mid
            mids.append(mid)
            gated = jnp.where(expert == e, gates * jnp.sum(product * raw, axis=1, keepdims=True), gated)
            raw = raw * gate
            grad_gate = (raw * up_pre * sigmoid * (1.0 + gate_pre * (1.0 - sigmoid))).astype(BF)
            grad_up = (raw * activated).astype(BF)
            gpre_ref[rows, e * 256 : (e + 1) * 256] = grad_gate
            gpre_ref[rows, (2 + e) * 256 : (3 + e) * 256] = grad_up
            grads.append((grad_gate, grad_up))
        gated_ref[rows] = gated
        high = gated.astype(BF)
        low = (gated - high.astype(F32)).astype(BF)
        for r in range(4):
            lanes = slice(r * 384, (r + 1) * 384)
            made = (nt(mids[0], weight_ref[r, 4]) + nt(mids[1], weight_ref[r, 5])).astype(BF)
            back = nn(high, router_ref[:, lanes]) + nn(low, router_ref[:, lanes])
            for e in range(2):
                back = back + nt(grads[e][0], weight_ref[r, e]) + nt(grads[e][1], weight_ref[r, 2 + e])
            back = back.astype(BF)
            for j in range(4):
                out_ref[j * 128 : j * 128 + 64, lanes] = made[j * 64 : (j + 1) * 64]
                out_ref[j * 128 + 64 : (j + 1) * 128, lanes] = back[j * 64 : (j + 1) * 64]


def last_experts(where, tokens, given, router, weights, *earlier):
    return pl.pallas_call(
        ignoring(len(earlier), last_expert_kernel),
        grid=(1,),
        in_specs=[ANY] * len(earlier)
        + [SMEM, whole(4, 6, 384, 256), whole(16, D)] + [whole(64, D)] * 8 + [whole(64, 1664)] * 8,
        out_specs=[whole(512, D)] * 2
        + [whole(512, 512), whole(512, 1024), whole(512, 16), whole(512, 16), whole(512, D), whole(512, D)],
        out_shape=[shaped(512, D), shaped(512, D), shaped(512, 512), shaped(512, 1024)]
        + [shaped(512, 16, dtype=F32), shaped(512, 16, dtype=F32), shaped(512, D), shaped(512, D)],
        compiler_params=params(48),
        cost_estimate=cost(512 * 1536 * 1536 * 4, 16 << 20, 512 * 512),
        name="last_experts",
    )(*earlier, where, weights, router, *tokens, *given)


def expert_weight_kernel(gpre_ref, mid_ref, tokens_ref, grads_ref, out_ref):
    for n in range(6):
        left_ref, right_ref = (tokens_ref, gpre_ref) if n < 4 else (grads_ref, mid_ref)
        out_ref[0, n] = tn(left_ref[...], right_ref[:, (n % 4) * 256 : (n % 4 + 1) * 256]).astype(BF)


def expert_weight_grads(tokens, grads, gpre, mid, *earlier):
    return pl.pallas_call(
        ignoring(len(earlier), expert_weight_kernel),
        grid=(4,),
        in_specs=[ANY] * len(earlier) + [whole(512, 1024), whole(512, 512)] + [column(512, 384, 0)] * 2,
        out_specs=pl.BlockSpec((1, 6, 384, 256), lambda r: (r, 0, 0, 0)),
        out_shape=shaped(4, 6, 384, 256),
        compiler_params=params(40),
        cost_estimate=cost(512 * 1536 * 1536 * 2, 10 << 20),
        name="expert_weight_grads",
    )(*earlier, gpre, mid, tokens, grads)


def chosen(size, width, me):
    row = lax.broadcasted_iota(jnp.int32, (size, width), 0)
    lane = lax.broadcasted_iota(jnp.int32, (size, width), 1)
    return (row == lane + me * width).astype(BF)


def source(where_ref, b):
    return ((where_ref[1] - (b & 3)) & 3) * 2 + (where_ref[2] if b < 4 else 1 - where_ref[2])


def dense_slice_kernel(pieces, where_ref, left_ref, gated_ref, gates_ref, gains_ref, tokens_ref, right_ref, *refs):
    me = where_ref[3]
    out_ref = refs[8 if pieces else 0]
    if pieces:
        right = refs[9]
        for b in range(8):
            right[pl.ds(pl.multiple_of(source(where_ref, b) * 64, 64), 64), :] = refs[b][...]
        right = right[...]
    else:
        right = right_ref[:, 1664:2944]
    left = nn(left_ref[:, 0:1536], chosen(1536, 192, me)).astype(BF)
    rows = tn(left, right).astype(BF)
    left = nn(left_ref[:, 1536:2304], chosen(768, 96, me)).astype(BF)
    lane = lax.broadcasted_iota(jnp.int32, (64, 16), 1)
    logits = []
    for b in range(8):
        block = slice(b * 64, (b + 1) * 64)
        start = pl.multiple_of(source(where_ref, b) * 64, 64)
        lanes = right_ref[pl.ds(start, 64), 1536:1664].astype(F32)
        inner = lanes[:, 0:1] + lanes[:, 1:2]
        grad = gated_ref[block] - 0.5 * gates_ref[block] * inner
        one = [jnp.sum(jnp.where(lane == 2 * me + e, grad, 0.0), axis=1, keepdims=True) for e in range(2)]
        logits.append(jnp.where(lane == 0, one[0], jnp.where(lane == 1, one[1], 0.0)).astype(BF))
    extra = tn(jnp.concatenate(logits, axis=0), tokens_ref[...])
    row = lax.broadcasted_iota(jnp.int32, (16, D), 0)
    extra = jnp.where(row == 2, gains_ref[0:1], jnp.where(row == 3, gains_ref[1:2], extra))
    wide = jnp.concatenate([tn(left, right_ref[:, 0:1536]), extra], axis=0).astype(BF)
    for r in range(4):
        to = (where_ref[0] - r) & 3 if pieces else r
        for c in range(10):
            out_ref[to, c * 48 : (c + 1) * 48] = rows[r * 48 : (r + 1) * 48, c * 128 : (c + 1) * 128]
        for c in range(3):
            lanes = slice(r * 384 + c * 128, r * 384 + (c + 1) * 128)
            out_ref[to, 480 + c * 112 : 480 + (c + 1) * 112] = wide[:, lanes]


def dense_slice(layer, where, left, gated, gates, gains, tokens, right, pieces, *earlier):
    return pl.pallas_call(
        ignoring(len(earlier), functools.partial(dense_slice_kernel, len(pieces) > 0)),
        grid=(1,),
        in_specs=[ANY] * len(earlier)
        + [SMEM, pl.BlockSpec((512, 2304), lambda j: (0, layer)), whole(512, 16), whole(512, 16), whole(2, D)]
        + [whole(512, D), whole(*right.shape)]
        + [whole(64, 1280)] * len(pieces),
        out_specs=whole(4, 816, 128),
        out_shape=shaped(4, 816, 128),
        scratch_shapes=[pltpu.VMEM((512, 1280), BF)] if pieces else [],
        compiler_params=params(40),
        cost_estimate=cost(512 * 1536 * 1024 * 2, 8 << 20),
        name="dense_slice",
    )(*earlier, where, left, gated, gates, gains, tokens, right, *pieces)


def dense_rows_kernel(in_ref, q_ref, k_ref, v_ref, out_ref, router_ref, gains_ref, held_ref):
    j = pl.program_id(0)
    for x in range(4):
        rows = slice(x * 48, (x + 1) * 48)
        for c in range(10):
            to_ref, lane = (q_ref, c) if c < 6 else (k_ref, c - 6) if c < 8 else (v_ref, c - 8)
            to_ref[rows, lane * 128 : (lane + 1) * 128] = in_ref[x, 0, c * 48 : (c + 1) * 48].astype(F32)
        for c in range(3):
            lanes = slice(x * 384 + c * 128, x * 384 + (c + 1) * 128)
            out_ref[:, lanes] = in_ref[x, 0, 480 + c * 112 : 576 + c * 112].astype(F32)
            held_ref[j, :, lanes] = in_ref[x, 0, 576 + c * 112 : 592 + c * 112].astype(F32)

    @pl.when(j == 7)
    def _():
        held = held_ref[...]
        router = jnp.concatenate([held[i, 0:2] for i in range(8)], axis=0)
        router_ref[...] = router.T
        gains_ref[...] = jnp.sum(held, axis=0)


def dense_rows(everything):
    rows = lambda count, width: pl.BlockSpec((count, width), lambda j: (j, 0))
    return pl.pallas_call(
        dense_rows_kernel,
        grid=(8,),
        in_specs=[pl.BlockSpec((4, 1, 816, 128), lambda j: (0, j, 0, 0))],
        out_specs=[rows(192, 768), rows(192, 256), rows(192, 256), rows(96, D), whole(D, 16), whole(16, D)],
        out_shape=[shaped(D, 768, dtype=F32), shaped(D, 256, dtype=F32), shaped(D, 256, dtype=F32)]
        + [shaped(768, D, dtype=F32), shaped(D, 16, dtype=F32), shaped(16, D, dtype=F32)],
        scratch_shapes=[pltpu.VMEM((8, 16, D), F32)],
        compiler_params=params(40),
        cost_estimate=cost(0, 20 << 20),
        name="dense_rows",
    )(everything)


def gates_of(tokens, router, routed):
    logits = dot(tokens, router)
    top = jnp.max(jnp.where(routed > 0, logits, NEGATIVE), axis=1, keepdims=True)
    raised = jnp.where(routed > 0, jnp.exp(jnp.minimum(logits - top, 0.0)), 0.0)
    return raised / jnp.sum(raised, axis=1, keepdims=True)


X_GROUPS = [[(x * NY + y) * 2 + c for x in range(NX)] for y in range(NY) for c in range(2)]


Y_GROUPS = [[(x * NY + y) * 2 + c for y in range(NY) for c in range(2)] for x in range(NX)]


def replica_gather(shard):
    return lax.all_gather(shard, "dp", axis=0, axis_index_groups=X_GROUPS)


def replica_scatter(grads):
    flat = grads.reshape(-1, grads.shape[-1])
    return lax.psum_scatter(flat, "dp", scatter_dimension=0, axis_index_groups=X_GROUPS, tiled=True)


def after(value, *others):
    return lax.optimization_barrier((value, *others))[0]


def group_pieces(block):
    near = [block] + [moved(block, 0, j, 0) for j in (1, 2, 3)]
    return near + [moved(piece, 0, 0, 1) for piece in near]


def ordered(value):
    probe = value[(-1,) * value.ndim]
    return probe == probe


def behind(value, *earlier):
    known = ordered(earlier[0])
    for other in earlier[1:]:
        known = known & ordered(other)
    return jnp.where(known, value, jnp.zeros_like(value))


def per_device(
    inputs,
    cotangent,
    segments,
    routes,
    norm_first,
    w_query,
    w_key,
    w_value,
    w_out,
    norm_second,
    w_router,
    w_gate,
    w_up,
    w_down,
):
    section = lax.axis_index("section")
    place = lax.axis_index("dp")
    here_x, here_y, here_c = place // (NY * 2), place // 2 % NY, place % 2
    me = place % 8
    first = section == 0
    rows = inputs.shape[1]

    def in_order(own, other):
        return jnp.where(first, own, other), jnp.where(first, other, own)

    def pick(pair):
        return lax.dynamic_index_in_dim(pair, section, 0, False)

    weights_in = (w_query[0], w_key[0], w_value[0])
    dense = jnp.concatenate(
        [lax.dynamic_slice_in_dim(w, place * 48, 48, 0) for w in weights_in]
        + [lax.dynamic_slice(w_out[0], (place % 16 * 48, place // 16 * 768), (48, 768))],
        axis=1,
    )
    dense = swapped(dense, "section")

    act_both = norm_apply(inputs.astype(F32), norm_first[0]).astype(BF).reshape(2 * rows, D)
    qkv_both = jnp.concatenate([dot(act_both, w).astype(BF) for w in weights_in], axis=1)
    qkv_sent = lax.ppermute(qkv_both[rows:], "section", [(0, 1)])
    qkv_first = jnp.where(first, qkv_both[:rows], qkv_sent)
    dense_all = lax.all_gather(behind(dense, qkv_both), "dp", axis=0).reshape(D, 2048)

    pack = jnp.concatenate([norm_first, norm_second, w_router[0].T.astype(F32)], axis=0)
    packs = in_order(pack, swapped(pack, "section"))
    routers = [p[2:].astype(BF) for p in packs]
    turned_down = jnp.swapaxes(w_down[0], 1, 2)
    sent_gate = swapped(w_gate[0], "section")
    sent_rest = swapped(side_by_side([w_up[0], turned_down], 0, qkv_sent), "section")
    halves = (w_gate[0], w_up[0], turned_down, sent_gate, sent_rest)
    expert_weights = [None, None]
    where = jnp.stack([here_x, here_y, here_c, me, section]).astype(jnp.int32)

    labels = pick(segments)
    query_labels = lax.dynamic_slice_in_dim(labels, place * rows, rows, 0)
    starts = jnp.sum((labels[None, :] < query_labels[:, None]).astype(jnp.int32), axis=1)
    masks = (where, jnp.concatenate([starts, starts])[None])

    own_routes = pick(routes)
    expert_ids = jnp.arange(EXPERTS, dtype=jnp.int32)
    routed_own = jnp.sum((own_routes[:, :, None] == expert_ids).astype(F32), axis=1)
    given = pick(cotangent)
    sent = jnp.concatenate([given, jnp.pad(routed_own.astype(BF), ((0, 0), (0, 128 - EXPERTS)))], axis=1)
    given_all = group_pieces(sent)

    hidden = pick(inputs).astype(F32)
    saved = []
    for layer in range(2):
        gain_one, gain_two = packs[layer][0:1], packs[layer][1:2]
        if layer == 0:
            activation, qkv = norm_apply(hidden, gain_one).astype(BF), qkv_first
        else:
            activation, qkv = qkv_of(1, where, hidden, gain_one, weights_in, dense_all)
        query, pair = qkv[:, :768], qkv[:, 768:]
        around = [moved(pair, j, 0, 0) for j in (1, 2, 3)]
        slab = jnp.concatenate([pair] + around, axis=0)
        near = [slab] + [moved(slab, 0, j, 0) for j in (1, 2, 3)]
        pieces = near + [moved(piece, 0, 0, 1) for piece in near]
        mixed, log_total = attend_forward(masks, query, pieces)
        if layer == 0:
            mixed_sent = lax.ppermute(mixed, "section", [(1, 0)])
            partial = dot(jnp.concatenate([mixed, mixed_sent], axis=0), w_out[0]).astype(BF)
            both_axes = ("section", "tensor")
            straight = lax.ppermute(partial[rows:], both_axes, [(0, 2), (1, 3)])
            across = lax.ppermute(partial[rows:], both_axes, [(0, 3), (1, 2)])
            turned = lax.ppermute(partial[:rows], both_axes, [(0, 1), (1, 0)])
            experts_first = choose(0, section[None].astype(jnp.int32), halves, dense_all, mixed)
            expert_weights[0] = replica_gather(experts_first)
            middle = hidden + (
                jnp.where(first, partial[:rows], straight).astype(F32) + jnp.where(first, turned, across).astype(F32)
            )
        else:
            partial = out_of(1, where, mixed, w_out[0], dense_all)
            middle = hidden + (partial.astype(F32) + swapped(partial, "tensor").astype(F32))
        second = norm_apply(middle, gain_two).astype(BF)
        tokens = group_pieces(second)
        if layer == 0:
            experts_second = choose(1, section[None].astype(jnp.int32), halves, second)
            expert_weights[1] = replica_gather(experts_second)
        cut = (activation, mixed)
        if layer == 0:
            made_near, made_far, pre, mid, gates, tokens = experts_forward(
                where, tokens, given_all, routers[0], expert_weights[0], experts_second
            )
            made = group_sum(made_near, made_far).reshape(rows, D).astype(BF)
            branch = tensor_sum(made)
            rest = (mid, gates, pre)
        else:
            near, far, mid, grad_pre, gates, gated, tokens, grad_all = last_experts(
                where, tokens, given_all, routers[1], expert_weights[1]
            )
            both = (near.astype(F32) + moved(far, 0, 0, 1).astype(F32)).astype(BF)
            low = back_y(both).reshape(2 * rows, D).astype(BF)
            lefts = side_by_side([*saved[0][8], *cut], 1, low)
            weight_grads = expert_weight_grads(tokens, grad_all, grad_pre, mid, lefts)
            lefts = lax.all_gather(lefts, "dp", axis=0, axis_index_groups=Y_GROUPS).reshape(8 * rows, 4608)
            got = behind(swapped(low, "tensor"), weight_grads)
            branch = low[:rows].astype(F32) + got[:rows].astype(F32)
            low, got = low[rows:], got[rows:]
            rest = (mid, gates, gated)
        result = middle + branch
        saved.append((hidden, query, pieces, log_total, middle, second, tokens, branch, cut, result, rest))
        hidden = result

    def own_of(a, b):
        return jnp.where(first, a, b)

    def from_other(for_first, for_second):
        return swapped(own_of(for_second, for_first).astype(BF), "section").astype(F32)

    def over_sections(a, b):
        return own_of(a, b).astype(F32) + from_other(a, b)

    grad_output = given.astype(F32)
    grads = []
    for layer in (1, 0):
        hidden, query, pieces, log_total, middle, second, tokens, branch, _, _, rest = saved[layer]
        gain_one, gain_two = packs[layer][0:1], packs[layer][1:2]
        router = routers[layer]
        mid, gates, rest = rest
        if layer == 1:
            gated = rest
        else:
            grad_all, back_near, back_far, grad_pre, gated = experts_backward(
                where, group_pieces(grad_output.astype(BF)), rest, gates, router, expert_weights[0], *earlier
            )
            both = (back_near.astype(F32) + moved(back_far, 0, 0, 1).astype(F32)).astype(BF)
            weight_grads = expert_weight_grads(tokens, grad_all, grad_pre, mid, both)
            low = behind(back_y(both), weight_grads).reshape(rows, D).astype(BF)
            got = swapped(low, "tensor")
        expert_part = replica_scatter(weight_grads)
        grad_middle, right, grad_mixed, gain_two_grad = middle_back(
            layer, where, low, got, grad_output, branch, middle, gain_two, router, routed_own, w_out[0], dense_all
        )
        grad_query, back_near, back_far = attend_backward(masks, query, grad_mixed, log_total, pieces)
        both = (back_near.astype(F32) + moved(back_far, 0, 0, 1).astype(F32)).astype(BF)
        half = back_y(both)
        if layer == 0:
            late = dense_slice(1, *grads[0][1], [], both)
            half = behind(half, late)
        grad_pair = back_x(half.astype(BF)).reshape(rows, 512).astype(BF)
        grad_qkv = jnp.concatenate([grad_query, grad_pair], axis=1)
        partial = act_back(layer, where, grad_qkv, weights_in, dense_all, lefts if layer == 1 else expert_part)
        grad_activation = partial.astype(F32) + swapped(partial, "tensor").astype(F32)
        grad_from_first, gain_one_grad = norm_back(hidden, gain_one, grad_activation)
        grad_input = grad_middle + grad_from_first
        gains = jnp.concatenate([gain_two_grad, gain_one_grad[None]], axis=0)
        if layer == 1:
            right = jnp.concatenate([right, grad_qkv], axis=1)
            earlier = [right, expert_part]
            right = lax.all_gather(right, "dp", axis=0, axis_index_groups=Y_GROUPS).reshape(8 * rows, 2944)
            grads.append((grad_input, (where, lefts, gated, gates, gains, tokens, right), expert_part))
        else:
            late = replica_scatter(late)
            right = lax.all_gather(right, "dp", axis=0, axis_index_groups=Y_GROUPS).reshape(8 * rows, 1664)
            blocks = dense_slice(0, where, lefts, gated, gates, gains, tokens, right, group_pieces(grad_qkv))
            grads.append((grad_input, back_x(blocks.reshape(4 * 816, 128)).reshape(816, 128), expert_part))
        grad_output = grad_input
    grads = grads[::-1]

    def by_batch(own, other):
        return jnp.stack([jnp.where(first, own, other), jnp.where(first, other, own)])[None]

    results = by_batch(own_of(saved[0][9], saved[1][9]), from_other(saved[0][9], saved[1][9]))
    input_grads = by_batch(own_of(grads[0][0], grads[1][0]), from_other(grads[0][0], grads[1][0]))
    first_part, late = grads[0][1], late.astype(F32)

    def extras(block):
        return block.reshape(-1, 128)[480:].reshape(3, 112, 128)[:, 96:98].reshape(6, 128)

    straight = swapped(jnp.concatenate([extras(first_part), extras(late)], axis=0).astype(BF), "tensor").astype(F32)
    across = lax.ppermute(
        own_of(extras(late), extras(first_part)).astype(BF), ("section", "tensor"), [(0, 3), (1, 2), (2, 1), (3, 0)]
    ).astype(F32)
    block = over_sections(first_part, late)
    more = own_of(straight[:6], straight[6:]) + across
    wide = block[480:].reshape(3, 112, 128)
    wide = wide + jnp.pad(more.reshape(3, 2, 128), ((0, 0), (96, 14), (0, 0)))
    block = jnp.concatenate([block[:480], wide.reshape(336, 128)], axis=0).astype(BF)
    everything = lax.all_gather(block, "dp", axis=0).reshape(4, 8, 816, 128)
    query_sum, key_sum, value_sum, out_full, router_sum, gains = dense_rows(everything)
    expert_sum = over_sections(grads[0][2], grads[1][2]).reshape(3, 2, 384, 256)
    return (
        results,
        input_grads,
        gains[3:4],
        query_sum[None],
        key_sum[None],
        value_sum[None],
        out_full[None],
        gains[2:3],
        router_sum[None],
        expert_sum[0][None],
        expert_sum[1][None],
        jnp.swapaxes(expert_sum[2], 1, 2)[None],
    )


def solution(mesh):
    in_specs = (
        P(None, "dp", None),
        P(None, "dp", None),
        P(),
        P(None, "dp", None),
        P("section", None),
        P("section", None, "tensor"),
        P("section", None, "tensor"),
        P("section", None, "tensor"),
        P("section", "tensor", None),
        P("section", None),
        P("section", None, None),
        P("section", "dp", None, "tensor"),
        P("section", "dp", None, "tensor"),
        P("section", "dp", "tensor", None),
    )
    out_specs = (
        P("section", None, "dp", None),
        P("section", None, "dp", None),
        P("section", None),
        P("section", None, "tensor"),
        P("section", None, "tensor"),
        P("section", None, "tensor"),
        P("section", "tensor", None),
        P("section", None),
        P("section", None, None),
        P("section", "dp", None, "tensor"),
        P("section", "dp", None, "tensor"),
        P("section", "dp", "tensor", None),
    )
    return jax.shard_map(
        per_device, mesh=mesh, in_specs=in_specs, out_specs=out_specs, check_vma=False
    )
```

```python
import functools

import jax
import jax.numpy as jnp
from jax import lax
from jax.experimental import pallas as pl
from jax.experimental.pallas import tpu as pltpu
from jax.sharding import PartitionSpec as P

D = 1536
HD = 64
EXPERTS = 16
NX, NY = 4, 4
EPSILON = 1e-06
SCALE = 0.125
NEGATIVE = -1e30
BF = jnp.bfloat16
F32 = jnp.float32


def moved(value, dx, dy, dc):
    route = []
    for x in range(NX):
        for y in range(NY):
            for c in range(2):
                target = (((x + dx) % NX) * NY + (y + dy) % NY) * 2 + (c ^ dc)
                route.append(((x * NY + y) * 2 + c, target))
    return lax.ppermute(value, "dp", route)


def swapped(value, axis):
    return lax.ppermute(value, axis, [(0, 1), (1, 0)])


def along_y(block):
    return jnp.concatenate([block] + [moved(block, 0, j, 0) for j in (1, 2, 3)], axis=0)


def along_x(block):
    return jnp.concatenate([block] + [moved(block, j, 0, 0) for j in (1, 2, 3)], axis=0)


def back_y(sums):
    parts = sums.reshape(4, -1, sums.shape[-1])
    total = parts[0].astype(F32)
    for j in (1, 2, 3):
        total = total + moved(parts[j], 0, -j, 0).astype(F32)
    return total


def back_x(sums):
    parts = sums.reshape(4, -1, sums.shape[-1])
    total = parts[0].astype(F32)
    for j in (1, 2, 3):
        total = total + moved(parts[j], -j, 0, 0).astype(F32)
    return total


def group_gather(block):
    column = along_y(block)
    return column, moved(column, 0, 0, 1)


def group_sum(own, other):
    both = own.astype(F32) + moved(other, 0, 0, 1).astype(F32)
    return back_y(both.astype(BF))


def tensor_sum(value):
    low = value.astype(BF)
    return low.astype(F32) + swapped(low, "tensor").astype(F32)


def norm_apply(value, gain):
    inverse = lax.rsqrt(jnp.mean(value * value, axis=-1, keepdims=True) + EPSILON)
    return value * inverse * gain


def norm_back(value, gain, grad):
    inverse = lax.rsqrt(jnp.mean(value * value, axis=-1, keepdims=True) + EPSILON)
    scaled = grad * gain
    inner = jnp.mean(scaled * value, axis=-1, keepdims=True)
    gain_grad = jnp.sum(grad * value * inverse, axis=0)
    return (inverse * scaled - inverse * inverse * inverse * value * inner, gain_grad)


def dot(left, right):
    return jnp.dot(left, right, preferred_element_type=F32)


def over_rows(left, right):
    return lax.dot_general(left, right, (((0,), (0,)), ((), ())), preferred_element_type=F32)


def against(left, right):
    return lax.dot_general(left, right, (((1,), (1,)), ((), ())), preferred_element_type=F32)


def nn(a, b):
    return lax.dot_general(a, b, (((1,), (0,)), ((), ())), preferred_element_type=F32)


def nt(a, b):
    return lax.dot_general(a, b, (((1,), (1,)), ((), ())), preferred_element_type=F32)


def tn(a, b):
    return lax.dot_general(a, b, (((0,), (0,)), ((), ())), preferred_element_type=F32)


SMEM = pl.BlockSpec(memory_space=pltpu.SMEM)
VMEM = pl.BlockSpec(memory_space=pltpu.VMEM)
ANY = pl.BlockSpec(memory_space=pl.ANY)
HBM = pl.BlockSpec(memory_space=pltpu.HBM)


def shaped(*shape, dtype=BF):
    return jax.ShapeDtypeStruct(shape, dtype)


def params(mib=58):
    return pltpu.CompilerParams(vmem_limit_bytes=mib << 20)


def cost(flops, bytes_accessed, exps=0):
    return pl.CostEstimate(flops=flops, bytes_accessed=bytes_accessed, transcendentals=exps)


def stacked(refs):
    return jnp.concatenate([ref[...] for ref in refs], axis=0)


def spread(block):
    lane = lax.broadcasted_iota(jnp.int32, (64, 128), 1)
    parts = []
    for k in range(6):
        wide = block[:, (k // 2) * 128 : (k // 2 + 1) * 128].astype(F32)
        half = k // 3
        if k % 2 != half:
            wide = pltpu.roll(wide, 64, 1)
        parts.append(jnp.where((lane >= 64) == (half == 1), wide, 0.0))
    return jnp.concatenate(parts, axis=0)


def gathered(turned):
    rows = turned.T
    lane = lax.broadcasted_iota(jnp.int32, (64, 128), 1)
    outs = []
    for b in range(3):
        two = []
        for k in (2 * b, 2 * b + 1):
            part = rows[k * 64 : (k + 1) * 64]
            if k % 2 != k // 3:
                part = pltpu.roll(part, 64, 1)
            two.append(part)
        outs.append(jnp.where(lane < 64, two[0], two[1]))
    return jnp.concatenate(outs, axis=1)


def bias_of(place_ref, h, start_ref):
    row = lax.broadcasted_iota(jnp.int32, (1024, 128), 0)
    token = lax.broadcasted_iota(jnp.int32, (1024, 128), 1) & 63
    x = (place_ref[0] - (row >> 6)) & 3
    y = (place_ref[1] - (row >> 8)) & 3
    c = place_ref[2] if h == 0 else 1 - place_ref[2]
    key = ((x * 4 + y) * 2 + c) * 64 + (row & 63)
    query = ((place_ref[0] * 4 + place_ref[1]) * 2 + place_ref[2]) * 64 + token
    bias = jnp.where((key <= query) & (key >= start_ref[...]), 0.0, NEGATIVE)
    return jnp.concatenate([bias, bias, bias], axis=1)


def attend_kernel(layer, place_ref, st_ref, q_ref, *refs):
    j = pl.program_id(0)
    keys = [stacked(refs[0:4]), stacked(refs[4:8])]
    values = [stacked(refs[8:12]), stacked(refs[12:16])]
    if layer == 1:
        earlier_refs, act_ref, out_w_ref, sent_ref = refs[16:18], refs[18], refs[19], refs[20]
        out_ref, lse_ref, near_ref, far_ref, partial_ref, lefts_ref, held, sems = refs[21:]
        start, wait = fetch_out(layer, place_ref, out_w_ref, sent_ref, held, sems)
        pl.when(j == 0)(start)
    else:
        out_ref, lse_ref, near_ref, far_ref = refs[16:]
    for k, v, to_ref in zip(keys, values, (near_ref, far_ref)):
        to_ref[:, pl.ds(pl.multiple_of(j * 128, 128), 128)] = k
        to_ref[:, pl.ds(pl.multiple_of(256 + j * 128, 128), 128)] = v
    query = (spread(q_ref[...]) * 0.125).astype(BF)
    scores = [nt(k, query) + bias_of(place_ref, h, st_ref) for h, k in enumerate(keys)]
    top = jnp.maximum(*[jnp.max(s, axis=0, keepdims=True) for s in scores])
    total = jnp.zeros_like(top)
    mixed = jnp.zeros((128, 384), F32)
    for s, v in zip(scores, values):
        raised = jnp.exp(s - top)
        total = total + jnp.sum(raised, axis=0, keepdims=True)
        mixed = mixed + tn(v, raised.astype(BF))
    out_ref[:, pl.ds(pl.multiple_of(j * 384, 128), 384)] = gathered(mixed / total).astype(BF)
    lse_ref[0] = top + jnp.log(total)
    if layer == 1:

        @pl.when(j == 1)
        def _():
            wait()
            partial_ref[...] = nn(out_ref[...], held[...]).astype(BF)
            lefts_ref[:, 0:1536], lefts_ref[:, 1536:2304] = earlier_refs[0][...], earlier_refs[1][...]
            lefts_ref[:, 2304:3840], lefts_ref[:, 3840:4608] = act_ref[...], out_ref[...]


def column(rows, width, base):
    return pl.BlockSpec((rows, width), lambda j: (0, j + base))


PAIRS = [SMEM, pl.BlockSpec((1, 128), lambda j: (0, 0))], [column(256, 128, 0)] * 8 + [column(256, 128, 2)] * 8
LSE = pl.BlockSpec((1, 1, 384), lambda j: (j, 0, 0))


def ignoring(count, kernel):
    return lambda *refs: kernel(*refs[count:])


def fixed(*shape):
    return pl.BlockSpec(shape, lambda j: (0,) * len(shape))


def attend_forward(layer, masks, query, pieces, factors=(), weights=()):
    last = layer == 1
    return pl.pallas_call(
        functools.partial(attend_kernel, layer),
        grid=(2,),
        in_specs=PAIRS[0] + [column(64, 384, 0)] + PAIRS[1] + [fixed(*f.shape) for f in factors] + [HBM] * len(weights),
        out_specs=[fixed(64, 768), LSE, fixed(1024, 512), fixed(1024, 512)] + [fixed(64, D), fixed(64, 4608)] * last,
        out_shape=[shaped(64, 768), shaped(2, 1, 384, dtype=F32), shaped(1024, 512), shaped(1024, 512)]
        + [shaped(64, D), shaped(64, 4608)] * last,
        scratch_shapes=OUT_HELD if last else [],
        compiler_params=params(),
        cost_estimate=cost(12 * 64 * 2048 * 64 * 4, 2 << 20, 12 * 64 * 2048),
        name="attend_forward",
    )(*masks, query, *pieces, *pieces, *factors, *weights)


def attend_back_kernel(place_ref, st_ref, q_ref, do_ref, lse_ref, *refs):
    j = pl.program_id(0)
    key_columns = pl.ds(pl.multiple_of(j * 128, 128), 128)
    value_columns = pl.ds(pl.multiple_of(256 + j * 128, 128), 128)
    keys, values = [ref[...] for ref in refs[0:2]], [ref[...] for ref in refs[2:4]]
    dq_ref, near_ref, far_ref = refs[4:]
    query = (spread(q_ref[...]) * 0.125).astype(BF)
    grad = spread(do_ref[...]).astype(BF)
    weights, raws = [], []
    inner = jnp.zeros((1, 384), F32)
    for h, (k, v) in enumerate(zip(keys, values)):
        s = nt(k, query) + bias_of(place_ref, h, st_ref)
        w = jnp.exp(s - lse_ref[0])
        raw = nt(v, grad)
        inner = inner + jnp.sum(w * raw, axis=0, keepdims=True)
        weights.append(w)
        raws.append(raw)
    turned = jnp.zeros((128, 384), F32)
    for w, raw, k, out_ref in zip(weights, raws, keys, (near_ref, far_ref)):
        ds = (w * (raw - inner)).astype(BF)
        out_ref[:, key_columns] = nn(ds, query).astype(BF)
        out_ref[:, value_columns] = nn(w.astype(BF), grad).astype(BF)
        turned = turned + tn(k, ds)
    dq_ref[...] = gathered(turned * 0.125).astype(BF)


def attend_backward(masks, query, grad, lse, near, far, *earlier):
    return pl.pallas_call(
        ignoring(len(earlier), attend_back_kernel),
        grid=(2,),
        in_specs=[ANY] * len(earlier) + PAIRS[0] + [column(64, 384, 0)] * 2 + [LSE] + [column(1024, 128, 0)] * 2 + [column(1024, 128, 2)] * 2,
        out_specs=[column(64, 384, 0)] + [pl.BlockSpec((1024, 512), lambda j: (0, 0))] * 2,
        out_shape=[shaped(64, 768), shaped(1024, 512), shaped(1024, 512)],
        compiler_params=params(),
        cost_estimate=cost(12 * 64 * 2048 * 64 * 10, 4 << 20, 12 * 64 * 2048),
        name="attend_backward",
    )(*earlier, *masks, query, grad, lse, near, far, near, far)


def choose_kernel(layer, section_ref, gate_ref, up_ref, down_ref, sent_gate_ref, sent_ref, out_ref, sems):
    def copied(pairs):
        copies = [pltpu.make_async_copy(a, b, sems.at[i]) for i, (a, b) in enumerate(pairs)]
        for copy in copies:
            copy.start()
        for copy in copies:
            copy.wait()

    gates, ups, downs = out_ref.at[0:2], out_ref.at[2:4], out_ref.at[4:6]

    @pl.when(section_ref[0] == layer)
    def _():
        copied([(gate_ref, gates), (up_ref, ups), (down_ref, downs)])

    @pl.when(section_ref[0] != layer)
    def _():
        copied([(sent_gate_ref, gates), (sent_ref, out_ref.at[2:6])])


def choose(layer, section, parts, *earlier):
    return pl.pallas_call(
        ignoring(len(earlier), lambda *refs: choose_kernel(layer, *refs)),
        in_specs=[ANY] * len(earlier) + [SMEM] + [ANY] * len(parts),
        out_specs=VMEM,
        out_shape=shaped(6, 384, 256),
        scratch_shapes=[pltpu.SemaphoreType.DMA((3,))],
        compiler_params=params(),
        cost_estimate=cost(0, 3 << 20),
        name="choose",
    )(*earlier, section, *parts)


def side_by_side(parts, axis, *earlier):
    def kernel(*refs):
        refs[-1][...] = jnp.concatenate([ref[...] for ref in refs[:-1]], axis=axis)

    shape = list(parts[0].shape)
    shape[axis] = sum(part.shape[axis] for part in parts)
    return pl.pallas_call(
        ignoring(len(earlier), kernel),
        in_specs=[ANY] * len(earlier) + [VMEM] * len(parts),
        out_specs=VMEM,
        out_shape=jax.ShapeDtypeStruct(tuple(shape), parts[0].dtype),
        compiler_params=params(),
        cost_estimate=cost(0, 2 << 20),
        name="side_by_side",
    )(*earlier, *parts)


def held_until(value, *earlier):
    return pl.pallas_call(
        lambda *refs: None,
        in_specs=[ANY] * (1 + len(earlier)),
        out_specs=ANY,
        out_shape=jax.ShapeDtypeStruct(value.shape, value.dtype),
        input_output_aliases={0: 0},
        name="held_until",
    )(value, *earlier)


def fetched(own, refs, held, sems, where_ref, others):
    def copies(pairs):
        return [pltpu.make_async_copy(a, b, sems.at[i]) for i, (a, b) in enumerate(pairs)]

    mine, sent = copies(refs), copies(others)
    is_own = where_ref[4] == own

    def start():
        @pl.when(is_own)
        def _():
            for copy in mine:
                copy.start()

        @pl.when(jnp.logical_not(is_own))
        def _():
            for copy in sent:
                copy.start()

    def wait():
        @pl.when(is_own)
        def _():
            for copy in mine:
                copy.wait()

        @pl.when(jnp.logical_not(is_own))
        def _():
            for copy in sent:
                copy.wait()

    return start, wait


def fetch_qkv(layer, where_ref, q_ref, k_ref, v_ref, sent_ref, held, sems):
    own, sent = [], []
    for i in range(4):
        rows = slice(i * 384, (i + 1) * 384)
        own += [(q_ref.at[rows], held.at[rows, 0:768]), (k_ref.at[rows], held.at[rows, 768:1024])]
        own += [(v_ref.at[rows], held.at[rows, 1024:1280])]
        sent += [(sent_ref.at[rows, 0:640], held.at[rows, 0:640]), (sent_ref.at[rows, 640:1280], held.at[rows, 640:1280])]
    return fetched(layer, own, held, sems, where_ref, sent)


def fetch_out(layer, where_ref, out_ref, sent_ref, held, sems):
    own, sent = [], []
    for i in range(4):
        rows = slice(i * 192, (i + 1) * 192)
        own.append((out_ref.at[rows], held.at[rows]))
        for h in range(2):
            from_rows = slice(h * 768 + i * 192, h * 768 + (i + 1) * 192)
            sent.append((sent_ref.at[from_rows, 1280:2048], held.at[rows, h * 768 : (h + 1) * 768]))
    return fetched(layer, own, held, sems, where_ref, sent)


QKV_HELD = [pltpu.VMEM((1536, 1280), BF), pltpu.SemaphoreType.DMA((12,))]
OUT_HELD = [pltpu.VMEM((768, 1536), BF), pltpu.SemaphoreType.DMA((8,))]


def normed(value, gain):
    inverse = lax.rsqrt(jnp.mean(value * value, axis=-1, keepdims=True) + EPSILON)
    return inverse, value * inverse * gain


def qkv_kernel(layer, where_ref, hidden_ref, gain_ref, q_ref, k_ref, v_ref, sent_ref, act_ref, out_ref, held, sems):
    start, wait = fetch_qkv(layer, where_ref, q_ref, k_ref, v_ref, sent_ref, held, sems)
    start()
    act = normed(hidden_ref[...], gain_ref[...])[1].astype(BF)
    act_ref[...] = act
    wait()
    out_ref[...] = nn(act, held[...]).astype(BF)


def qkv_of(layer, where, hidden, gain, weights, sent):
    return pl.pallas_call(
        functools.partial(qkv_kernel, layer),
        in_specs=[SMEM, VMEM, VMEM] + [ANY] * 4,
        out_specs=[VMEM, VMEM],
        out_shape=[shaped(64, D), shaped(64, 1280)],
        scratch_shapes=QKV_HELD,
        compiler_params=params(20),
        cost_estimate=cost(64 * 1536 * 1280 * 2, 4 << 20),
        name="qkv_of",
    )(where, hidden, gain, *weights, sent)


def act_back_kernel(layer, where_ref, grad_ref, q_ref, k_ref, v_ref, sent_ref, out_ref, held, sems):
    start, wait = fetch_qkv(layer, where_ref, q_ref, k_ref, v_ref, sent_ref, held, sems)
    start()
    wait()
    out_ref[...] = nt(grad_ref[...], held[...]).astype(BF)


def act_back(layer, where, grad, weights, sent, *earlier):
    return pl.pallas_call(
        ignoring(len(earlier), functools.partial(act_back_kernel, layer)),
        in_specs=[ANY] * len(earlier) + [SMEM, VMEM] + [ANY] * 4,
        out_specs=VMEM,
        out_shape=shaped(64, D),
        scratch_shapes=QKV_HELD,
        compiler_params=params(),
        cost_estimate=cost(64 * 1536 * 1280 * 2, 4 << 20),
        name="act_back",
    )(*earlier, where, grad, *weights, sent)


def middle_back_kernel(
    layer, where_ref, low_ref, got_ref, grad_ref, branch_ref, middle_ref, gain_ref, router_ref, routed_ref, out_w_ref, sent_ref,
    grad_middle_ref, right_ref, mixed_ref, gain_grad_ref, held, sems,
):
    start, wait = fetch_out(layer, where_ref, out_w_ref, sent_ref, held, sems)
    start()
    grad, middle, gain = grad_ref[...], middle_ref[...], gain_ref[...]
    inverse, second = normed(middle, gain)
    routed = routed_ref[...] > 0
    logits = jnp.where(routed, nt(second.astype(BF), router_ref[...]), NEGATIVE)
    raised = jnp.exp(logits - jnp.max(logits, axis=1, keepdims=True))
    raised = jnp.where(routed, raised, 0.0)
    gates = raised / jnp.sum(raised, axis=1, keepdims=True)
    inner = jnp.sum(grad * branch_ref[...], axis=1, keepdims=True)
    own = inner * gates
    high = own.astype(BF)
    low = (own - high.astype(F32)).astype(BF)
    total = low_ref[...].astype(F32) + got_ref[...].astype(F32)
    total = total - nn(high, router_ref[...]) - nn(low, router_ref[...])
    scaled = total * gain
    mean = jnp.mean(scaled * middle, axis=-1, keepdims=True)
    gain_grad_ref[...] = jnp.sum(total * middle * inverse, axis=0, keepdims=True)
    grad_middle = grad + inverse * scaled - inverse * inverse * inverse * middle * mean
    grad_middle_ref[...] = grad_middle
    grad_branch = grad_middle.astype(BF)
    right_ref[:, 0:1536] = grad_branch
    inner_high = inner.astype(BF).astype(F32)
    lane = lax.broadcasted_iota(jnp.int32, (64, 128), 1)
    lanes = jnp.where(lane == 0, inner_high, jnp.where(lane == 1, inner - inner_high, 0.0))
    right_ref[:, 1536:1664] = lanes.astype(BF)
    wait()
    mixed_ref[...] = nt(grad_branch, held[...]).astype(BF)


def middle_back(layer, where, low, got, grad, branch, middle, gain, router, routed, weight, sent):
    return pl.pallas_call(
        functools.partial(middle_back_kernel, layer),
        in_specs=[SMEM] + [VMEM] * 8 + [ANY] * 2,
        out_specs=[VMEM] * 4,
        out_shape=[shaped(64, D, dtype=F32), shaped(64, 1664), shaped(64, 768), shaped(1, D, dtype=F32)],
        scratch_shapes=OUT_HELD,
        compiler_params=params(),
        cost_estimate=cost(64 * 1536 * 768 * 2, 5 << 20),
        name="middle_back",
    )(where, low, got, grad, branch, middle, gain, router, routed, weight, sent)


def whole(*shape):
    return pl.BlockSpec(shape, lambda j: (0,) * len(shape))


class Quarters:
    def __init__(self, refs):
        self.refs = refs

    def __getitem__(self, index):
        return self.refs[index[0]][0, index[1]]


QUARTERS = [pl.BlockSpec((1, 6, 384, 256), functools.partial(lambda r, j: (r, 0, 0, 0), r)) for r in range(4)]


def expert_kernel(where_ref, router_ref, *refs):
    weight_ref, refs = Quarters(refs[:4]), refs[4:]
    token_refs, routed_refs, (pa_ref, pb_ref, pre_ref, mid_ref, gates_ref, all_ref) = refs[:8], refs[8:16], refs[16:]
    for h, out_ref in enumerate((pa_ref, pb_ref)):
        rows = pl.ds(h * 256, 256)
        tokens = stacked(token_refs[4 * h : 4 * h + 4])
        all_ref[rows] = tokens
        parts = [tokens[:, r * 384 : (r + 1) * 384] for r in range(4)]
        routed = stacked(routed_refs[4 * h : 4 * h + 4])[:, 0:16].astype(F32) > 0
        logits = jnp.where(routed, nt(tokens, router_ref[...]), NEGATIVE)
        raised = jnp.exp(logits - jnp.max(logits, axis=1, keepdims=True))
        raised = jnp.where(routed, raised, 0.0)
        gates = raised / jnp.sum(raised, axis=1, keepdims=True)
        expert = lax.broadcasted_iota(jnp.int32, (256, 16), 1) - 2 * where_ref[3]
        gates = jnp.where((expert == 0) | (expert == 1), gates, 0.0)
        gates_ref[rows] = gates
        mids = []
        for e in range(2):
            gate_pre = sum(nn(parts[r], weight_ref[r, e]) for r in range(4))
            up_pre = sum(nn(parts[r], weight_ref[r, 2 + e]) for r in range(4))
            pre_ref[rows, e * 256 : (e + 1) * 256] = gate_pre.astype(BF)
            pre_ref[rows, (2 + e) * 256 : (3 + e) * 256] = up_pre.astype(BF)
            gate = jnp.sum(jnp.where(expert == e, gates, 0.0), axis=1, keepdims=True)
            mid = (gate_pre * jax.nn.sigmoid(gate_pre) * up_pre * gate).astype(BF)
            mid_ref[rows, e * 256 : (e + 1) * 256] = mid
            mids.append(mid)
        for r in range(4):
            made = nt(mids[0], weight_ref[r, 4]) + nt(mids[1], weight_ref[r, 5])
            out_ref[:, r * 384 : (r + 1) * 384] = made.astype(BF)


def experts_forward(where, tokens, given, router, weights, *earlier):
    routed = pl.BlockSpec((64, 128), lambda j: (0, 12))
    return pl.pallas_call(
        ignoring(len(earlier), expert_kernel),
        grid=(1,),
        in_specs=[ANY] * len(earlier)
        + [SMEM, whole(16, D)] + QUARTERS + [whole(64, D)] * 8 + [routed] * 8,
        out_specs=[whole(256, D)] * 2 + [whole(512, 1024), whole(512, 512), whole(512, 16), whole(512, D)],
        out_shape=[shaped(256, D), shaped(256, D), shaped(512, 1024), shaped(512, 512)]
        + [shaped(512, 16, dtype=F32), shaped(512, D)],
        compiler_params=params(),
        cost_estimate=cost(512 * 1536 * 1536 * 2, 10 << 20, 512 * 512),
        name="experts_forward",
    )(*earlier, where, router, *[weights] * 4, *tokens, *given)


def weight_products(out_ref, tokens_ref, grads_ref, gpre_ref, mid_ref):
    for r in range(4):
        lanes = slice(r * 384, (r + 1) * 384)
        for left_ref, right_ref, base in ((tokens_ref, gpre_ref, 0), (grads_ref, mid_ref, 4)):
            total = tn(left_ref[:, lanes], right_ref[...]).astype(BF)
            for n in range(total.shape[1] // 256):
                out_ref[r, base + n] = total[:, n * 256 : (n + 1) * 256]


def expert_back_kernel(order_ref, router_ref, *refs):
    weight_ref, pre_ref, gates_ref, refs = Quarters(refs[:4]), refs[4], refs[5], refs[6:]
    tokens_ref, mid_ref, grad_refs = refs[0], refs[1], refs[2:10]
    pa_ref, pb_ref, gated_ref, weight_grad_ref, all_ref, gpre_ref = refs[10:]
    for h, out_ref in enumerate((pa_ref, pb_ref)):
        rows = pl.ds(h * 256, 256)
        grad_out = stacked(grad_refs[4 * h : 4 * h + 4])
        all_ref[rows] = grad_out
        parts = [grad_out[:, r * 384 : (r + 1) * 384] for r in range(4)]
        gates = gates_ref[rows]
        expert = lax.broadcasted_iota(jnp.int32, (256, 16), 1) - 2 * order_ref[3]
        gated = jnp.zeros((256, 16), F32)
        grads = []
        for e in range(2):
            raw = sum(nn(parts[r], weight_ref[r, 4 + e]) for r in range(4))
            gate_pre = pre_ref[rows, e * 256 : (e + 1) * 256].astype(F32)
            up_pre = pre_ref[rows, (2 + e) * 256 : (3 + e) * 256].astype(F32)
            sigmoid = jax.nn.sigmoid(gate_pre)
            activated = gate_pre * sigmoid
            grad_gates = jnp.sum(activated * up_pre * raw, axis=1, keepdims=True)
            gated = jnp.where(expert == e, gates * grad_gates, gated)
            raw = raw * jnp.sum(jnp.where(expert == e, gates, 0.0), axis=1, keepdims=True)
            grad_gate = (raw * up_pre * sigmoid * (1.0 + gate_pre * (1.0 - sigmoid))).astype(BF)
            grad_up = (raw * activated).astype(BF)
            gpre_ref[rows, e * 256 : (e + 1) * 256] = grad_gate
            gpre_ref[rows, (2 + e) * 256 : (3 + e) * 256] = grad_up
            grads.append((grad_gate, grad_up))
        gated_ref[rows] = gated
        high = gated.astype(BF)
        low = (gated - high.astype(F32)).astype(BF)
        for r in range(4):
            router = router_ref[:, r * 384 : (r + 1) * 384]
            made = nn(high, router) + nn(low, router)
            for e in range(2):
                made = made + nt(grads[e][0], weight_ref[r, e]) + nt(grads[e][1], weight_ref[r, 2 + e])
            out_ref[:, r * 384 : (r + 1) * 384] = made.astype(BF)
    weight_products(weight_grad_ref, tokens_ref, all_ref, gpre_ref, mid_ref)


def experts_backward(where, grads, pre, gates, tokens, mid, router, weights, *earlier):
    return pl.pallas_call(
        ignoring(len(earlier), expert_back_kernel),
        grid=(1,),
        in_specs=[ANY] * len(earlier)
        + [SMEM, whole(16, D)] + QUARTERS + [whole(512, 1024), whole(512, 16)]
        + [whole(512, D), whole(512, 512)] + [whole(64, D)] * 8,
        out_specs=[whole(256, D), whole(256, D), whole(512, 16), whole(4, 6, 384, 256)],
        out_shape=[shaped(256, D), shaped(256, D), shaped(512, 16, dtype=F32), shaped(4, 6, 384, 256)],
        scratch_shapes=[pltpu.VMEM((512, D), BF), pltpu.VMEM((512, 1024), BF)],
        compiler_params=params(),
        cost_estimate=cost(512 * 1536 * 1536 * 2, 10 << 20, 512 * 512),
        name="experts_backward",
    )(*earlier, where, router, *[weights] * 4, pre, gates, tokens, mid, *grads)


def last_expert_kernel(where_ref, router_ref, *refs):
    weight_ref, refs = Quarters(refs[:4]), refs[4:]
    token_refs, given_refs = refs[:8], refs[8:16]
    pa_ref, pb_ref, gates_ref, gated_ref, tokens_ref, weight_grad_ref, mid_ref, gpre_ref, all_ref = refs[16:]
    for h, out_ref in enumerate((pa_ref, pb_ref)):
        rows = pl.ds(h * 256, 256)
        tokens = stacked(token_refs[4 * h : 4 * h + 4])
        tokens_ref[rows] = tokens
        given = stacked(given_refs[4 * h : 4 * h + 4])
        grad_out = given[:, 0:1536]
        all_ref[rows] = grad_out
        parts = [tokens[:, r * 384 : (r + 1) * 384] for r in range(4)]
        grad_parts = [grad_out[:, r * 384 : (r + 1) * 384] for r in range(4)]
        routed = given[:, 1536:1552].astype(F32) > 0
        logits = jnp.where(routed, nt(tokens, router_ref[...]), NEGATIVE)
        raised = jnp.exp(logits - jnp.max(logits, axis=1, keepdims=True))
        raised = jnp.where(routed, raised, 0.0)
        gates = raised / jnp.sum(raised, axis=1, keepdims=True)
        expert = lax.broadcasted_iota(jnp.int32, (256, 16), 1) - 2 * where_ref[3]
        gates = jnp.where((expert == 0) | (expert == 1), gates, 0.0)
        gates_ref[rows] = gates
        gated = jnp.zeros((256, 16), F32)
        mids, grads = [], []
        for e in range(2):
            gate_pre = sum(nn(parts[r], weight_ref[r, e]) for r in range(4))
            up_pre = sum(nn(parts[r], weight_ref[r, 2 + e]) for r in range(4))
            raw = sum(nn(grad_parts[r], weight_ref[r, 4 + e]) for r in range(4))
            gate = jnp.sum(jnp.where(expert == e, gates, 0.0), axis=1, keepdims=True)
            sigmoid = jax.nn.sigmoid(gate_pre)
            activated = gate_pre * sigmoid
            product = activated * up_pre
            mid = (product * gate).astype(BF)
            mid_ref[rows, e * 256 : (e + 1) * 256] = mid
            mids.append(mid)
            gated = jnp.where(expert == e, gates * jnp.sum(product * raw, axis=1, keepdims=True), gated)
            raw = raw * gate
            grad_gate = (raw * up_pre * sigmoid * (1.0 + gate_pre * (1.0 - sigmoid))).astype(BF)
            grad_up = (raw * activated).astype(BF)
            gpre_ref[rows, e * 256 : (e + 1) * 256] = grad_gate
            gpre_ref[rows, (2 + e) * 256 : (3 + e) * 256] = grad_up
            grads.append((grad_gate, grad_up))
        gated_ref[rows] = gated
        high = gated.astype(BF)
        low = (gated - high.astype(F32)).astype(BF)
        for r in range(4):
            lanes = slice(r * 384, (r + 1) * 384)
            made = (nt(mids[0], weight_ref[r, 4]) + nt(mids[1], weight_ref[r, 5])).astype(BF)
            back = nn(high, router_ref[:, lanes]) + nn(low, router_ref[:, lanes])
            for e in range(2):
                back = back + nt(grads[e][0], weight_ref[r, e]) + nt(grads[e][1], weight_ref[r, 2 + e])
            back = back.astype(BF)
            for j in range(4):
                out_ref[j * 128 : j * 128 + 64, lanes] = made[j * 64 : (j + 1) * 64]
                out_ref[j * 128 + 64 : (j + 1) * 128, lanes] = back[j * 64 : (j + 1) * 64]
    weight_products(weight_grad_ref, tokens_ref, all_ref, gpre_ref, mid_ref)


def last_experts(where, tokens, given, router, weights, *earlier):
    return pl.pallas_call(
        ignoring(len(earlier), last_expert_kernel),
        grid=(1,),
        in_specs=[ANY] * len(earlier)
        + [SMEM, whole(16, D)] + QUARTERS + [whole(64, D)] * 8 + [whole(64, 1664)] * 8,
        out_specs=[whole(512, D)] * 2 + [whole(512, 16)] * 2 + [whole(512, D), whole(4, 6, 384, 256)],
        out_shape=[shaped(512, D), shaped(512, D), shaped(512, 16, dtype=F32), shaped(512, 16, dtype=F32)]
        + [shaped(512, D), shaped(4, 6, 384, 256)],
        scratch_shapes=[pltpu.VMEM((512, 512), BF), pltpu.VMEM((512, 1024), BF), pltpu.VMEM((512, D), BF)],
        compiler_params=params(),
        cost_estimate=cost(512 * 1536 * 1536 * 4, 16 << 20, 512 * 512),
        name="last_experts",
    )(*earlier, where, router, *[weights] * 4, *tokens, *given)


def chosen(size, width, me):
    row = lax.broadcasted_iota(jnp.int32, (size, width), 0)
    lane = lax.broadcasted_iota(jnp.int32, (size, width), 1)
    return (row == lane + me * width).astype(BF)


def source(where_ref, b):
    return ((where_ref[1] - (b & 3)) & 3) * 2 + (where_ref[2] if b < 4 else 1 - where_ref[2])


def dense_slice_kernel(pieces, where_ref, gated_ref, gates_ref, gains_ref, *refs):
    me = where_ref[3]
    left, tokens, right_all = stacked(refs[0:4]), stacked(refs[4:8]), stacked(refs[8:12])
    lane_refs, refs = refs[12], refs[13:]
    out_ref = refs[8 if pieces else 0]
    if pieces:
        right = refs[9]
        for b in range(8):
            right[pl.ds(pl.multiple_of(source(where_ref, b) * 64, 64), 64), :] = refs[b][...]
        right = right[...]
    else:
        right = right_all[:, 1664:2944]
    rows = tn(nn(left[:, 0:1536], chosen(1536, 192, me)).astype(BF), right).astype(BF)
    left = nn(left[:, 1536:2304], chosen(768, 96, me)).astype(BF)
    lane = lax.broadcasted_iota(jnp.int32, (64, 16), 1)
    logits = []
    for b in range(8):
        block = slice(b * 64, (b + 1) * 64)
        start = pl.multiple_of(source(where_ref, b) * 64, 64)
        lanes = lane_refs[pl.ds(start, 64), :].astype(F32)
        inner = lanes[:, 0:1] + lanes[:, 1:2]
        grad = gated_ref[block] - 0.5 * gates_ref[block] * inner
        one = [jnp.sum(jnp.where(lane == 2 * me + e, grad, 0.0), axis=1, keepdims=True) for e in range(2)]
        logits.append(jnp.where(lane == 0, one[0], jnp.where(lane == 1, one[1], 0.0)).astype(BF))
    extra = tn(jnp.concatenate(logits, axis=0), tokens)
    row = lax.broadcasted_iota(jnp.int32, (16, D), 0)
    extra = jnp.where(row == 2, gains_ref[...], extra)
    wide = jnp.concatenate([tn(left, right_all[:, 0:1536]), extra], axis=0).astype(BF)
    for r in range(4):
        to = (where_ref[0] - r) & 3
        for c in range(10):
            out_ref[to, c * 48 : (c + 1) * 48] = rows[r * 48 : (r + 1) * 48, c * 128 : (c + 1) * 128]
        for c in range(3):
            lanes = slice(r * 384 + c * 128, r * 384 + (c + 1) * 128)
            out_ref[to, 480 + c * 112 : 480 + (c + 1) * 112] = wide[:, lanes]


def quarters(width, base):
    return [pl.BlockSpec((128, width), functools.partial(lambda i, j: (i, base), i)) for i in range(4)]


def dense_slice(layer, where, left, gated, gates, gains, tokens, right, pieces, *earlier):
    return pl.pallas_call(
        ignoring(len(earlier), functools.partial(dense_slice_kernel, len(pieces) > 0)),
        grid=(1,),
        in_specs=[ANY] * len(earlier)
        + [SMEM, whole(512, 16), whole(512, 16), whole(1, D)]
        + quarters(2304, layer)
        + quarters(D, 0)
        + quarters(right.shape[1], 0)
        + [pl.BlockSpec((512, 128), lambda j: (0, 12))]
        + [whole(64, 1280)] * len(pieces),
        out_specs=whole(4, 816, 128),
        out_shape=shaped(4, 816, 128),
        scratch_shapes=[pltpu.VMEM((512, 1280), BF)] if pieces else [],
        compiler_params=params(),
        cost_estimate=cost(512 * 1536 * 1024 * 2, 8 << 20),
        name="dense_slice",
    )(*earlier, where, gated, gates, gains, *[left] * 4, *[tokens] * 4, *[right] * 5, *pieces)


def dense_rows_kernel(in_ref, q_ref, k_ref, v_ref, out_ref, router_ref, gains_ref, first_ref, held_ref):
    j = pl.program_id(0)
    for x in range(4):
        rows = slice(x * 48, (x + 1) * 48)
        for c in range(10):
            to_ref, lane = (q_ref, c) if c < 6 else (k_ref, c - 6) if c < 8 else (v_ref, c - 8)
            to_ref[rows, lane * 128 : (lane + 1) * 128] = in_ref[x, 0, c * 48 : (c + 1) * 48].astype(F32)
        for c in range(3):
            lanes = slice(x * 384 + c * 128, x * 384 + (c + 1) * 128)
            out_ref[:, lanes] = in_ref[x, 0, 480 + c * 112 : 576 + c * 112].astype(F32)
            held_ref[j, :, lanes] = in_ref[x, 0, 576 + c * 112 : 592 + c * 112].astype(F32)

    own = in_ref[0, 0, 816:832].astype(F32)
    for x in range(1, 4):
        own = own + in_ref[x, 0, 816:832].astype(F32)

    @pl.when(j == 0)
    def _():
        first_ref[...] = own

    @pl.when(j != 0)
    def _():
        first_ref[...] = first_ref[...] + own

    @pl.when(j == 7)
    def _():
        held = held_ref[...]
        router = jnp.concatenate([held[i, 0:2] for i in range(8)], axis=0)
        router_ref[...] = router
        gains_ref[...] = jnp.sum(held, axis=0)


def dense_rows(everything):
    rows = lambda count, width: pl.BlockSpec((count, width), lambda j: (j, 0))
    return pl.pallas_call(
        dense_rows_kernel,
        grid=(8,),
        in_specs=[pl.BlockSpec((4, 1, 832, 128), lambda j: (0, j, 0, 0))],
        out_specs=[rows(192, 768), rows(192, 256), rows(192, 256), rows(96, D), whole(16, D), whole(16, D), whole(16, 128)],
        out_shape=[shaped(D, 768, dtype=F32), shaped(D, 256, dtype=F32), shaped(D, 256, dtype=F32)]
        + [shaped(768, D, dtype=F32), shaped(16, D, dtype=F32), shaped(16, D, dtype=F32)]
        + [shaped(16, 128, dtype=F32)],
        scratch_shapes=[pltpu.VMEM((8, 16, D), F32)],
        compiler_params=params(28),
        cost_estimate=cost(0, 20 << 20),
        name="dense_rows",
    )(everything)


def gates_of(tokens, router, routed):
    logits = dot(tokens, router)
    top = jnp.max(jnp.where(routed > 0, logits, NEGATIVE), axis=1, keepdims=True)
    raised = jnp.where(routed > 0, jnp.exp(jnp.minimum(logits - top, 0.0)), 0.0)
    return raised / jnp.sum(raised, axis=1, keepdims=True)


X_GROUPS = [[(x * NY + y) * 2 + c for x in range(NX)] for y in range(NY) for c in range(2)]


Y_GROUPS = [[(x * NY + y) * 2 + c for y in range(NY) for c in range(2)] for x in range(NX)]


def replica_gather(shard):
    return lax.all_gather(shard, "dp", axis=0, axis_index_groups=X_GROUPS)


def replica_scatter(grads):
    flat = grads.reshape(-1, grads.shape[-1])
    return lax.psum_scatter(flat, "dp", scatter_dimension=0, axis_index_groups=X_GROUPS, tiled=True)


def after(value, *others):
    return lax.optimization_barrier((value, *others))[0]


def group_pieces(block):
    near = [block] + [moved(block, 0, j, 0) for j in (1, 2, 3)]
    return near + [moved(piece, 0, 0, 1) for piece in near]


def ordered(value):
    probe = value[(-1,) * value.ndim]
    return probe == probe


def behind(value, *earlier):
    known = ordered(earlier[0])
    for other in earlier[1:]:
        known = known & ordered(other)
    return jnp.where(known, value, jnp.zeros_like(value))


def per_device(
    inputs,
    cotangent,
    segments,
    routes,
    norm_first,
    w_query,
    w_key,
    w_value,
    w_out,
    norm_second,
    w_router,
    w_gate,
    w_up,
    w_down,
):
    section = lax.axis_index("section")
    place = lax.axis_index("dp")
    here_x, here_y, here_c = place // (NY * 2), place // 2 % NY, place % 2
    me = place % 8
    first = section == 0
    rows = inputs.shape[1]

    def in_order(own, other):
        return jnp.where(first, own, other), jnp.where(first, other, own)

    def pick(pair):
        return lax.dynamic_index_in_dim(pair, section, 0, False)

    weights_in = (w_query[0], w_key[0], w_value[0])
    dense = jnp.concatenate(
        [lax.dynamic_slice_in_dim(w, place * 48, 48, 0) for w in weights_in]
        + [lax.dynamic_slice(w_out[0], (place % 16 * 48, place // 16 * 768), (48, 768))],
        axis=1,
    )
    dense = swapped(dense, "section")

    act_both = norm_apply(inputs.astype(F32), norm_first[0]).astype(BF).reshape(2 * rows, D)
    qkv_both = jnp.concatenate([dot(act_both, w).astype(BF) for w in weights_in], axis=1)
    qkv_sent = lax.ppermute(qkv_both[rows:], "section", [(0, 1)])
    qkv_first = jnp.where(first, qkv_both[:rows], qkv_sent)
    dense_all = lax.all_gather(behind(dense, qkv_both), "dp", axis=0).reshape(D, 2048)

    pack = jnp.concatenate([norm_first, norm_second, w_router[0].T.astype(F32)], axis=0)
    packs = in_order(pack, swapped(pack, "section"))
    routers = [p[2:].astype(BF) for p in packs]
    turned_down = jnp.swapaxes(w_down[0], 1, 2)
    sent_gate = swapped(w_gate[0], "section")
    sent_rest = swapped(side_by_side([w_up[0], turned_down], 0, qkv_sent), "section")
    halves = (w_gate[0], w_up[0], turned_down, sent_gate, sent_rest)
    expert_weights = [None, None]
    where = jnp.stack([here_x, here_y, here_c, me, section]).astype(jnp.int32)

    labels = pick(segments)
    query_labels = lax.dynamic_slice_in_dim(labels, place * rows, rows, 0)
    starts = jnp.sum((labels[None, :] < query_labels[:, None]).astype(jnp.int32), axis=1)
    masks = (where, jnp.concatenate([starts, starts])[None])

    own_routes = pick(routes)
    expert_ids = jnp.arange(EXPERTS, dtype=jnp.int32)
    routed_own = jnp.sum((own_routes[:, :, None] == expert_ids).astype(F32), axis=1)
    given = pick(cotangent)
    sent = jnp.concatenate([given, jnp.pad(routed_own.astype(BF), ((0, 0), (0, 128 - EXPERTS)))], axis=1)
    given_all = group_pieces(sent)

    hidden = pick(inputs).astype(F32)
    saved = []
    for layer in range(2):
        gain_one, gain_two = packs[layer][0:1], packs[layer][1:2]
        if layer == 0:
            activation, qkv = norm_apply(hidden, gain_one).astype(BF), qkv_first
        else:
            activation, qkv = qkv_of(1, where, hidden, gain_one, weights_in, dense_all)
        query, pair = qkv[:, :768], qkv[:, 768:]
        around = [moved(pair, j, 0, 0) for j in (1, 2, 3)]
        slab = jnp.concatenate([pair] + around, axis=0)
        near = [slab] + [moved(slab, 0, j, 0) for j in (1, 2, 3)]
        pieces = near + [moved(piece, 0, 0, 1) for piece in near]
        if layer == 0:
            mixed, log_total, *pieces = attend_forward(0, masks, query, pieces)
        else:
            mixed, log_total, *pieces, partial, lefts = attend_forward(
                1, masks, query, pieces, (*saved[0][8], activation), (w_out[0], dense_all)
            )
        if layer == 0:
            mixed_sent = lax.ppermute(mixed, "section", [(1, 0)])
            partial = dot(jnp.concatenate([mixed, mixed_sent], axis=0), w_out[0]).astype(BF)
            both_axes = ("section", "tensor")
            straight = lax.ppermute(partial[rows:], both_axes, [(0, 2), (1, 3)])
            across = lax.ppermute(partial[rows:], both_axes, [(0, 3), (1, 2)])
            turned = lax.ppermute(partial[:rows], both_axes, [(0, 1), (1, 0)])
            experts_first = choose(0, section[None].astype(jnp.int32), halves, mixed)
            expert_weights[0] = replica_gather(experts_first)
            middle = hidden + (
                jnp.where(first, partial[:rows], straight).astype(F32) + jnp.where(first, turned, across).astype(F32)
            )
        else:
            middle = hidden + (partial.astype(F32) + swapped(partial, "tensor").astype(F32))
        second = norm_apply(middle, gain_two).astype(BF)
        tokens = group_pieces(second)
        if layer == 0:
            experts_second = choose(1, section[None].astype(jnp.int32), halves, second, dense_all)
            expert_weights[1] = replica_gather(experts_second)
        cut = (activation, mixed)
        if layer == 0:
            made_near, made_far, pre, mid, gates, tokens = experts_forward(
                where, tokens, given_all, routers[0], expert_weights[0], experts_second
            )
            made = group_sum(made_near, made_far).reshape(rows, D).astype(BF)
            branch = tensor_sum(made)
            rest = (gates, (pre, mid))
        else:
            near, far, gates, gated, tokens, weight_grads = last_experts(
                where, tokens, given_all, routers[1], expert_weights[1]
            )
            both = (near.astype(F32) + moved(far, 0, 0, 1).astype(F32)).astype(BF)
            low = back_y(both).reshape(2 * rows, D).astype(BF)
            lefts = held_until(lefts, low)
            lefts = lax.all_gather(lefts, "dp", axis=0, axis_index_groups=Y_GROUPS).reshape(8 * rows, 4608)
            got = swapped(low, "tensor")
            branch = low[:rows].astype(F32) + got[:rows].astype(F32)
            low, got = low[rows:], got[rows:]
            rest = (gates, gated)
        result = middle + branch
        saved.append((hidden, query, pieces, log_total, middle, second, tokens, branch, cut, result, rest))
        hidden = result

    def own_of(a, b):
        return jnp.where(first, a, b)

    def from_other(for_first, for_second):
        return swapped(own_of(for_second, for_first).astype(BF), "section").astype(F32)

    def over_sections(a, b):
        return own_of(a, b).astype(F32) + from_other(a, b)

    grad_output = given.astype(F32)
    grads = []
    for layer in (1, 0):
        hidden, query, pieces, log_total, middle, second, tokens, branch, _, _, rest = saved[layer]
        gain_one, gain_two = packs[layer][0:1], packs[layer][1:2]
        router = routers[layer]
        gates, rest = rest
        if layer == 1:
            gated = rest
        else:
            back_near, back_far, gated, weight_grads = experts_backward(
                where, group_pieces(grad_output.astype(BF)), rest[0], gates, tokens, rest[1], router, expert_weights[0], *earlier
            )
            both = (back_near.astype(F32) + moved(back_far, 0, 0, 1).astype(F32)).astype(BF)
            low = back_y(both).reshape(rows, D).astype(BF)
            got = swapped(low, "tensor")
        expert_part = replica_scatter(weight_grads)
        grad_middle, right, grad_mixed, gain_two_grad = middle_back(
            layer, where, low, got, grad_output, branch, middle, gain_two, router, routed_own, w_out[0], dense_all
        )
        grad_query, back_near, back_far = attend_backward(masks, query, grad_mixed, log_total, *pieces)
        both = (back_near.astype(F32) + moved(back_far, 0, 0, 1).astype(F32)).astype(BF)
        half = back_y(both)
        if layer == 0:
            late = dense_slice(1, *grads[0][1], [], both)
            half = behind(half, late)
        grad_pair = back_x(half.astype(BF)).reshape(rows, 512).astype(BF)
        grad_qkv = jnp.concatenate([grad_query, grad_pair], axis=1)
        if layer == 0:
            grad_qkv = held_until(grad_qkv, expert_part)
            right_pieces = group_pieces(grad_qkv)
        partial = act_back(layer, where, grad_qkv, weights_in, dense_all, lefts if layer == 1 else right_pieces[1])
        grad_activation = partial.astype(F32) + swapped(partial, "tensor").astype(F32)
        grad_from_first, gain_one_grad = norm_back(hidden, gain_one, grad_activation)
        grad_input = grad_middle + grad_from_first
        if layer == 1:
            right = jnp.concatenate([right, grad_qkv], axis=1)
            earlier = [right, expert_part]
            right = lax.all_gather(right, "dp", axis=0, axis_index_groups=Y_GROUPS).reshape(8 * rows, 2944)
            grads.append((grad_input, (where, lefts, gated, gates, gain_two_grad, tokens, right), expert_part, gain_one_grad))
        else:
            right = lax.all_gather(right, "dp", axis=0, axis_index_groups=Y_GROUPS).reshape(8 * rows, 1664)
            blocks = dense_slice(0, where, lefts, gated, gates, gain_two_grad, tokens, right, right_pieces, partial)
            late = back_x(late.reshape(4 * 816, 128)).reshape(816, 128)
            grads.append((grad_input, back_x(blocks.reshape(4 * 816, 128)).reshape(816, 128), expert_part, gain_one_grad))
        grad_output = grad_input
    grads = grads[::-1]

    def by_batch(own, other):
        return jnp.stack([jnp.where(first, own, other), jnp.where(first, other, own)])[None]

    results = by_batch(own_of(saved[0][9], saved[1][9]), from_other(saved[0][9], saved[1][9]))
    input_grads = by_batch(own_of(grads[0][0], grads[1][0]), from_other(grads[0][0], grads[1][0]))
    first_part = grads[0][1]

    def extras(block):
        return block[480:816].reshape(3, 112, 128)[:, 96:98].reshape(6, 128)

    straight = swapped(jnp.concatenate([extras(first_part), extras(late)], axis=0).astype(BF), "tensor").astype(F32)
    across = lax.ppermute(
        own_of(extras(late), extras(first_part)).astype(BF), ("section", "tensor"), [(0, 3), (1, 2), (2, 1), (3, 0)]
    ).astype(F32)
    gain_rows = [jnp.pad(g[3].reshape(12, 128), ((0, 4), (0, 0))) for g in grads]
    block = over_sections(*[jnp.concatenate(pair, axis=0) for pair in ((first_part, gain_rows[0]), (late, gain_rows[1]))])
    more = own_of(straight[:6], straight[6:]) + across
    wide = block[480:816].reshape(3, 112, 128)
    wide = wide + jnp.pad(more.reshape(3, 2, 128), ((0, 0), (96, 14), (0, 0)))
    block = jnp.concatenate([block[:480], wide.reshape(336, 128), block[816:]], axis=0).astype(BF)
    everything = lax.all_gather(block, "dp", axis=0).reshape(4, 8, 832, 128)
    query_sum, key_sum, value_sum, out_full, router_sum, gains, gain_one_sum = dense_rows(everything)
    expert_sum = over_sections(grads[0][2], grads[1][2]).reshape(3, 2, 384, 256)
    return (
        results,
        input_grads,
        gain_one_sum[:12].reshape(1, D),
        query_sum[None],
        key_sum[None],
        value_sum[None],
        out_full[None],
        gains[2:3],
        router_sum.T[None],
        expert_sum[0][None],
        expert_sum[1][None],
        jnp.swapaxes(expert_sum[2], 1, 2)[None],
    )


def solution(mesh):
    in_specs = (
        P(None, "dp", None),
        P(None, "dp", None),
        P(),
        P(None, "dp", None),
        P("section", None),
        P("section", None, "tensor"),
        P("section", None, "tensor"),
        P("section", None, "tensor"),
        P("section", "tensor", None),
        P("section", None),
        P("section", None, None),
        P("section", "dp", None, "tensor"),
        P("section", "dp", None, "tensor"),
        P("section", "dp", "tensor", None),
    )
    out_specs = (
        P("section", None, "dp", None),
        P("section", None, "dp", None),
        P("section", None),
        P("section", None, "tensor"),
        P("section", None, "tensor"),
        P("section", None, "tensor"),
        P("section", "tensor", None),
        P("section", None),
        P("section", None, None),
        P("section", "dp", None, "tensor"),
        P("section", "dp", None, "tensor"),
        P("section", "dp", "tensor", None),
    )
    return jax.shard_map(
        per_device, mesh=mesh, in_specs=in_specs, out_specs=out_specs, check_vma=False
    )
```

```python
import functools

import jax
import jax.numpy as jnp
from jax import lax
from jax.experimental import pallas as pl
from jax.experimental.pallas import tpu as pltpu
from jax.sharding import PartitionSpec as P

D = 1536
HD = 64
EXPERTS = 16
NX, NY = 4, 4
EPSILON = 1e-06
SCALE = 0.125
NEGATIVE = -1e30
BF = jnp.bfloat16
F32 = jnp.float32


def moved(value, dx, dy, dc):
    route = []
    for x in range(NX):
        for y in range(NY):
            for c in range(2):
                target = (((x + dx) % NX) * NY + (y + dy) % NY) * 2 + (c ^ dc)
                route.append(((x * NY + y) * 2 + c, target))
    return lax.ppermute(value, "dp", route)


def swapped(value, axis):
    return lax.ppermute(value, axis, [(0, 1), (1, 0)])


def along_y(block):
    return jnp.concatenate([block] + [moved(block, 0, j, 0) for j in (1, 2, 3)], axis=0)


def along_x(block):
    return jnp.concatenate([block] + [moved(block, j, 0, 0) for j in (1, 2, 3)], axis=0)


def back_y(sums):
    parts = sums.reshape(4, -1, sums.shape[-1])
    total = parts[0].astype(F32)
    for j in (1, 2, 3):
        total = total + moved(parts[j], 0, -j, 0).astype(F32)
    return total


def back_x(sums):
    parts = sums.reshape(4, -1, sums.shape[-1])
    total = parts[0].astype(F32)
    for j in (1, 2, 3):
        total = total + moved(parts[j], -j, 0, 0).astype(F32)
    return total


def group_gather(block):
    column = along_y(block)
    return column, moved(column, 0, 0, 1)


def group_sum(own, other):
    both = own.astype(F32) + moved(other, 0, 0, 1).astype(F32)
    return back_y(both.astype(BF))


def tensor_sum(value):
    low = value.astype(BF)
    return low.astype(F32) + swapped(low, "tensor").astype(F32)


def norm_apply(value, gain):
    inverse = lax.rsqrt(jnp.mean(value * value, axis=-1, keepdims=True) + EPSILON)
    return value * inverse * gain


def norm_back(value, gain, grad):
    inverse = lax.rsqrt(jnp.mean(value * value, axis=-1, keepdims=True) + EPSILON)
    scaled = grad * gain
    inner = jnp.mean(scaled * value, axis=-1, keepdims=True)
    gain_grad = jnp.sum(grad * value * inverse, axis=0)
    return (inverse * scaled - inverse * inverse * inverse * value * inner, gain_grad)


def dot(left, right):
    return jnp.dot(left, right, preferred_element_type=F32)


def over_rows(left, right):
    return lax.dot_general(left, right, (((0,), (0,)), ((), ())), preferred_element_type=F32)


def against(left, right):
    return lax.dot_general(left, right, (((1,), (1,)), ((), ())), preferred_element_type=F32)


def nn(a, b):
    return lax.dot_general(a, b, (((1,), (0,)), ((), ())), preferred_element_type=F32)


def nt(a, b):
    return lax.dot_general(a, b, (((1,), (1,)), ((), ())), preferred_element_type=F32)


def tn(a, b):
    return lax.dot_general(a, b, (((0,), (0,)), ((), ())), preferred_element_type=F32)


SMEM = pl.BlockSpec(memory_space=pltpu.SMEM)
VMEM = pl.BlockSpec(memory_space=pltpu.VMEM)
ANY = pl.BlockSpec(memory_space=pl.ANY)
HBM = pl.BlockSpec(memory_space=pltpu.HBM)


def shaped(*shape, dtype=BF):
    return jax.ShapeDtypeStruct(shape, dtype)


def params(mib=58):
    return pltpu.CompilerParams(vmem_limit_bytes=mib << 20)


def cost(flops, bytes_accessed, exps=0):
    return pl.CostEstimate(flops=flops, bytes_accessed=bytes_accessed, transcendentals=exps)


def stacked(refs):
    return jnp.concatenate([ref[...] for ref in refs], axis=0)


def spread(block):
    lane = lax.broadcasted_iota(jnp.int32, (64, 128), 1)
    parts = []
    for k in range(6):
        wide = block[:, (k // 2) * 128 : (k // 2 + 1) * 128].astype(F32)
        half = k // 3
        if k % 2 != half:
            wide = pltpu.roll(wide, 64, 1)
        parts.append(jnp.where((lane >= 64) == (half == 1), wide, 0.0))
    return jnp.concatenate(parts, axis=0)


def gathered(turned):
    rows = turned.T
    lane = lax.broadcasted_iota(jnp.int32, (64, 128), 1)
    outs = []
    for b in range(3):
        two = []
        for k in (2 * b, 2 * b + 1):
            part = rows[k * 64 : (k + 1) * 64]
            if k % 2 != k // 3:
                part = pltpu.roll(part, 64, 1)
            two.append(part)
        outs.append(jnp.where(lane < 64, two[0], two[1]))
    return jnp.concatenate(outs, axis=1)


def bias_of(place_ref, h, start_ref):
    row = lax.broadcasted_iota(jnp.int32, (1024, 128), 0)
    token = lax.broadcasted_iota(jnp.int32, (1024, 128), 1) & 63
    x = (place_ref[0] - (row >> 6)) & 3
    y = (place_ref[1] - (row >> 8)) & 3
    c = place_ref[2] if h == 0 else 1 - place_ref[2]
    key = ((x * 4 + y) * 2 + c) * 64 + (row & 63)
    query = ((place_ref[0] * 4 + place_ref[1]) * 2 + place_ref[2]) * 64 + token
    bias = jnp.where((key <= query) & (key >= start_ref[...]), 0.0, NEGATIVE)
    return jnp.concatenate([bias, bias, bias], axis=1)


def attend_kernel(layer, place_ref, st_ref, q_ref, *refs):
    j = pl.program_id(0)
    keys = [stacked(refs[0:4]), stacked(refs[4:8])]
    values = [stacked(refs[8:12]), stacked(refs[12:16])]
    if layer == 1:
        earlier_refs, act_ref, out_w_ref, sent_ref = refs[16:18], refs[18], refs[19], refs[20]
        out_ref, lse_ref, near_ref, far_ref, partial_ref, lefts_ref, held, sems = refs[21:]
        start, wait = fetch_out(layer, place_ref, out_w_ref, sent_ref, held, sems)
        pl.when(j == 0)(start)
    else:
        out_ref, lse_ref, near_ref, far_ref = refs[16:]
    for k, v, to_ref in zip(keys, values, (near_ref, far_ref)):
        to_ref[:, pl.ds(pl.multiple_of(j * 128, 128), 128)] = k
        to_ref[:, pl.ds(pl.multiple_of(256 + j * 128, 128), 128)] = v
    query = (spread(q_ref[...]) * 0.125).astype(BF)
    scores = [nt(k, query) + bias_of(place_ref, h, st_ref) for h, k in enumerate(keys)]
    top = jnp.maximum(*[jnp.max(s, axis=0, keepdims=True) for s in scores])
    total = jnp.zeros_like(top)
    mixed = jnp.zeros((128, 384), F32)
    for s, v in zip(scores, values):
        raised = jnp.exp(s - top)
        total = total + jnp.sum(raised, axis=0, keepdims=True)
        mixed = mixed + tn(v, raised.astype(BF))
    out_ref[:, pl.ds(pl.multiple_of(j * 384, 128), 384)] = gathered(mixed / total).astype(BF)
    lse_ref[0] = top + jnp.log(total)
    if layer == 1:

        @pl.when(j == 1)
        def _():
            wait()
            partial_ref[...] = nn(out_ref[...], held[...]).astype(BF)
            lefts_ref[:, 0:1536], lefts_ref[:, 1536:2304] = earlier_refs[0][...], earlier_refs[1][...]
            lefts_ref[:, 2304:3840], lefts_ref[:, 3840:4608] = act_ref[...], out_ref[...]


def column(rows, width, base):
    return pl.BlockSpec((rows, width), lambda j: (0, j + base))


PAIRS = [SMEM, pl.BlockSpec((1, 128), lambda j: (0, 0))], [column(256, 128, 0)] * 8 + [column(256, 128, 2)] * 8
LSE = pl.BlockSpec((1, 1, 384), lambda j: (j, 0, 0))


def ignoring(count, kernel):
    return lambda *refs: kernel(*refs[count:])


def fixed(*shape):
    return pl.BlockSpec(shape, lambda j: (0,) * len(shape))


def attend_forward(layer, masks, query, pieces, factors=(), weights=()):
    last = layer == 1
    return pl.pallas_call(
        functools.partial(attend_kernel, layer),
        grid=(2,),
        in_specs=PAIRS[0] + [column(64, 384, 0)] + PAIRS[1] + [fixed(*f.shape) for f in factors] + [HBM] * len(weights),
        out_specs=[fixed(64, 768), LSE, fixed(1024, 512), fixed(1024, 512)] + [fixed(64, D), fixed(64, 4608)] * last,
        out_shape=[shaped(64, 768), shaped(2, 1, 384, dtype=F32), shaped(1024, 512), shaped(1024, 512)]
        + [shaped(64, D), shaped(64, 4608)] * last,
        scratch_shapes=OUT_HELD if last else [],
        compiler_params=params(),
        cost_estimate=cost(12 * 64 * 2048 * 64 * 4, 2 << 20, 12 * 64 * 2048),
        name="attend_forward",
    )(*masks, query, *pieces, *pieces, *factors, *weights)


def attend_back_kernel(place_ref, st_ref, q_ref, do_ref, lse_ref, *refs):
    j = pl.program_id(0)
    key_columns = pl.ds(pl.multiple_of(j * 128, 128), 128)
    value_columns = pl.ds(pl.multiple_of(256 + j * 128, 128), 128)
    keys, values = [ref[...] for ref in refs[0:2]], [ref[...] for ref in refs[2:4]]
    dq_ref, near_ref, far_ref = refs[4:]
    query = (spread(q_ref[...]) * 0.125).astype(BF)
    grad = spread(do_ref[...]).astype(BF)
    weights, raws = [], []
    inner = jnp.zeros((1, 384), F32)
    for h, (k, v) in enumerate(zip(keys, values)):
        s = nt(k, query) + bias_of(place_ref, h, st_ref)
        w = jnp.exp(s - lse_ref[0])
        raw = nt(v, grad)
        inner = inner + jnp.sum(w * raw, axis=0, keepdims=True)
        weights.append(w)
        raws.append(raw)
    turned = jnp.zeros((128, 384), F32)
    for w, raw, k, out_ref in zip(weights, raws, keys, (near_ref, far_ref)):
        ds = (w * (raw - inner)).astype(BF)
        out_ref[:, key_columns] = nn(ds, query).astype(BF)
        out_ref[:, value_columns] = nn(w.astype(BF), grad).astype(BF)
        turned = turned + tn(k, ds)
    dq_ref[...] = gathered(turned * 0.125).astype(BF)


def attend_backward(masks, query, grad, lse, near, far, *earlier):
    return pl.pallas_call(
        ignoring(len(earlier), attend_back_kernel),
        grid=(2,),
        in_specs=[ANY] * len(earlier) + PAIRS[0] + [column(64, 384, 0)] * 2 + [LSE] + [column(1024, 128, 0)] * 2 + [column(1024, 128, 2)] * 2,
        out_specs=[column(64, 384, 0)] + [pl.BlockSpec((1024, 512), lambda j: (0, 0))] * 2,
        out_shape=[shaped(64, 768), shaped(1024, 512), shaped(1024, 512)],
        compiler_params=params(),
        cost_estimate=cost(12 * 64 * 2048 * 64 * 10, 4 << 20, 12 * 64 * 2048),
        name="attend_backward",
    )(*earlier, *masks, query, grad, lse, near, far, near, far)


def choose_kernel(layer, section_ref, gate_ref, up_ref, down_ref, sent_gate_ref, sent_ref, out_ref, sems):
    def copied(pairs):
        copies = [pltpu.make_async_copy(a, b, sems.at[i]) for i, (a, b) in enumerate(pairs)]
        for copy in copies:
            copy.start()
        for copy in copies:
            copy.wait()

    gates, ups, downs = out_ref.at[0:2], out_ref.at[2:4], out_ref.at[4:6]

    @pl.when(section_ref[0] == layer)
    def _():
        copied([(gate_ref, gates), (up_ref, ups), (down_ref, downs)])

    @pl.when(section_ref[0] != layer)
    def _():
        copied([(sent_gate_ref, gates), (sent_ref, out_ref.at[2:6])])


def choose(layer, section, parts, *earlier):
    return pl.pallas_call(
        ignoring(len(earlier), lambda *refs: choose_kernel(layer, *refs)),
        in_specs=[ANY] * len(earlier) + [SMEM] + [ANY] * len(parts),
        out_specs=VMEM,
        out_shape=shaped(6, 384, 256),
        scratch_shapes=[pltpu.SemaphoreType.DMA((3,))],
        compiler_params=params(),
        cost_estimate=cost(0, 3 << 20),
        name="choose",
    )(*earlier, section, *parts)


def side_by_side(parts, axis, *earlier):
    def kernel(*refs):
        refs[-1][...] = jnp.concatenate([ref[...] for ref in refs[:-1]], axis=axis)

    shape = list(parts[0].shape)
    shape[axis] = sum(part.shape[axis] for part in parts)
    return pl.pallas_call(
        ignoring(len(earlier), kernel),
        in_specs=[ANY] * len(earlier) + [VMEM] * len(parts),
        out_specs=VMEM,
        out_shape=jax.ShapeDtypeStruct(tuple(shape), parts[0].dtype),
        compiler_params=params(),
        cost_estimate=cost(0, 2 << 20),
        name="side_by_side",
    )(*earlier, *parts)


def held_until(value, *earlier):
    return pl.pallas_call(
        lambda *refs: None,
        in_specs=[ANY] * (1 + len(earlier)),
        out_specs=ANY,
        out_shape=jax.ShapeDtypeStruct(value.shape, value.dtype),
        input_output_aliases={0: 0},
        name="held_until",
    )(value, *earlier)


def fetched(own, refs, held, sems, where_ref, others):
    def copies(pairs):
        return [pltpu.make_async_copy(a, b, sems.at[i]) for i, (a, b) in enumerate(pairs)]

    mine, sent = copies(refs), copies(others)
    is_own = where_ref[4] == own

    def start():
        @pl.when(is_own)
        def _():
            for copy in mine:
                copy.start()

        @pl.when(jnp.logical_not(is_own))
        def _():
            for copy in sent:
                copy.start()

    def wait():
        @pl.when(is_own)
        def _():
            for copy in mine:
                copy.wait()

        @pl.when(jnp.logical_not(is_own))
        def _():
            for copy in sent:
                copy.wait()

    return start, wait


def fetch_qkv(layer, where_ref, q_ref, k_ref, v_ref, sent_ref, held, sems):
    own, sent = [], []
    for i in range(4):
        rows = slice(i * 384, (i + 1) * 384)
        own += [(q_ref.at[rows], held.at[rows, 0:768]), (k_ref.at[rows], held.at[rows, 768:1024])]
        own += [(v_ref.at[rows], held.at[rows, 1024:1280])]
        sent += [(sent_ref.at[rows, 0:640], held.at[rows, 0:640]), (sent_ref.at[rows, 640:1280], held.at[rows, 640:1280])]
    return fetched(layer, own, held, sems, where_ref, sent)


def fetch_out(layer, where_ref, out_ref, sent_ref, held, sems):
    own, sent = [], []
    for i in range(4):
        rows = slice(i * 192, (i + 1) * 192)
        own.append((out_ref.at[rows], held.at[rows]))
        for h in range(2):
            from_rows = slice(h * 768 + i * 192, h * 768 + (i + 1) * 192)
            sent.append((sent_ref.at[from_rows, 1280:2048], held.at[rows, h * 768 : (h + 1) * 768]))
    return fetched(layer, own, held, sems, where_ref, sent)


QKV_HELD = [pltpu.VMEM((1536, 1280), BF), pltpu.SemaphoreType.DMA((12,))]
OUT_HELD = [pltpu.VMEM((768, 1536), BF), pltpu.SemaphoreType.DMA((8,))]


def normed(value, gain):
    inverse = lax.rsqrt(jnp.mean(value * value, axis=-1, keepdims=True) + EPSILON)
    return inverse, value * inverse * gain


def qkv_kernel(layer, where_ref, hidden_ref, gain_ref, q_ref, k_ref, v_ref, sent_ref, act_ref, out_ref, held, sems):
    start, wait = fetch_qkv(layer, where_ref, q_ref, k_ref, v_ref, sent_ref, held, sems)
    start()
    act = normed(hidden_ref[...], gain_ref[...])[1].astype(BF)
    act_ref[...] = act
    wait()
    out_ref[...] = nn(act, held[...]).astype(BF)


def qkv_of(layer, where, hidden, gain, weights, sent):
    return pl.pallas_call(
        functools.partial(qkv_kernel, layer),
        in_specs=[SMEM, VMEM, VMEM] + [ANY] * 4,
        out_specs=[VMEM, VMEM],
        out_shape=[shaped(64, D), shaped(64, 1280)],
        scratch_shapes=QKV_HELD,
        compiler_params=params(20),
        cost_estimate=cost(64 * 1536 * 1280 * 2, 4 << 20),
        name="qkv_of",
    )(where, hidden, gain, *weights, sent)


def act_back_kernel(layer, where_ref, grad_ref, q_ref, k_ref, v_ref, sent_ref, out_ref, held, sems):
    start, wait = fetch_qkv(layer, where_ref, q_ref, k_ref, v_ref, sent_ref, held, sems)
    start()
    wait()
    out_ref[...] = nt(grad_ref[...], held[...]).astype(BF)


def act_back(layer, where, grad, weights, sent, *earlier):
    return pl.pallas_call(
        ignoring(len(earlier), functools.partial(act_back_kernel, layer)),
        in_specs=[ANY] * len(earlier) + [SMEM, VMEM] + [ANY] * 4,
        out_specs=VMEM,
        out_shape=shaped(64, D),
        scratch_shapes=QKV_HELD,
        compiler_params=params(),
        cost_estimate=cost(64 * 1536 * 1280 * 2, 4 << 20),
        name="act_back",
    )(*earlier, where, grad, *weights, sent)


def middle_back_kernel(
    layer, where_ref, low_ref, got_ref, grad_ref, branch_ref, middle_ref, gain_ref, router_ref, routed_ref, out_w_ref, sent_ref,
    grad_middle_ref, right_ref, mixed_ref, gain_grad_ref, held, sems,
):
    start, wait = fetch_out(layer, where_ref, out_w_ref, sent_ref, held, sems)
    start()
    grad, middle, gain = grad_ref[...], middle_ref[...], gain_ref[...]
    inverse, second = normed(middle, gain)
    routed = routed_ref[...] > 0
    logits = jnp.where(routed, nt(second.astype(BF), router_ref[...]), NEGATIVE)
    raised = jnp.exp(logits - jnp.max(logits, axis=1, keepdims=True))
    raised = jnp.where(routed, raised, 0.0)
    gates = raised / jnp.sum(raised, axis=1, keepdims=True)
    inner = jnp.sum(grad * branch_ref[...], axis=1, keepdims=True)
    own = inner * gates
    high = own.astype(BF)
    low = (own - high.astype(F32)).astype(BF)
    total = low_ref[...].astype(F32) + got_ref[...].astype(F32)
    total = total - nn(high, router_ref[...]) - nn(low, router_ref[...])
    scaled = total * gain
    mean = jnp.mean(scaled * middle, axis=-1, keepdims=True)
    gain_grad_ref[...] = jnp.sum(total * middle * inverse, axis=0, keepdims=True)
    grad_middle = grad + inverse * scaled - inverse * inverse * inverse * middle * mean
    grad_middle_ref[...] = grad_middle
    grad_branch = grad_middle.astype(BF)
    right_ref[:, 0:1536] = grad_branch
    inner_high = inner.astype(BF).astype(F32)
    lane = lax.broadcasted_iota(jnp.int32, (64, 128), 1)
    lanes = jnp.where(lane == 0, inner_high, jnp.where(lane == 1, inner - inner_high, 0.0))
    right_ref[:, 1536:1664] = lanes.astype(BF)
    wait()
    mixed_ref[...] = nt(grad_branch, held[...]).astype(BF)


def middle_back(layer, where, low, got, grad, branch, middle, gain, router, routed, weight, sent):
    return pl.pallas_call(
        functools.partial(middle_back_kernel, layer),
        in_specs=[SMEM] + [VMEM] * 8 + [ANY] * 2,
        out_specs=[VMEM] * 4,
        out_shape=[shaped(64, D, dtype=F32), shaped(64, 1664), shaped(64, 768), shaped(1, D, dtype=F32)],
        scratch_shapes=OUT_HELD,
        compiler_params=params(),
        cost_estimate=cost(64 * 1536 * 768 * 2, 5 << 20),
        name="middle_back",
    )(where, low, got, grad, branch, middle, gain, router, routed, weight, sent)


def whole(*shape):
    return pl.BlockSpec(shape, lambda j: (0,) * len(shape))


class Quarters:
    def __init__(self, refs):
        self.refs = refs

    def __getitem__(self, index):
        return self.refs[index[0]][0, index[1]]


QUARTERS = [pl.BlockSpec((1, 6, 384, 256), functools.partial(lambda r, j: (r, 0, 0, 0), r)) for r in range(4)]


def expert_kernel(where_ref, router_ref, *refs):
    weight_ref, refs = Quarters(refs[:4]), refs[4:]
    token_refs, routed_refs, (pa_ref, pb_ref, pre_ref, mid_ref, gates_ref, all_ref) = refs[:8], refs[8:16], refs[16:]
    for h, out_ref in enumerate((pa_ref, pb_ref)):
        rows = pl.ds(h * 256, 256)
        tokens = stacked(token_refs[4 * h : 4 * h + 4])
        all_ref[rows] = tokens
        parts = [tokens[:, r * 384 : (r + 1) * 384] for r in range(4)]
        routed = stacked(routed_refs[4 * h : 4 * h + 4])[:, 0:16].astype(F32) > 0
        logits = jnp.where(routed, nt(tokens, router_ref[...]), NEGATIVE)
        raised = jnp.exp(logits - jnp.max(logits, axis=1, keepdims=True))
        raised = jnp.where(routed, raised, 0.0)
        gates = raised / jnp.sum(raised, axis=1, keepdims=True)
        expert = lax.broadcasted_iota(jnp.int32, (256, 16), 1) - 2 * where_ref[3]
        gates = jnp.where((expert == 0) | (expert == 1), gates, 0.0)
        gates_ref[rows] = gates
        mids = []
        for e in range(2):
            gate_pre = sum(nn(parts[r], weight_ref[r, e]) for r in range(4))
            up_pre = sum(nn(parts[r], weight_ref[r, 2 + e]) for r in range(4))
            pre_ref[rows, e * 256 : (e + 1) * 256] = gate_pre.astype(BF)
            pre_ref[rows, (2 + e) * 256 : (3 + e) * 256] = up_pre.astype(BF)
            gate = jnp.sum(jnp.where(expert == e, gates, 0.0), axis=1, keepdims=True)
            mid = (gate_pre * jax.nn.sigmoid(gate_pre) * up_pre * gate).astype(BF)
            mid_ref[rows, e * 256 : (e + 1) * 256] = mid
            mids.append(mid)
        for r in range(4):
            made = nt(mids[0], weight_ref[r, 4]) + nt(mids[1], weight_ref[r, 5])
            out_ref[:, r * 384 : (r + 1) * 384] = made.astype(BF)


def experts_forward(where, tokens, given, router, weights, *earlier):
    routed = pl.BlockSpec((64, 128), lambda j: (0, 12))
    return pl.pallas_call(
        ignoring(len(earlier), expert_kernel),
        grid=(1,),
        in_specs=[ANY] * len(earlier)
        + [SMEM, whole(16, D)] + QUARTERS + [whole(64, D)] * 8 + [routed] * 8,
        out_specs=[whole(256, D)] * 2 + [whole(512, 1024), whole(512, 512), whole(512, 16), whole(512, D)],
        out_shape=[shaped(256, D), shaped(256, D), shaped(512, 1024), shaped(512, 512)]
        + [shaped(512, 16, dtype=F32), shaped(512, D)],
        compiler_params=params(),
        cost_estimate=cost(512 * 1536 * 1536 * 2, 10 << 20, 512 * 512),
        name="experts_forward",
    )(*earlier, where, router, *[weights] * 4, *tokens, *given)


def weight_products(out_ref, tokens_ref, grads_ref, gpre_ref, mid_ref):
    for r in range(4):
        lanes = slice(r * 384, (r + 1) * 384)
        for left_ref, right_ref, base in ((tokens_ref, gpre_ref, 0), (grads_ref, mid_ref, 4)):
            total = tn(left_ref[:, lanes], right_ref[...]).astype(BF)
            for n in range(total.shape[1] // 256):
                out_ref[r, base + n] = total[:, n * 256 : (n + 1) * 256]


def expert_back_kernel(order_ref, router_ref, *refs):
    weight_ref, pre_ref, gates_ref, refs = Quarters(refs[:4]), refs[4], refs[5], refs[6:]
    tokens_ref, mid_ref, grad_refs = refs[0], refs[1], refs[2:10]
    pa_ref, pb_ref, gated_ref, weight_grad_ref, all_ref, gpre_ref = refs[10:]
    for h, out_ref in enumerate((pa_ref, pb_ref)):
        rows = pl.ds(h * 256, 256)
        grad_out = stacked(grad_refs[4 * h : 4 * h + 4])
        all_ref[rows] = grad_out
        parts = [grad_out[:, r * 384 : (r + 1) * 384] for r in range(4)]
        gates = gates_ref[rows]
        expert = lax.broadcasted_iota(jnp.int32, (256, 16), 1) - 2 * order_ref[3]
        gated = jnp.zeros((256, 16), F32)
        grads = []
        for e in range(2):
            raw = sum(nn(parts[r], weight_ref[r, 4 + e]) for r in range(4))
            gate_pre = pre_ref[rows, e * 256 : (e + 1) * 256].astype(F32)
            up_pre = pre_ref[rows, (2 + e) * 256 : (3 + e) * 256].astype(F32)
            sigmoid = jax.nn.sigmoid(gate_pre)
            activated = gate_pre * sigmoid
            grad_gates = jnp.sum(activated * up_pre * raw, axis=1, keepdims=True)
            gated = jnp.where(expert == e, gates * grad_gates, gated)
            raw = raw * jnp.sum(jnp.where(expert == e, gates, 0.0), axis=1, keepdims=True)
            grad_gate = (raw * up_pre * sigmoid * (1.0 + gate_pre * (1.0 - sigmoid))).astype(BF)
            grad_up = (raw * activated).astype(BF)
            gpre_ref[rows, e * 256 : (e + 1) * 256] = grad_gate
            gpre_ref[rows, (2 + e) * 256 : (3 + e) * 256] = grad_up
            grads.append((grad_gate, grad_up))
        gated_ref[rows] = gated
        high = gated.astype(BF)
        low = (gated - high.astype(F32)).astype(BF)
        for r in range(4):
            router = router_ref[:, r * 384 : (r + 1) * 384]
            made = nn(high, router) + nn(low, router)
            for e in range(2):
                made = made + nt(grads[e][0], weight_ref[r, e]) + nt(grads[e][1], weight_ref[r, 2 + e])
            out_ref[:, r * 384 : (r + 1) * 384] = made.astype(BF)
    weight_products(weight_grad_ref, tokens_ref, all_ref, gpre_ref, mid_ref)


def experts_backward(where, grads, pre, gates, tokens, mid, router, weights, *earlier):
    return pl.pallas_call(
        ignoring(len(earlier), expert_back_kernel),
        grid=(1,),
        in_specs=[ANY] * len(earlier)
        + [SMEM, whole(16, D)] + QUARTERS + [whole(512, 1024), whole(512, 16)]
        + [whole(512, D), whole(512, 512)] + [whole(64, D)] * 8,
        out_specs=[whole(256, D), whole(256, D), whole(512, 16), whole(4, 6, 384, 256)],
        out_shape=[shaped(256, D), shaped(256, D), shaped(512, 16, dtype=F32), shaped(4, 6, 384, 256)],
        scratch_shapes=[pltpu.VMEM((512, D), BF), pltpu.VMEM((512, 1024), BF)],
        compiler_params=params(),
        cost_estimate=cost(512 * 1536 * 1536 * 2, 10 << 20, 512 * 512),
        name="experts_backward",
    )(*earlier, where, router, *[weights] * 4, pre, gates, tokens, mid, *grads)


def last_expert_kernel(where_ref, router_ref, *refs):
    weight_ref, refs = Quarters(refs[:4]), refs[4:]
    token_refs, given_refs = refs[:8], refs[8:16]
    pa_ref, pb_ref, gates_ref, gated_ref, tokens_ref, weight_grad_ref, mid_ref, gpre_ref, all_ref = refs[16:]
    for h, out_ref in enumerate((pa_ref, pb_ref)):
        rows = pl.ds(h * 256, 256)
        tokens = stacked(token_refs[4 * h : 4 * h + 4])
        tokens_ref[rows] = tokens
        given = stacked(given_refs[4 * h : 4 * h + 4])
        grad_out = given[:, 0:1536]
        all_ref[rows] = grad_out
        parts = [tokens[:, r * 384 : (r + 1) * 384] for r in range(4)]
        grad_parts = [grad_out[:, r * 384 : (r + 1) * 384] for r in range(4)]
        routed = given[:, 1536:1552].astype(F32) > 0
        logits = jnp.where(routed, nt(tokens, router_ref[...]), NEGATIVE)
        raised = jnp.exp(logits - jnp.max(logits, axis=1, keepdims=True))
        raised = jnp.where(routed, raised, 0.0)
        gates = raised / jnp.sum(raised, axis=1, keepdims=True)
        expert = lax.broadcasted_iota(jnp.int32, (256, 16), 1) - 2 * where_ref[3]
        gates = jnp.where((expert == 0) | (expert == 1), gates, 0.0)
        gates_ref[rows] = gates
        gated = jnp.zeros((256, 16), F32)
        mids, grads = [], []
        for e in range(2):
            gate_pre = sum(nn(parts[r], weight_ref[r, e]) for r in range(4))
            up_pre = sum(nn(parts[r], weight_ref[r, 2 + e]) for r in range(4))
            raw = sum(nn(grad_parts[r], weight_ref[r, 4 + e]) for r in range(4))
            gate = jnp.sum(jnp.where(expert == e, gates, 0.0), axis=1, keepdims=True)
            sigmoid = jax.nn.sigmoid(gate_pre)
            activated = gate_pre * sigmoid
            product = activated * up_pre
            mid = (product * gate).astype(BF)
            mid_ref[rows, e * 256 : (e + 1) * 256] = mid
            mids.append(mid)
            gated = jnp.where(expert == e, gates * jnp.sum(product * raw, axis=1, keepdims=True), gated)
            raw = raw * gate
            grad_gate = (raw * up_pre * sigmoid * (1.0 + gate_pre * (1.0 - sigmoid))).astype(BF)
            grad_up = (raw * activated).astype(BF)
            gpre_ref[rows, e * 256 : (e + 1) * 256] = grad_gate
            gpre_ref[rows, (2 + e) * 256 : (3 + e) * 256] = grad_up
            grads.append((grad_gate, grad_up))
        gated_ref[rows] = gated
        high = gated.astype(BF)
        low = (gated - high.astype(F32)).astype(BF)
        for r in range(4):
            lanes = slice(r * 384, (r + 1) * 384)
            made = (nt(mids[0], weight_ref[r, 4]) + nt(mids[1], weight_ref[r, 5])).astype(BF)
            back = nn(high, router_ref[:, lanes]) + nn(low, router_ref[:, lanes])
            for e in range(2):
                back = back + nt(grads[e][0], weight_ref[r, e]) + nt(grads[e][1], weight_ref[r, 2 + e])
            back = back.astype(BF)
            for j in range(4):
                out_ref[j * 128 : j * 128 + 64, lanes] = made[j * 64 : (j + 1) * 64]
                out_ref[j * 128 + 64 : (j + 1) * 128, lanes] = back[j * 64 : (j + 1) * 64]
    weight_products(weight_grad_ref, tokens_ref, all_ref, gpre_ref, mid_ref)


def last_experts(where, tokens, given, router, weights, *earlier):
    return pl.pallas_call(
        ignoring(len(earlier), last_expert_kernel),
        grid=(1,),
        in_specs=[ANY] * len(earlier)
        + [SMEM, whole(16, D)] + QUARTERS + [whole(64, D)] * 8 + [whole(64, 1664)] * 8,
        out_specs=[whole(512, D)] * 2 + [whole(512, 16)] * 2 + [whole(512, D), whole(4, 6, 384, 256)],
        out_shape=[shaped(512, D), shaped(512, D), shaped(512, 16, dtype=F32), shaped(512, 16, dtype=F32)]
        + [shaped(512, D), shaped(4, 6, 384, 256)],
        scratch_shapes=[pltpu.VMEM((512, 512), BF), pltpu.VMEM((512, 1024), BF), pltpu.VMEM((512, D), BF)],
        compiler_params=params(),
        cost_estimate=cost(512 * 1536 * 1536 * 4, 16 << 20, 512 * 512),
        name="last_experts",
    )(*earlier, where, router, *[weights] * 4, *tokens, *given)


def chosen(size, width, me):
    row = lax.broadcasted_iota(jnp.int32, (size, width), 0)
    lane = lax.broadcasted_iota(jnp.int32, (size, width), 1)
    return (row == lane + me * width).astype(BF)


def source(where_ref, b):
    return ((where_ref[1] - (b & 3)) & 3) * 2 + (where_ref[2] if b < 4 else 1 - where_ref[2])


def dense_slice_kernel(pieces, where_ref, gated_ref, gates_ref, gains_ref, *refs):
    me = where_ref[3]
    left, tokens, right_all = stacked(refs[0:4]), stacked(refs[4:8]), stacked(refs[8:12])
    lane_refs, refs = refs[12], refs[13:]
    out_ref = refs[8 if pieces else 0]
    if pieces:
        right = refs[9]
        for b in range(8):
            right[pl.ds(pl.multiple_of(source(where_ref, b) * 64, 64), 64), :] = refs[b][...]
        right = right[...]
    else:
        right = right_all[:, 1664:2944]
    rows = tn(nn(left[:, 0:1536], chosen(1536, 192, me)).astype(BF), right).astype(BF)
    left = nn(left[:, 1536:2304], chosen(768, 96, me)).astype(BF)
    lane = lax.broadcasted_iota(jnp.int32, (64, 16), 1)
    logits = []
    for b in range(8):
        block = slice(b * 64, (b + 1) * 64)
        start = pl.multiple_of(source(where_ref, b) * 64, 64)
        lanes = lane_refs[pl.ds(start, 64), :].astype(F32)
        inner = lanes[:, 0:1] + lanes[:, 1:2]
        grad = gated_ref[block] - 0.5 * gates_ref[block] * inner
        one = [jnp.sum(jnp.where(lane == 2 * me + e, grad, 0.0), axis=1, keepdims=True) for e in range(2)]
        logits.append(jnp.where(lane == 0, one[0], jnp.where(lane == 1, one[1], 0.0)).astype(BF))
    extra = tn(jnp.concatenate(logits, axis=0), tokens)
    row = lax.broadcasted_iota(jnp.int32, (16, D), 0)
    extra = jnp.where(row == 2, gains_ref[...], extra)
    wide = jnp.concatenate([tn(left, right_all[:, 0:1536]), extra], axis=0).astype(BF)
    for r in range(4):
        to = (where_ref[0] - r) & 3
        for c in range(10):
            out_ref[to, c * 48 : (c + 1) * 48] = rows[r * 48 : (r + 1) * 48, c * 128 : (c + 1) * 128]
        for c in range(3):
            lanes = slice(r * 384 + c * 128, r * 384 + (c + 1) * 128)
            out_ref[to, 480 + c * 112 : 480 + (c + 1) * 112] = wide[:, lanes]


def quarters(width, base):
    return [pl.BlockSpec((128, width), functools.partial(lambda i, j: (i, base), i)) for i in range(4)]


def dense_slice(layer, where, left, gated, gates, gains, tokens, right, pieces, *earlier):
    return pl.pallas_call(
        ignoring(len(earlier), functools.partial(dense_slice_kernel, len(pieces) > 0)),
        grid=(1,),
        in_specs=[ANY] * len(earlier)
        + [SMEM, whole(512, 16), whole(512, 16), whole(1, D)]
        + quarters(2304, layer)
        + quarters(D, 0)
        + quarters(right.shape[1], 0)
        + [pl.BlockSpec((512, 128), lambda j: (0, 12))]
        + [whole(64, 1280)] * len(pieces),
        out_specs=whole(4, 816, 128),
        out_shape=shaped(4, 816, 128),
        scratch_shapes=[pltpu.VMEM((512, 1280), BF)] if pieces else [],
        compiler_params=params(),
        cost_estimate=cost(512 * 1536 * 1024 * 2, 8 << 20),
        name="dense_slice",
    )(*earlier, where, gated, gates, gains, *[left] * 4, *[tokens] * 4, *[right] * 5, *pieces)


def dense_rows_kernel(in_ref, q_ref, k_ref, v_ref, out_ref, router_ref, gains_ref, held_ref):
    j = pl.program_id(0)
    for x in range(4):
        rows = slice(x * 48, (x + 1) * 48)
        for c in range(10):
            to_ref, lane = (q_ref, c) if c < 6 else (k_ref, c - 6) if c < 8 else (v_ref, c - 8)
            to_ref[rows, lane * 128 : (lane + 1) * 128] = in_ref[x, 0, c * 48 : (c + 1) * 48].astype(F32)
        for c in range(3):
            lanes = slice(x * 384 + c * 128, x * 384 + (c + 1) * 128)
            out_ref[:, lanes] = in_ref[x, 0, 480 + c * 112 : 576 + c * 112].astype(F32)
            held_ref[j, :, lanes] = in_ref[x, 0, 576 + c * 112 : 592 + c * 112].astype(F32)

    @pl.when(j == 7)
    def _():
        held = held_ref[...]
        router = jnp.concatenate([held[i, 0:2] for i in range(8)], axis=0)
        router_ref[...] = router
        gains_ref[...] = jnp.sum(held, axis=0)


def dense_rows(everything):
    rows = lambda count, width: pl.BlockSpec((count, width), lambda j: (j, 0))
    return pl.pallas_call(
        dense_rows_kernel,
        grid=(8,),
        in_specs=[pl.BlockSpec((4, 1, 816, 128), lambda j: (0, j, 0, 0))],
        out_specs=[rows(192, 768), rows(192, 256), rows(192, 256), rows(96, D), whole(16, D), whole(16, D)],
        out_shape=[shaped(D, 768, dtype=F32), shaped(D, 256, dtype=F32), shaped(D, 256, dtype=F32)]
        + [shaped(768, D, dtype=F32), shaped(16, D, dtype=F32), shaped(16, D, dtype=F32)],
        scratch_shapes=[pltpu.VMEM((8, 16, D), F32)],
        compiler_params=params(28),
        cost_estimate=cost(0, 20 << 20),
        name="dense_rows",
    )(everything)


def gates_of(tokens, router, routed):
    logits = dot(tokens, router)
    top = jnp.max(jnp.where(routed > 0, logits, NEGATIVE), axis=1, keepdims=True)
    raised = jnp.where(routed > 0, jnp.exp(jnp.minimum(logits - top, 0.0)), 0.0)
    return raised / jnp.sum(raised, axis=1, keepdims=True)


X_GROUPS = [[(x * NY + y) * 2 + c for x in range(NX)] for y in range(NY) for c in range(2)]


Y_GROUPS = [[(x * NY + y) * 2 + c for y in range(NY) for c in range(2)] for x in range(NX)]


def replica_gather(shard):
    return lax.all_gather(shard, "dp", axis=0, axis_index_groups=X_GROUPS)


def replica_scatter(grads):
    flat = grads.reshape(-1, grads.shape[-1])
    return lax.psum_scatter(flat, "dp", scatter_dimension=0, axis_index_groups=X_GROUPS, tiled=True)


def after(value, *others):
    return lax.optimization_barrier((value, *others))[0]


def group_pieces(block):
    near = [block] + [moved(block, 0, j, 0) for j in (1, 2, 3)]
    return near + [moved(piece, 0, 0, 1) for piece in near]


def ordered(value):
    probe = value[(-1,) * value.ndim]
    return probe == probe


def behind(value, *earlier):
    known = ordered(earlier[0])
    for other in earlier[1:]:
        known = known & ordered(other)
    return jnp.where(known, value, jnp.zeros_like(value))


def per_device(
    inputs,
    cotangent,
    segments,
    routes,
    norm_first,
    w_query,
    w_key,
    w_value,
    w_out,
    norm_second,
    w_router,
    w_gate,
    w_up,
    w_down,
):
    section = lax.axis_index("section")
    place = lax.axis_index("dp")
    here_x, here_y, here_c = place // (NY * 2), place // 2 % NY, place % 2
    me = place % 8
    first = section == 0
    rows = inputs.shape[1]

    def in_order(own, other):
        return jnp.where(first, own, other), jnp.where(first, other, own)

    def pick(pair):
        return lax.dynamic_index_in_dim(pair, section, 0, False)

    weights_in = (w_query[0], w_key[0], w_value[0])
    dense = jnp.concatenate(
        [lax.dynamic_slice_in_dim(w, place * 48, 48, 0) for w in weights_in]
        + [lax.dynamic_slice(w_out[0], (place % 16 * 48, place // 16 * 768), (48, 768))],
        axis=1,
    )
    dense = swapped(dense, "section")

    act_both = norm_apply(inputs.astype(F32), norm_first[0]).astype(BF).reshape(2 * rows, D)
    qkv_both = jnp.concatenate([dot(act_both, w).astype(BF) for w in weights_in], axis=1)
    qkv_sent = lax.ppermute(qkv_both[rows:], "section", [(0, 1)])
    qkv_first = jnp.where(first, qkv_both[:rows], qkv_sent)
    dense_all = lax.all_gather(behind(dense, qkv_both), "dp", axis=0).reshape(D, 2048)

    pack = jnp.concatenate([norm_first, norm_second, w_router[0].T.astype(F32)], axis=0)
    packs = in_order(pack, swapped(pack, "section"))
    routers = [p[2:].astype(BF) for p in packs]
    turned_down = jnp.swapaxes(w_down[0], 1, 2)
    sent_gate = swapped(w_gate[0], "section")
    sent_rest = swapped(side_by_side([w_up[0], turned_down], 0, qkv_sent), "section")
    halves = (w_gate[0], w_up[0], turned_down, sent_gate, sent_rest)
    expert_weights = [None, None]
    where = jnp.stack([here_x, here_y, here_c, me, section]).astype(jnp.int32)

    labels = pick(segments)
    query_labels = lax.dynamic_slice_in_dim(labels, place * rows, rows, 0)
    starts = jnp.sum((labels[None, :] < query_labels[:, None]).astype(jnp.int32), axis=1)
    masks = (where, jnp.concatenate([starts, starts])[None])

    own_routes = pick(routes)
    expert_ids = jnp.arange(EXPERTS, dtype=jnp.int32)
    routed_own = jnp.sum((own_routes[:, :, None] == expert_ids).astype(F32), axis=1)
    given = pick(cotangent)
    sent = jnp.concatenate([given, jnp.pad(routed_own.astype(BF), ((0, 0), (0, 128 - EXPERTS)))], axis=1)
    given_all = group_pieces(sent)

    hidden = pick(inputs).astype(F32)
    saved = []
    for layer in range(2):
        gain_one, gain_two = packs[layer][0:1], packs[layer][1:2]
        if layer == 0:
            activation, qkv = norm_apply(hidden, gain_one).astype(BF), qkv_first
        else:
            activation, qkv = qkv_of(1, where, hidden, gain_one, weights_in, dense_all)
        query, pair = qkv[:, :768], qkv[:, 768:]
        around = [moved(pair, j, 0, 0) for j in (1, 2, 3)]
        slab = jnp.concatenate([pair] + around, axis=0)
        near = [slab] + [moved(slab, 0, j, 0) for j in (1, 2, 3)]
        pieces = near + [moved(piece, 0, 0, 1) for piece in near]
        if layer == 0:
            mixed, log_total, *pieces = attend_forward(0, masks, query, pieces)
        else:
            mixed, log_total, *pieces, partial, lefts = attend_forward(
                1, masks, query, pieces, (*saved[0][8], activation), (w_out[0], dense_all)
            )
        if layer == 0:
            mixed_sent = lax.ppermute(mixed, "section", [(1, 0)])
            partial = dot(jnp.concatenate([mixed, mixed_sent], axis=0), w_out[0]).astype(BF)
            both_axes = ("section", "tensor")
            straight = lax.ppermute(partial[rows:], both_axes, [(0, 2), (1, 3)])
            across = lax.ppermute(partial[rows:], both_axes, [(0, 3), (1, 2)])
            turned = lax.ppermute(partial[:rows], both_axes, [(0, 1), (1, 0)])
            experts_first = choose(0, section[None].astype(jnp.int32), halves, mixed)
            expert_weights[0] = replica_gather(experts_first)
            middle = hidden + (
                jnp.where(first, partial[:rows], straight).astype(F32) + jnp.where(first, turned, across).astype(F32)
            )
        else:
            middle = hidden + (partial.astype(F32) + swapped(partial, "tensor").astype(F32))
        second = norm_apply(middle, gain_two).astype(BF)
        tokens = group_pieces(second)
        if layer == 0:
            experts_second = choose(1, section[None].astype(jnp.int32), halves, second, dense_all)
            expert_weights[1] = replica_gather(experts_second)
        cut = (activation, mixed)
        if layer == 0:
            made_near, made_far, pre, mid, gates, tokens = experts_forward(
                where, tokens, given_all, routers[0], expert_weights[0], experts_second
            )
            made = group_sum(made_near, made_far).reshape(rows, D).astype(BF)
            branch = tensor_sum(made)
            rest = (gates, (pre, mid))
        else:
            lefts = held_until(lefts, *tokens[1:])
            near, far, gates, gated, tokens, weight_grads = last_experts(
                where, tokens, given_all, routers[1], expert_weights[1]
            )
            both = (near.astype(F32) + moved(far, 0, 0, 1).astype(F32)).astype(BF)
            low = back_y(both).reshape(2 * rows, D).astype(BF)
            weight_grads = held_until(weight_grads, low)
            lefts = lax.all_gather(lefts, "dp", axis=0, axis_index_groups=Y_GROUPS).reshape(8 * rows, 4608)
            got = swapped(low, "tensor")
            branch = low[:rows].astype(F32) + got[:rows].astype(F32)
            low, got = low[rows:], got[rows:]
            rest = (gates, gated)
        result = middle + branch
        saved.append((hidden, query, pieces, log_total, middle, second, tokens, branch, cut, result, rest))
        hidden = result

    def own_of(a, b):
        return jnp.where(first, a, b)

    def from_other(for_first, for_second):
        return swapped(own_of(for_second, for_first).astype(BF), "section").astype(F32)

    def over_sections(a, b):
        return own_of(a, b).astype(F32) + from_other(a, b)

    early_sent = own_of(saved[1][9], saved[0][9]).astype(BF)
    grad_output = given.astype(F32)
    grads = []
    for layer in (1, 0):
        hidden, query, pieces, log_total, middle, second, tokens, branch, _, _, rest = saved[layer]
        gain_one, gain_two = packs[layer][0:1], packs[layer][1:2]
        router = routers[layer]
        gates, rest = rest
        if layer == 1:
            gated = rest
        else:
            back_near, back_far, gated, weight_grads = experts_backward(
                where, group_pieces(grad_output.astype(BF)), rest[0], gates, tokens, rest[1], router, expert_weights[0], *earlier
            )
            both = (back_near.astype(F32) + moved(back_far, 0, 0, 1).astype(F32)).astype(BF)
            low = back_y(both).reshape(rows, D).astype(BF)
            got = swapped(low, "tensor")
        expert_part = replica_scatter(weight_grads)
        grad_middle, right, grad_mixed, gain_two_grad = middle_back(
            layer, where, low, got, grad_output, branch, middle, gain_two, router, routed_own, w_out[0], dense_all
        )
        grad_query, back_near, back_far = attend_backward(masks, query, grad_mixed, log_total, *pieces)
        both = (back_near.astype(F32) + moved(back_far, 0, 0, 1).astype(F32)).astype(BF)
        half = back_y(both)
        if layer == 0:
            late = dense_slice(1, *grads[0][1], [], both)
            half = behind(half, late)
            late = back_x(late.reshape(4 * 816, 128)).reshape(816, 128)
        grad_pair = back_x(half.astype(BF)).reshape(rows, 512).astype(BF)
        grad_qkv = jnp.concatenate([grad_query, grad_pair], axis=1)
        if layer == 0:
            grad_qkv = held_until(grad_qkv, expert_part, late)
            right_pieces = group_pieces(grad_qkv)
            right = lax.all_gather(right, "dp", axis=0, axis_index_groups=Y_GROUPS).reshape(8 * rows, 1664)
            results_sent = swapped(held_until(early_sent, both), "section")
            blocks = dense_slice(0, where, lefts, gated, gates, gain_two_grad, tokens, right, right_pieces, results_sent)
        partial = act_back(layer, where, grad_qkv, weights_in, dense_all, *([lefts] if layer == 1 else []))
        grad_activation = partial.astype(F32) + swapped(partial, "tensor").astype(F32)
        grad_from_first, gain_one_grad = norm_back(hidden, gain_one, grad_activation)
        grad_input = grad_middle + grad_from_first
        if layer == 1:
            right = jnp.concatenate([right, grad_qkv], axis=1)
            earlier = [right, expert_part]
            right = lax.all_gather(right, "dp", axis=0, axis_index_groups=Y_GROUPS).reshape(8 * rows, 2944)
            grads.append((grad_input, (where, lefts, gated, gates, gain_two_grad, tokens, right), expert_part, gain_one_grad))
        else:
            grads.append((grad_input, back_x(blocks.reshape(4 * 816, 128)).reshape(816, 128), expert_part, gain_one_grad))
        grad_output = grad_input
    grads = grads[::-1]

    def by_batch(own, other):
        return jnp.stack([jnp.where(first, own, other), jnp.where(first, other, own)])[None]

    results = by_batch(own_of(saved[0][9], saved[1][9]), results_sent.astype(F32))
    input_grads = by_batch(own_of(grads[0][0], grads[1][0]), from_other(grads[0][0], grads[1][0]))
    first_part = grads[0][1]

    def extras(block):
        return block[480:816].reshape(3, 112, 128)[:, 96:98].reshape(6, 128)

    straight = swapped(jnp.concatenate([extras(first_part), extras(late)], axis=0).astype(BF), "tensor").astype(F32)
    across = lax.ppermute(
        own_of(extras(late), extras(first_part)).astype(BF), ("section", "tensor"), [(0, 3), (1, 2), (2, 1), (3, 0)]
    ).astype(F32)
    block = over_sections(first_part, late)
    more = own_of(straight[:6], straight[6:]) + across
    wide = block[480:].reshape(3, 112, 128)
    wide = wide + jnp.pad(more.reshape(3, 2, 128), ((0, 0), (96, 14), (0, 0)))
    block = jnp.concatenate([block[:480], wide.reshape(336, 128)], axis=0).astype(BF)
    everything = lax.all_gather(block, "dp", axis=0).reshape(4, 8, 816, 128)
    query_sum, key_sum, value_sum, out_full, router_sum, gains = dense_rows(everything)
    gain_sent = from_other(grads[0][3], grads[1][3])
    gain_one_sum = (own_of(grads[0][3], grads[1][3]) + gain_sent).astype(BF)
    gain_one_sum = jnp.sum(lax.all_gather(gain_one_sum, "dp", axis=0).astype(F32), axis=0)[None]
    expert_sent = swapped(behind(own_of(grads[1][2], grads[0][2]), gain_sent), "section")
    expert_sum = own_of(grads[0][2], grads[1][2]).astype(F32) + expert_sent.astype(F32)
    expert_sum = expert_sum.reshape(3, 2, 384, 256)
    return (
        results,
        input_grads,
        gain_one_sum,
        query_sum[None],
        key_sum[None],
        value_sum[None],
        out_full[None],
        gains[2:3],
        router_sum.T[None],
        expert_sum[0][None],
        expert_sum[1][None],
        jnp.swapaxes(expert_sum[2], 1, 2)[None],
    )


def solution(mesh):
    in_specs = (
        P(None, "dp", None),
        P(None, "dp", None),
        P(),
        P(None, "dp", None),
        P("section", None),
        P("section", None, "tensor"),
        P("section", None, "tensor"),
        P("section", None, "tensor"),
        P("section", "tensor", None),
        P("section", None),
        P("section", None, None),
        P("section", "dp", None, "tensor"),
        P("section", "dp", None, "tensor"),
        P("section", "dp", "tensor", None),
    )
    out_specs = (
        P("section", None, "dp", None),
        P("section", None, "dp", None),
        P("section", None),
        P("section", None, "tensor"),
        P("section", None, "tensor"),
        P("section", None, "tensor"),
        P("section", "tensor", None),
        P("section", None),
        P("section", None, None),
        P("section", "dp", None, "tensor"),
        P("section", "dp", None, "tensor"),
        P("section", "dp", "tensor", None),
    )
    return jax.shard_map(
        per_device, mesh=mesh, in_specs=in_specs, out_specs=out_specs, check_vma=False
    )
```
